32 devices in a mesh: batch: 4 (over y, x), proto: 8 (over z, core).
Axes of the slice: x: 2, y: 2, z: 4, core: 2. Of those that a mesh axis runs over, the one named last changes fastest.
Arguments:
- embeddings: bfloat16 [8192, 1024], P('batch'), may hold values from -0.5 to 0.5
- prototypes: bfloat16 [8192, 1024], P('proto'), may hold values from -6 to 6
- partners: int32 [8192, 2], P('batch'), may hold values from 0 to 8191
Outputs:
- loss: float32 [], replicated
- grad_proto: float32 [8192, 1024], P('proto', 'batch')
- grad_embed: float32 [8192, 1024], P(('batch', 'proto'))
The draws below stay inside these ranges and needn't reach their ends.
Inputs may be any that keep to these rules, and one draw needn't show every extreme that they name: `partners`: row indices over the whole batch.
All inputs are finite; a program needn't handle non-finite values.
Results may differ from the reference program's by a relative error of at most 0.0016.
Values may be sent and summed in bfloat16 or wider, within the bound.
No kernel may reach another device: no remote copies, remote signals or barrier semaphores. Data moves between devices by JAX's collectives and lax.ppermute only.
A program may use at most 128 MiB of HBM per device.

```python
import jax
import jax.numpy as jnp
from jax import lax

D = 1024
ROWS_DEV = 2048
ITERS = 3
TOTAL = 8192
CENTROID_NUMBER = 8192


def family_centers(key):
    return jax.random.normal(key, (4, D), jnp.float32)


def draw_prototypes(key, part):
    centers = family_centers(key)
    key = jax.random.fold_in(key, 1)
    noise_key, label_key = jax.random.split(key)
    noise = jax.random.normal(noise_key, (CENTROID_NUMBER, D), jnp.float32)
    level = jax.random.randint(label_key, (CENTROID_NUMBER,), 0, 10)
    family = (level >= 1).astype(jnp.int32) + (level >= 3).astype(jnp.int32) + (level >= 6).astype(jnp.int32)
    values = noise + 1.5 * jnp.take(centers, family, axis=0)
    return jnp.clip(values, -6.0, 6.0).astype(jnp.bfloat16)


def grouped_rows(noise, centers, label_key, level_key, order_key):
    level = jax.random.randint(label_key, (TOTAL,), 0, 10)
    group = (level >= 4).astype(jnp.int32) + (level >= 7).astype(jnp.int32) + (level >= 9).astype(jnp.int32)
    order = jax.random.permutation(order_key, 4)
    block = jnp.arange(TOTAL) // ROWS_DEV % 4
    lower = 0.48 + 0.05 * jnp.take(order, block).astype(jnp.float32)
    along_center = lower + 0.2 * jax.random.uniform(level_key, (TOTAL,), jnp.float32)
    strength = along_center / jnp.sqrt(1.0 - along_center * along_center)
    mixed = 0.03125 * (noise + strength[:, None] * jnp.take(centers, group, axis=0))
    return jnp.clip(mixed, -0.5, 0.5)


def draw_embeddings(key, part):
    centers = family_centers(key)
    key = jax.random.fold_in(key, 7)
    noise_key, label_key, level_key, order_key = jax.random.split(key, 4)
    noise = jax.random.normal(noise_key, (TOTAL, D), jnp.float32)
    values = grouped_rows(noise, centers, label_key, level_key, order_key)
    return values.astype(jnp.bfloat16)


def with_ends(result, stream_key, least, top_value):
    place = [jax.random.randint(jax.random.fold_in(stream_key, axis), (), 0, length) for axis, length in enumerate(result.shape)]
    longest = result.shape.index(max(result.shape))
    beside = place[:longest] + [(place[longest] + 1) % result.shape[longest]] + place[longest + 1:]
    return result.at[tuple(place)].set(least).at[tuple(beside)].set(top_value)


def setup_inputs(seed: int = 0) -> dict:
    key_of = jax.random.split(jax.random.key(seed), 4)
    embeddings = draw_embeddings(jax.random.fold_in(key_of[3], 71), 0)
    prototypes = draw_prototypes(jax.random.fold_in(key_of[3], 71), 0)
    partners = with_ends(jax.random.randint(key_of[2], (TOTAL, 2), 0, TOTAL), jax.random.fold_in(key_of[2], 1), 0, TOTAL - 1).astype(jnp.int32)
    return {"embeddings": embeddings, "prototypes": prototypes, "partners": partners}


BALANCE_SMOOTHING = 0.05
SOFTMAX_HEAT = 0.1
NORM_EPSILON = 1e-06

def reference(embeddings, prototypes, partners):
    hidden_f = embeddings.astype(jnp.float32)
    inverse = 1.0 / jnp.sqrt(lax.optimization_barrier(jnp.sum(hidden_f * hidden_f, axis=1, keepdims=True)) + NORM_EPSILON)
    unit = (hidden_f * inverse).astype(jnp.bfloat16)
    proto_f = prototypes.astype(jnp.float32)
    wnorm = (proto_f / jnp.sqrt(lax.optimization_barrier(jnp.sum(proto_f * proto_f, axis=1, keepdims=True)) + NORM_EPSILON)).astype(jnp.bfloat16)
    cosine_affinities = jnp.dot(unit, wnorm.T, preferred_element_type=jnp.float32)
    exponent_matrix = jnp.exp(cosine_affinities / BALANCE_SMOOTHING)
    row_scale = jnp.ones((TOTAL,), jnp.float32)
    col_scale = jnp.ones((CENTROID_NUMBER,), jnp.float32)
    for iteration in range(ITERS):
        col_scale = 1.0 / (CENTROID_NUMBER * lax.optimization_barrier(jnp.sum(exponent_matrix * row_scale[:, None], axis=0)))
        row_scale = 1.0 / (TOTAL * lax.optimization_barrier(jnp.sum(exponent_matrix * col_scale[None, :], axis=1)))
    assign = (TOTAL * row_scale[:, None] * exponent_matrix * col_scale[None, :]).astype(jnp.bfloat16)
    first_idx = partners[:, 0].astype(jnp.int32)
    second_idx = partners[:, 1].astype(jnp.int32)
    cluster_codes = 0.5 * (assign[first_idx].astype(jnp.float32) + assign[second_idx].astype(jnp.float32))
    raw_activation_table = cosine_affinities / SOFTMAX_HEAT
    exponentiated_guesses = jnp.exp(raw_activation_table)
    normalizer_value = lax.optimization_barrier(jnp.sum(exponentiated_guesses, axis=1))
    code_accumulated = lax.optimization_barrier(jnp.sum(cluster_codes, axis=1))
    loss = jnp.sum(code_accumulated * jnp.log(normalizer_value) - lax.optimization_barrier(jnp.sum(cluster_codes * raw_activation_table, axis=1))) / TOTAL
    affinity_derivative = (exponentiated_guesses / normalizer_value[:, None] * code_accumulated[:, None] - cluster_codes) * (CENTROID_NUMBER / (32.0 * SOFTMAX_HEAT))
    affinity_derivative = affinity_derivative.astype(jnp.bfloat16)
    grad_proto = jnp.dot(affinity_derivative.T, unit, preferred_element_type=jnp.float32)
    gunit = jnp.dot(affinity_derivative, wnorm, preferred_element_type=jnp.float32)
    along = lax.optimization_barrier(jnp.sum(hidden_f * gunit, axis=1, keepdims=True))
    grad_embed = inverse * gunit - hidden_f * inverse * inverse * inverse * along
    return (loss, grad_proto, grad_embed)
```

```python
import functools

import jax
import jax.numpy as jnp
from jax import lax
from jax.experimental import pallas as pl
from jax.experimental.pallas import tpu as pltpu
from jax.sharding import PartitionSpec as P

ITERS = 3
BALANCE_SMOOTHING = 0.05
SOFTMAX_HEAT = 0.1
NORM_EPSILON = 1e-06
BLOCK = 256
LANES = 128
MIB = 1 << 20
F32 = jnp.float32
BF16 = jnp.bfloat16


def params(mib):
    return pltpu.CompilerParams(vmem_limit_bytes=mib * MIB)


def cost(flops, moved, exps=0):
    return pl.CostEstimate(flops=flops, bytes_accessed=moved, transcendentals=exps)


def normalized(block):
    wide = block.astype(F32)
    inverse = 1.0 / jnp.sqrt(jnp.sum(wide * wide, axis=1, keepdims=True) + NORM_EPSILON)
    return wide * inverse


def lane_row_sums(values):
    columns = values.shape[1]
    part = values[:, 0:LANES]
    for start in range(LANES, columns, LANES):
        part = part + values[:, start : start + LANES]
    return jnp.sum(part.T, axis=0, keepdims=True)


def split_rows(row):
    high = row.astype(BF16).astype(F32)
    middle = (row - high).astype(BF16).astype(F32)
    low = row - high - middle
    place = lax.broadcasted_iota(jnp.int32, (16, row.shape[1]), 0)
    stacked = jnp.where(place == 0, high, jnp.where(place == 1, middle, jnp.where(place == 2, low, 0.0)))
    return stacked.astype(BF16)


def own_rows_kernel(index_ref, embeddings_ref, table_ref, stage_ref):
    del index_ref
    rows, columns = embeddings_ref.shape
    unit = normalized(embeddings_ref[...]).astype(BF16).astype(F32)
    groups = columns // LANES
    for k in range(groups):
        stage_ref[pl.ds(k, rows, stride=groups), :] = unit[:, k * LANES : (k + 1) * LANES]
    table_ref[...] = stage_ref[...].reshape(rows, groups, LANES).astype(BF16)


def own_rows(embeddings, index, share):
    columns = embeddings.shape[1]
    groups = columns // LANES
    return pl.pallas_call(
        own_rows_kernel,
        grid_spec=pltpu.PrefetchScalarGridSpec(
            num_scalar_prefetch=1,
            grid=(1,),
            in_specs=[pl.BlockSpec((share, columns), lambda i, index: (index[0], 0))],
            out_specs=pl.BlockSpec((share, groups, LANES), lambda i, index: (0, 0, 0)),
            scratch_shapes=[pltpu.VMEM((share * groups, LANES), F32)],
        ),
        out_shape=jax.ShapeDtypeStruct((share, groups, LANES), BF16),
        compiler_params=params(16),
        name="own_rows",
    )(index, embeddings)


def scores_kernel(embeddings_ref, prototypes_ref, unit_ref, wnorm_ref, scores_ref, expo_ref, zsum_ref, column_ref):
    step = pl.program_id(0)

    @pl.when(step == 0)
    def _():
        wnorm_ref[...] = normalized(prototypes_ref[...]).astype(BF16)

    unit = normalized(embeddings_ref[...]).astype(BF16)
    unit_ref[...] = unit
    scores = lax.dot_general(unit, wnorm_ref[...], (((1,), (1,)), ((), ())), preferred_element_type=F32)
    scores_ref[...] = scores
    soft = jnp.exp(scores * (1.0 / SOFTMAX_HEAT))
    zsum_ref[...] = lane_row_sums(soft)
    expo = soft * soft
    expo_ref[...] = expo.astype(BF16)
    sums = jnp.sum(expo, axis=0, keepdims=True)

    @pl.when(step == 0)
    def _():
        column_ref[...] = sums

    @pl.when(step > 0)
    def _():
        column_ref[...] += sums


def scores_of(embeddings, prototypes):
    rows, columns = embeddings.shape
    protos = prototypes.shape[0]
    return pl.pallas_call(
        scores_kernel,
        grid=(rows // BLOCK,),
        in_specs=[
            pl.BlockSpec((BLOCK, columns), lambda i: (i, 0)),
            pl.BlockSpec((protos, columns), lambda i: (0, 0), pipeline_mode=pl.Buffered(1)),
        ],
        out_specs=[
            pl.BlockSpec((BLOCK, columns), lambda i: (i, 0)),
            pl.BlockSpec((protos, columns), lambda i: (0, 0)),
            pl.BlockSpec((BLOCK, protos), lambda i: (i, 0)),
            pl.BlockSpec((BLOCK, protos), lambda i: (i, 0)),
            pl.BlockSpec((1, BLOCK), lambda i: (0, i)),
            pl.BlockSpec((1, protos), lambda i: (0, 0)),
        ],
        out_shape=[
            jax.ShapeDtypeStruct((rows, columns), BF16),
            jax.ShapeDtypeStruct((protos, columns), BF16),
            jax.ShapeDtypeStruct((rows, protos), F32),
            jax.ShapeDtypeStruct((rows, protos), BF16),
            jax.ShapeDtypeStruct((1, rows), F32),
            jax.ShapeDtypeStruct((1, protos), F32),
        ],
        compiler_params=params(40),
        cost_estimate=cost(2 * rows * columns * protos, 22 * MIB, rows * protos),
        name="scores",
    )(embeddings, prototypes)


def row_kernel(count, column_ref, expo_ref, row_ref):
    scale = 1.0 / (count * jnp.sum(column_ref[...], axis=0, keepdims=True))
    sums = lax.dot_general(
        split_rows(scale), expo_ref[...], (((1,), (1,)), ((), ())), preferred_element_type=F32
    )
    row_ref[...] = jnp.sum(sums, axis=0, keepdims=True)


def row_pass(columns, expo, count):
    rows, protos = expo.shape
    block = 2 * BLOCK
    return pl.pallas_call(
        functools.partial(row_kernel, count),
        grid=(rows // block,),
        in_specs=[
            pl.BlockSpec(columns.shape, lambda i: (0, 0)),
            pl.BlockSpec((block, protos), lambda i: (i, 0)),
        ],
        out_specs=pl.BlockSpec((1, block), lambda i: (0, i)),
        out_shape=jax.ShapeDtypeStruct((1, rows), F32),
        compiler_params=params(16),
        cost_estimate=cost(2 * rows * protos, 4 * MIB),
        name="row_pass",
    )(columns, expo)


def column_kernel(count, row_ref, expo_ref, column_ref):
    step = pl.program_id(0)
    scale = 1.0 / (count * jnp.sum(row_ref[...], axis=0, keepdims=True))
    sums = lax.dot_general(
        split_rows(scale), expo_ref[...], (((1,), (0,)), ((), ())), preferred_element_type=F32
    )
    sums = jnp.sum(sums, axis=0, keepdims=True)

    @pl.when(step == 0)
    def _():
        column_ref[...] = sums

    @pl.when(step > 0)
    def _():
        column_ref[...] += sums


def column_pass(row_totals, expo, count):
    rows, protos = expo.shape
    block = 2 * BLOCK
    return pl.pallas_call(
        functools.partial(column_kernel, count),
        grid=(rows // block,),
        in_specs=[
            pl.BlockSpec((row_totals.shape[0], block), lambda i: (0, i)),
            pl.BlockSpec((block, protos), lambda i: (i, 0)),
        ],
        out_specs=pl.BlockSpec((1, protos), lambda i: (0, 0)),
        out_shape=jax.ShapeDtypeStruct((1, protos), F32),
        compiler_params=params(16),
        cost_estimate=cost(2 * rows * protos, 4 * MIB),
        name="column_pass",
    )(row_totals, expo)


def partner_kernel(first_ref, second_ref, table_ref, wnorm_ref, first_expo_ref, second_expo_ref, stage_ref):
    step = pl.program_id(0)
    groups = table_ref.shape[1]
    wnorm = wnorm_ref[...]
    for which_ref, out_ref in ((first_ref, first_expo_ref), (second_ref, second_expo_ref)):

        @pl.loop(0, BLOCK // 16)
        def _(i):
            for j in range(16):
                row = i * 16 + j
                place = which_ref[step * BLOCK + row]
                stage_ref[pl.ds(pl.multiple_of(row * groups, groups), groups), :] = table_ref[place].astype(F32)

        unit = jnp.concatenate(
            [stage_ref[pl.ds(k, BLOCK, stride=groups), :].astype(BF16) for k in range(groups)], axis=1
        )
        scores = lax.dot_general(unit, wnorm, (((1,), (1,)), ((), ())), preferred_element_type=F32)
        soft = jnp.exp(scores * (1.0 / SOFTMAX_HEAT))
        out_ref[...] = soft * soft


def partner_pass(first, second, table, wnorm):
    rows = first.shape[0]
    protos, columns = wnorm.shape
    groups = columns // LANES
    return pl.pallas_call(
        partner_kernel,
        grid_spec=pltpu.PrefetchScalarGridSpec(
            num_scalar_prefetch=2,
            grid=(rows // BLOCK,),
            in_specs=[
                pl.BlockSpec(table.shape, lambda i, *_: (0, 0, 0), pipeline_mode=pl.Buffered(1)),
                pl.BlockSpec((protos, columns), lambda i, *_: (0, 0), pipeline_mode=pl.Buffered(1)),
            ],
            out_specs=[
                pl.BlockSpec((BLOCK, protos), lambda i, *_: (i, 0)),
                pl.BlockSpec((BLOCK, protos), lambda i, *_: (i, 0)),
            ],
            scratch_shapes=[pltpu.VMEM((BLOCK * groups, LANES), F32)],
        ),
        out_shape=[jax.ShapeDtypeStruct((rows, protos), F32)] * 2,
        compiler_params=params(52),
        cost_estimate=cost(4 * rows * columns * protos, 36 * MIB, 2 * rows * protos),
        name="partner_scores",
    )(first, second, table, wnorm)


def partner_row_kernel(count, column_ref, first_ref, second_ref, row_ref):
    scale = 1.0 / (count * jnp.sum(column_ref[...], axis=0, keepdims=True))
    row_ref[...] = jnp.concatenate(
        [lane_row_sums(first_ref[...] * scale), lane_row_sums(second_ref[...] * scale)], axis=0
    )


def partner_row_pass(columns, first, second, count):
    rows, protos = first.shape
    return pl.pallas_call(
        functools.partial(partner_row_kernel, count),
        grid=(rows // BLOCK,),
        in_specs=[
            pl.BlockSpec(columns.shape, lambda i: (0, 0)),
            pl.BlockSpec((BLOCK, protos), lambda i: (i, 0)),
            pl.BlockSpec((BLOCK, protos), lambda i: (i, 0)),
        ],
        out_specs=pl.BlockSpec((2, BLOCK), lambda i: (0, i)),
        out_shape=jax.ShapeDtypeStruct((2, rows), F32),
        compiler_params=params(16),
        cost_estimate=cost(4 * rows * protos, 16 * MIB),
        name="partner_row_pass",
    )(columns, first, second)


def gradient_kernel(
    count, total, heat_scale, proto_size,
    column_ref, row_ref, zsum_ref, first_ref, second_ref, scores_ref, unit_ref, wnorm_ref,
    gunit_ref, gproto_ref, loss_ref,
):
    step = pl.program_id(0)
    scale = 1.0 / (count * jnp.sum(column_ref[...], axis=0, keepdims=True))
    row_totals = row_ref[...]
    row_scales = 1.0 / (total * row_totals)
    weights = total * row_scales
    code_totals = 0.5 * jnp.sum(weights * row_totals, axis=0, keepdims=True)
    zsum = jnp.sum(zsum_ref[...], axis=0, keepdims=True)
    soft_scale = code_totals / zsum
    log_part = jnp.sum(code_totals * jnp.log(zsum)) * (1.0 / proto_size)
    place = lax.broadcasted_iota(jnp.int32, (8, BLOCK), 0)
    stacked = jnp.where(
        place == 0, weights[0:1], jnp.where(place == 1, weights[1:2], jnp.where(place == 2, soft_scale, 0.0))
    )
    stacked = stacked.T
    first = (stacked[:, 0:1] * first_ref[...] * scale).astype(BF16).astype(F32)
    second = (stacked[:, 1:2] * second_ref[...] * scale).astype(BF16).astype(F32)
    targets = 0.5 * (first + second)
    heated = scores_ref[...] * (1.0 / SOFTMAX_HEAT)
    loss = log_part - jnp.sum(targets * heated)
    dscore = ((jnp.exp(heated) * stacked[:, 2:3] - targets) * heat_scale).astype(BF16)
    gunit_ref[...] = jnp.dot(dscore, wnorm_ref[...], preferred_element_type=F32)
    gproto = lax.dot_general(dscore, unit_ref[...], (((0,), (0,)), ((), ())), preferred_element_type=F32)

    @pl.when(step == 0)
    def _():
        gproto_ref[...] = gproto
        loss_ref[...] = jnp.full(loss_ref.shape, loss, F32)

    @pl.when(step > 0)
    def _():
        gproto_ref[...] += gproto
        loss_ref[...] += loss


def gradients(columns, row_totals, zsum, first, second, scores, unit, wnorm, count, total, proto_size):
    rows, protos = first.shape
    width = wnorm.shape[1]
    heat_scale = count / (32.0 * SOFTMAX_HEAT)
    return pl.pallas_call(
        functools.partial(gradient_kernel, count, total, heat_scale, proto_size),
        grid=(rows // BLOCK,),
        in_specs=[
            pl.BlockSpec(columns.shape, lambda i: (0, 0)),
            pl.BlockSpec((2, BLOCK), lambda i: (0, i)),
            pl.BlockSpec((zsum.shape[0], BLOCK), lambda i: (0, i)),
            pl.BlockSpec((BLOCK, protos), lambda i: (i, 0)),
            pl.BlockSpec((BLOCK, protos), lambda i: (i, 0)),
            pl.BlockSpec((BLOCK, protos), lambda i: (i, 0)),
            pl.BlockSpec((BLOCK, width), lambda i: (i, 0)),
            pl.BlockSpec((protos, width), lambda i: (0, 0), pipeline_mode=pl.Buffered(1)),
        ],
        out_specs=[
            pl.BlockSpec((BLOCK, width), lambda i: (i, 0)),
            pl.BlockSpec((protos, width), lambda i: (0, 0)),
            pl.BlockSpec((8, LANES), lambda i: (0, 0)),
        ],
        out_shape=[
            jax.ShapeDtypeStruct((rows, width), F32),
            jax.ShapeDtypeStruct((protos, width), F32),
            jax.ShapeDtypeStruct((8, LANES), F32),
        ],
        compiler_params=params(52),
        cost_estimate=cost(4 * rows * width * protos, 42 * MIB, rows * protos),
        name="gradients",
    )(columns, row_totals, zsum, first, second, scores, unit, wnorm)


def swap(value, axis, distance):
    size = lax.axis_size(axis)
    return lax.ppermute(value, axis, [(i, i ^ distance) for i in range(size)])


def on_device(embeddings, prototypes, partners):
    row_count, width = embeddings.shape
    proto_count = prototypes.shape[0]
    batch_size = lax.axis_size("batch")
    proto_size = lax.axis_size("proto")
    total_rows = row_count * batch_size
    centroids = proto_count * proto_size
    share = row_count // proto_size
    batch_index = lax.axis_index("batch")
    proto_index = lax.axis_index("proto")

    own = own_rows(embeddings, jnp.full((1,), proto_index, jnp.int32), share)
    table = lax.all_gather(own, ("batch", "proto"), axis=0, tiled=True)

    unit, wnorm, scores, expo, zsum, columns = scores_of(embeddings, prototypes)
    columns = lax.psum(columns, "batch")
    for iteration in range(ITERS - 1):
        row_part = row_pass(columns, expo, centroids)
        if iteration == 0:
            row_totals, zsum = lax.psum((row_part, zsum), "proto")
        else:
            row_totals = lax.psum(row_part, "proto")
        columns = lax.psum(column_pass(row_totals, expo, total_rows), "batch")

    first, second = partner_pass(partners[:, 0], partners[:, 1], table, wnorm)
    row_totals = lax.psum(partner_row_pass(columns, first, second, centroids), "proto")
    gunit, gproto, loss = gradients(
        columns, row_totals, zsum, first, second, scores, unit, wnorm, centroids, total_rows, proto_size
    )
    loss = lax.psum(loss[0, 0], ("batch", "proto")) / total_rows

    pairs = gunit.reshape(proto_size // 2, 2, share, width)
    core = proto_index % 2
    kept = lax.dynamic_index_in_dim(pairs, core, 1, keepdims=False)
    sent = lax.dynamic_index_in_dim(pairs, 1 - core, 1, keepdims=False)
    halves = kept + swap(sent, "proto", 1)
    own_place = proto_index // 2
    gunit = lax.dynamic_index_in_dim(halves, own_place, 0, keepdims=False)
    for distance in range(1, proto_size // 2):
        block = lax.dynamic_index_in_dim(halves, own_place ^ distance, 0, keepdims=False).astype(BF16)
        gunit = gunit + swap(block, "proto", 2 * distance).astype(F32)

    part = width // batch_size
    grad_proto = lax.dynamic_slice_in_dim(gproto, batch_index * part, part, 1)
    for distance in range(1, batch_size):
        block = lax.dynamic_slice_in_dim(gproto, (batch_index ^ distance) * part, part, 1).astype(BF16)
        grad_proto = grad_proto + swap(block, "batch", distance).astype(F32)

    hidden = lax.dynamic_slice_in_dim(embeddings, proto_index * share, share, 0).astype(F32)
    inverse = 1.0 / jnp.sqrt(jnp.sum(hidden * hidden, axis=1, keepdims=True) + NORM_EPSILON)
    along = jnp.sum(hidden * gunit, axis=1, keepdims=True)
    grad_embed = inverse * gunit - hidden * inverse * inverse * inverse * along
    return (loss, grad_proto, grad_embed)


def solution(mesh):
    return jax.shard_map(
        on_device,
        mesh=mesh,
        in_specs=(P("batch", None), P("proto", None), P("batch", None)),
        out_specs=(P(), P("proto", "batch"), P(("batch", "proto"), None)),
        check_vma=False,
    )
```

```python
import functools

import jax
import jax.numpy as jnp
from jax import lax
from jax.experimental import pallas as pl
from jax.experimental.pallas import tpu as pltpu
from jax.sharding import PartitionSpec as P

ITERS = 3
BALANCE_SMOOTHING = 0.05
SOFTMAX_HEAT = 0.1
NORM_EPSILON = 1e-06
LANES = 128
MIB = 1 << 20
F32 = jnp.float32
BF16 = jnp.bfloat16


def params(mib=60):
    return pltpu.CompilerParams(vmem_limit_bytes=mib * MIB)


def cost(flops, moved, exps=0):
    return pl.CostEstimate(flops=flops, bytes_accessed=moved, transcendentals=exps)


def normalized(block):
    wide = block.astype(F32)
    inverse = 1.0 / jnp.sqrt(jnp.sum(wide * wide, axis=1, keepdims=True) + NORM_EPSILON)
    return wide * inverse


def lane_row_sums(values):
    columns = values.shape[1]
    part = values[:, 0:LANES]
    for start in range(LANES, columns, LANES):
        part = part + values[:, start : start + LANES]
    return jnp.sum(part.T, axis=0, keepdims=True)


def split_rows(row):
    high = row.astype(BF16).astype(F32)
    middle = (row - high).astype(BF16).astype(F32)
    low = row - high - middle
    place = lax.broadcasted_iota(jnp.int32, (16, row.shape[1]), 0)
    stacked = jnp.where(place == 0, high, jnp.where(place == 1, middle, jnp.where(place == 2, low, 0.0)))
    return stacked.astype(BF16)


def total_of(refs):
    total = refs[0][...]
    for ref in refs[1:]:
        total = total + ref[...]
    return total


def own_rows_kernel(index_ref, embeddings_ref, table_ref, stage_ref):
    del index_ref
    rows, columns = embeddings_ref.shape
    unit = normalized(embeddings_ref[...]).astype(BF16).astype(F32)
    groups = columns // LANES
    for k in range(groups):
        stage_ref[pl.ds(k, rows, stride=groups), :] = unit[:, k * LANES : (k + 1) * LANES]
    table_ref[...] = stage_ref[...].reshape(rows, groups, LANES).astype(BF16)


def own_rows(embeddings, index, share):
    columns = embeddings.shape[1]
    groups = columns // LANES
    return pl.pallas_call(
        own_rows_kernel,
        grid_spec=pltpu.PrefetchScalarGridSpec(
            num_scalar_prefetch=1,
            grid=(1,),
            in_specs=[pl.BlockSpec((share, columns), lambda i, index: (index[0], 0))],
            out_specs=pl.BlockSpec((share, groups, LANES), lambda i, index: (0, 0, 0)),
            scratch_shapes=[pltpu.VMEM((share * groups, LANES), F32)],
        ),
        out_shape=jax.ShapeDtypeStruct((share, groups, LANES), BF16),
        compiler_params=params(),
        name="own_rows",
    )(index, embeddings)


def scores_kernel(embeddings_ref, prototypes_ref, unit_ref, wnorm_ref, scores_ref, expo_ref, zsum_ref, column_ref):
    step = pl.program_id(0)

    @pl.when(step == 0)
    def _():
        wnorm_ref[...] = normalized(prototypes_ref[...]).astype(BF16)

    unit = normalized(embeddings_ref[...]).astype(BF16)
    unit_ref[...] = unit
    scores = lax.dot_general(unit, wnorm_ref[...], (((1,), (1,)), ((), ())), preferred_element_type=F32)
    scores_ref[...] = scores
    soft = jnp.exp(scores * (1.0 / SOFTMAX_HEAT))
    zsum_ref[...] = lane_row_sums(soft)
    expo = soft * soft
    expo_ref[...] = expo.astype(BF16)
    sums = jnp.sum(expo, axis=0, keepdims=True)

    @pl.when(step == 0)
    def _():
        column_ref[...] = sums

    @pl.when(step > 0)
    def _():
        column_ref[...] += sums


def scores_of(embeddings, prototypes, share):
    rows, columns = embeddings.shape
    protos = prototypes.shape[0]
    return pl.pallas_call(
        scores_kernel,
        grid=(rows // share,),
        in_specs=[
            pl.BlockSpec((share, columns), lambda i: (i, 0)),
            pl.BlockSpec((protos, columns), lambda i: (0, 0), pipeline_mode=pl.Buffered(1)),
        ],
        out_specs=[
            pl.BlockSpec((share, columns), lambda i: (i, 0)),
            pl.BlockSpec((protos, columns), lambda i: (0, 0)),
            pl.BlockSpec((share, protos), lambda i: (i, 0)),
            pl.BlockSpec((share, protos), lambda i: (i, 0)),
            pl.BlockSpec((None, None, 1, share), lambda i: (i % 2, i // 2, 0, 0)),
            pl.BlockSpec((1, protos), lambda i: (0, 0)),
        ],
        out_shape=[
            jax.ShapeDtypeStruct((rows, columns), BF16),
            jax.ShapeDtypeStruct((protos, columns), BF16),
            jax.ShapeDtypeStruct((rows, protos), F32),
            jax.ShapeDtypeStruct((rows, protos), BF16),
            jax.ShapeDtypeStruct((2, rows // share // 2, 1, share), F32),
            jax.ShapeDtypeStruct((1, protos), F32),
        ],
        compiler_params=params(),
        cost_estimate=cost(2 * rows * columns * protos, 22 * MIB, rows * protos),
        name="scores",
    )(embeddings, prototypes)


def row_kernel(count, *refs):
    *column_refs, expo_ref, row_ref = refs
    scale = 1.0 / (count * total_of(column_refs))
    sums = lax.dot_general(
        split_rows(scale), expo_ref[...], (((1,), (1,)), ((), ())), preferred_element_type=F32
    )
    row_ref[...] = jnp.sum(sums, axis=0, keepdims=True)


def row_pass(columns, expo, count):
    rows, protos = expo.shape
    block = rows // 4
    return pl.pallas_call(
        functools.partial(row_kernel, count),
        grid=(rows // block,),
        in_specs=[pl.BlockSpec((1, protos), lambda i: (0, 0)) for _ in columns]
        + [pl.BlockSpec((block, protos), lambda i: (i, 0))],
        out_specs=pl.BlockSpec((1, block), lambda i: (0, i)),
        out_shape=jax.ShapeDtypeStruct((1, rows), F32),
        compiler_params=params(),
        cost_estimate=cost(2 * rows * protos, 4 * MIB),
        name="row_pass",
    )(*columns, expo)


def column_kernel(count, *refs):
    *row_refs, expo_ref, column_ref = refs
    step = pl.program_id(0)
    scale = 1.0 / (count * total_of(row_refs))
    sums = lax.dot_general(
        split_rows(scale), expo_ref[...], (((1,), (0,)), ((), ())), preferred_element_type=F32
    )
    sums = jnp.sum(sums, axis=0, keepdims=True)

    @pl.when(step == 0)
    def _():
        column_ref[...] = sums

    @pl.when(step > 0)
    def _():
        column_ref[...] += sums


def column_pass(row_totals, expo, count):
    rows, protos = expo.shape
    block = rows // 4
    return pl.pallas_call(
        functools.partial(column_kernel, count),
        grid=(rows // block,),
        in_specs=[pl.BlockSpec((1, block), lambda i: (0, i)) for _ in row_totals]
        + [pl.BlockSpec((block, protos), lambda i: (i, 0))],
        out_specs=pl.BlockSpec((1, protos), lambda i: (0, 0)),
        out_shape=jax.ShapeDtypeStruct((1, protos), F32),
        compiler_params=params(),
        cost_estimate=cost(2 * rows * protos, 4 * MIB),
        name="column_pass",
    )(*row_totals, expo)


CHUNK = 256


def partner_kernel(first_ref, second_ref, table_ref, wnorm_ref, first_expo_ref, second_expo_ref, *stages):
    step = pl.program_id(0)
    groups = table_ref.shape[1]
    rows = first_expo_ref.shape[0]
    wnorm = wnorm_ref[...]
    chunks = [
        (which_ref, out_ref, start)
        for start in range(0, rows, CHUNK)
        for which_ref, out_ref in ((first_ref, first_expo_ref), (second_ref, second_expo_ref))
    ]
    for (which_ref, out_ref, start), stage_ref in zip(chunks, stages):
        for row in range(CHUNK):
            place = which_ref[step * rows + start + row]
            stage_ref[row * groups : (row + 1) * groups, :] = table_ref[place].astype(F32)
        unit = jnp.concatenate(
            [stage_ref[pl.ds(k, CHUNK, stride=groups), :].astype(BF16) for k in range(groups)], axis=1
        )
        scores = lax.dot_general(unit, wnorm, (((1,), (1,)), ((), ())), preferred_element_type=F32)
        soft = jnp.exp(scores * (1.0 / SOFTMAX_HEAT))
        out_ref[start : start + CHUNK, :] = (soft * soft).astype(out_ref.dtype)


def partner_pass(first, second, table, wnorm):
    rows = first.shape[0]
    protos, columns = wnorm.shape
    groups = columns // LANES
    block = 2 * CHUNK
    return pl.pallas_call(
        partner_kernel,
        grid_spec=pltpu.PrefetchScalarGridSpec(
            num_scalar_prefetch=2,
            grid=(rows // block,),
            in_specs=[
                pl.BlockSpec(table.shape, lambda i, *_: (0, 0, 0), pipeline_mode=pl.Buffered(1)),
                pl.BlockSpec((protos, columns), lambda i, *_: (0, 0), pipeline_mode=pl.Buffered(1)),
            ],
            out_specs=[
                pl.BlockSpec((block, protos), lambda i, *_: (i, 0)),
                pl.BlockSpec((block, protos), lambda i, *_: (i, 0)),
            ],
            scratch_shapes=[pltpu.VMEM((CHUNK * groups, LANES), F32)] * 4,
        ),
        out_shape=[jax.ShapeDtypeStruct((rows, protos), BF16)] * 2,
        compiler_params=params(),
        cost_estimate=cost(4 * rows * columns * protos, 28 * MIB, 2 * rows * protos),
        name="partner_scores",
    )(first, second, table, wnorm)


def partner_row_kernel(count, *refs):
    *column_refs, zsum_ref, first_ref, second_ref, row_ref = refs
    scale = 1.0 / (count * total_of(column_refs))
    row_ref[...] = jnp.concatenate(
        [
            lane_row_sums(first_ref[...].astype(F32) * scale),
            lane_row_sums(second_ref[...].astype(F32) * scale),
            zsum_ref[...],
        ],
        axis=0,
    )


def partner_row_pass(columns, zsum, first, second, count):
    rows, protos = first.shape
    share = zsum.shape[-1]
    return pl.pallas_call(
        functools.partial(partner_row_kernel, count),
        grid=(rows // share,),
        in_specs=[pl.BlockSpec((1, protos), lambda i: (0, 0)) for _ in columns]
        + [
            pl.BlockSpec((None, None, 1, share), lambda i: (i % 2, i // 2, 0, 0)),
            pl.BlockSpec((share, protos), lambda i: (i, 0)),
            pl.BlockSpec((share, protos), lambda i: (i, 0)),
        ],
        out_specs=pl.BlockSpec((None, None, 3, share), lambda i: (i % 2, i // 2, 0, 0)),
        out_shape=jax.ShapeDtypeStruct((2, rows // share // 2, 3, share), F32),
        compiler_params=params(),
        cost_estimate=cost(4 * rows * protos, 8 * MIB),
        name="partner_row_pass",
    )(*columns, zsum, first, second)


def gradient_kernel(count, total, heat_scale, proto_size, parts, core_ref, *refs):
    del core_ref
    column_refs, row_refs = refs[: parts[0]], refs[parts[0] : parts[0] + parts[1]]
    first_ref, second_ref, scores_ref, wnorm_ref, gunit_ref, dscore_ref, loss_ref = refs[parts[0] + parts[1] :]
    step = pl.program_id(0)
    scale = 1.0 / (count * total_of(column_refs))
    totals = total_of(row_refs)
    share = totals.shape[-1]
    place = lax.broadcasted_iota(jnp.int32, (8, share), 0)
    loss = jnp.zeros((), F32)
    for group in range(totals.shape[0]):
        row_totals, zsum = totals[group, 0:2], totals[group, 2:3]
        weights = total * (1.0 / (total * row_totals))
        code_totals = 0.5 * jnp.sum(weights * row_totals, axis=0, keepdims=True)
        log_part = jnp.sum(code_totals * jnp.log(zsum)) * (1.0 / proto_size)
        stacked = jnp.where(
            place == 0,
            weights[0:1],
            jnp.where(place == 1, weights[1:2], jnp.where(place == 2, code_totals / zsum, 0.0)),
        ).T
        first = (stacked[:, 0:1] * first_ref[group].astype(F32) * scale).astype(BF16).astype(F32)
        second = (stacked[:, 1:2] * second_ref[group].astype(F32) * scale).astype(BF16).astype(F32)
        targets = 0.5 * (first + second)
        heated = scores_ref[group] * (1.0 / SOFTMAX_HEAT)
        loss = loss + (log_part - jnp.sum(targets * heated))
        dscore = ((jnp.exp(heated) * stacked[:, 2:3] - targets) * heat_scale).astype(BF16)
        dscore_ref[group] = dscore
        gunit = jnp.dot(dscore, wnorm_ref[...], preferred_element_type=F32)
        gunit_ref[group] = gunit.astype(gunit_ref.dtype)

    @pl.when(step == 0)
    def _():
        loss_ref[...] = jnp.full(loss_ref.shape, loss, F32)

    @pl.when(step > 0)
    def _():
        loss_ref[...] += loss


def gradients(core, columns, row_totals, first, second, scores, wnorm, count, total, proto_size, dtype):
    rows, protos = first.shape
    width = wnorm.shape[1]
    heat_scale = count / (32.0 * SOFTMAX_HEAT)
    _, places, _, share = row_totals[0].shape
    group = 2
    by_core = pl.BlockSpec((group, None, share, protos), lambda i, core: (i, core[0], 0, 0))
    first, second, scores = [value.reshape(places, 2, share, protos) for value in (first, second, scores)]
    return pl.pallas_call(
        functools.partial(
            gradient_kernel, count, total, heat_scale, proto_size, (len(columns), len(row_totals))
        ),
        grid_spec=pltpu.PrefetchScalarGridSpec(
            num_scalar_prefetch=1,
            grid=(places // group,),
            in_specs=[pl.BlockSpec((1, protos), lambda i, core: (0, 0)) for _ in columns]
            + [pl.BlockSpec((None, group, 3, share), lambda i, core: (core[0], i, 0, 0)) for _ in row_totals]
            + [
                by_core,
                by_core,
                by_core,
                pl.BlockSpec((protos, width), lambda i, core: (0, 0), pipeline_mode=pl.Buffered(1)),
            ],
            out_specs=[
                pl.BlockSpec((group, share, width), lambda i, core: (i, 0, 0)),
                pl.BlockSpec((group, share, protos), lambda i, core: (i, 0, 0)),
                pl.BlockSpec((1, LANES), lambda i, core: (0, 0)),
            ],
        ),
        out_shape=[
            jax.ShapeDtypeStruct((places, share, width), dtype),
            jax.ShapeDtypeStruct((places, share, protos), BF16),
            jax.ShapeDtypeStruct((1, LANES), F32),
        ],
        compiler_params=params(),
        cost_estimate=cost(rows * width * protos, 16 * MIB, rows * protos // 2),
        name="gradients",
    )(core, *columns, *row_totals, first, second, scores, wnorm)


def combine_kernel(place_ref, kept_ref, received_ref, own_ref, sent_ref):
    del place_ref
    total = kept_ref[...] + received_ref[...].astype(F32)
    sent_ref[...] = total.astype(BF16)
    own_ref[...] = total


def combine(place, kept, received):
    places, share, width = kept.shape
    last = places - 1
    at = pl.BlockSpec((None, share, width), lambda i, place: (place[0] ^ (last - i), 0, 0))
    return pl.pallas_call(
        combine_kernel,
        grid_spec=pltpu.PrefetchScalarGridSpec(
            num_scalar_prefetch=1,
            grid=(places,),
            in_specs=[at, at],
            out_specs=[
                pl.BlockSpec((share, width), lambda i, place: (0, 0)),
                pl.BlockSpec((None, share, width), lambda i, place: (last - i, 0, 0)),
            ],
        ),
        out_shape=[jax.ShapeDtypeStruct((share, width), F32), jax.ShapeDtypeStruct(kept.shape, BF16)],
        compiler_params=params(),
        cost_estimate=cost(places * share * width, 9 * MIB),
        name="combine",
    )(place, kept, received)


def proto_gradient_kernel(index_ref, own_dscore_ref, other_dscore_ref, own_unit_ref, other_unit_ref, own_ref, sent_ref):
    del index_ref
    rows = own_dscore_ref.shape[0]
    part = own_unit_ref.shape[-1]
    both = (((0,), (0,)), ((), ()))
    total = lax.dot_general(
        own_dscore_ref[...], own_unit_ref[...].reshape(rows, part), both, preferred_element_type=F32
    ) + lax.dot_general(
        other_dscore_ref[...], other_unit_ref[...].reshape(rows, part), both, preferred_element_type=F32
    )
    sent_ref[...] = total.astype(BF16)
    own_ref[...] = total


def proto_gradient(index, own_dscore, other_dscore, unit, batch_size):
    places, share, protos = own_dscore.shape
    width = unit.shape[1]
    part = width // batch_size
    rows = places * share
    last = batch_size - 1
    unit = unit.reshape(places, 2, share, width)
    dscore_at = pl.BlockSpec((rows, protos), lambda i, index: (0, 0), pipeline_mode=pl.Buffered(1))
    return pl.pallas_call(
        proto_gradient_kernel,
        grid_spec=pltpu.PrefetchScalarGridSpec(
            num_scalar_prefetch=1,
            grid=(batch_size,),
            in_specs=[
                dscore_at,
                dscore_at,
                pl.BlockSpec((places, None, share, part), lambda i, index: (0, index[1], 0, index[0] ^ (last - i))),
                pl.BlockSpec((places, None, share, part), lambda i, index: (0, 1 - index[1], 0, index[0] ^ (last - i))),
            ],
            out_specs=[
                pl.BlockSpec((protos, part), lambda i, index: (0, 0)),
                pl.BlockSpec((None, protos, part), lambda i, index: (last - i, 0, 0)),
            ],
        ),
        out_shape=[
            jax.ShapeDtypeStruct((protos, part), F32),
            jax.ShapeDtypeStruct((batch_size, protos, part), BF16),
        ],
        compiler_params=params(),
        cost_estimate=cost(4 * rows * protos * width, 12 * MIB),
        name="proto_gradient",
    )(index, own_dscore.reshape(rows, protos), other_dscore.reshape(rows, protos), unit, unit)


def embed_gradient_kernel(index_ref, embeddings_ref, own_ref, *refs):
    del index_ref
    *received_refs, out_ref = refs
    gunit = own_ref[...]
    for ref in received_refs:
        gunit = gunit + ref[...].astype(F32)
    hidden = embeddings_ref[...].astype(F32)
    inverse = 1.0 / jnp.sqrt(jnp.sum(hidden * hidden, axis=1, keepdims=True) + NORM_EPSILON)
    along = jnp.sum(hidden * gunit, axis=1, keepdims=True)
    out_ref[...] = inverse * gunit - hidden * (inverse * inverse * inverse * along)


def embed_gradient(index, embeddings, own, received):
    share, width = own.shape
    whole = pl.BlockSpec((share, width), lambda i, index: (0, 0))
    return pl.pallas_call(
        embed_gradient_kernel,
        grid_spec=pltpu.PrefetchScalarGridSpec(
            num_scalar_prefetch=1,
            grid=(1,),
            in_specs=[pl.BlockSpec((share, width), lambda i, index: (index[0], 0))] + [whole] * (1 + len(received)),
            out_specs=whole,
        ),
        out_shape=jax.ShapeDtypeStruct((share, width), F32),
        compiler_params=params(),
        cost_estimate=cost(8 * share * width, 4 * MIB),
        name="embed_gradient",
    )(index, embeddings, own, *received)


def swap(value, axis, distance):
    size = lax.axis_size(axis)
    return lax.ppermute(value, axis, [(i, i ^ distance) for i in range(size)])


def parts_of(value, axis):
    size = lax.axis_size(axis)
    if size > 8:
        return [lax.psum(value, axis)]
    return [value] + [swap(value, axis, distance) for distance in range(1, size)]


def scalar(value):
    return jnp.full((1,), value, jnp.int32)


def on_device(embeddings, prototypes, partners):
    row_count, width = embeddings.shape
    proto_count = prototypes.shape[0]
    batch_size = lax.axis_size("batch")
    proto_size = lax.axis_size("proto")
    total_rows = row_count * batch_size
    centroids = proto_count * proto_size
    share = row_count // proto_size
    places = proto_size // 2
    batch_index = lax.axis_index("batch")
    proto_index = lax.axis_index("proto")
    core = proto_index % 2
    place = proto_index // 2

    own = own_rows(embeddings, scalar(proto_index), share)
    table = lax.all_gather(own, ("batch", "proto"), axis=0, tiled=True)

    unit, wnorm, scores, expo, zsum, columns = scores_of(embeddings, prototypes, share)
    columns = parts_of(columns, "batch")
    for iteration in range(ITERS - 1):
        row_totals = parts_of(row_pass(columns, expo, centroids), "proto")
        columns = parts_of(column_pass(row_totals, expo, total_rows), "batch")

    first, second = partner_pass(partners[:, 0], partners[:, 1], table, wnorm)
    row_totals = parts_of(partner_row_pass(columns, zsum, first, second, centroids), "proto")
    shared = (columns, row_totals, first, second, scores, wnorm, centroids, total_rows, proto_size)
    other_gunit, other_dscore, other_loss = gradients(scalar(1 - core), *shared, BF16)
    received = swap(other_gunit, "proto", 1)
    kept, own_dscore, own_loss = gradients(scalar(core), *shared, F32)

    own_gunit, sent = combine(scalar(place), kept, received)
    arrived = [swap(sent[distance], "proto", 2 * distance) for distance in range(places - 1, 0, -1)]

    loss = own_loss + other_loss
    for axis in ("batch", "proto"):
        loss = functools.reduce(jnp.add, parts_of(loss, axis))
    loss = loss[0, 0] / total_rows

    grad_proto, sent = proto_gradient(jnp.stack([batch_index, core]).astype(jnp.int32), own_dscore, other_dscore, unit, batch_size)
    for distance in range(batch_size - 1, 0, -1):
        grad_proto = grad_proto + swap(sent[distance], "batch", distance).astype(F32)

    grad_embed = embed_gradient(scalar(proto_index), embeddings, own_gunit, arrived)
    return (loss, grad_proto, grad_embed)


def solution(mesh):
    return jax.shard_map(
        on_device,
        mesh=mesh,
        in_specs=(P("batch", None), P("proto", None), P("batch", None)),
        out_specs=(P(), P("proto", "batch"), P(("batch", "proto"), None)),
        check_vma=False,
    )
```

```python
import functools

import jax
import jax.numpy as jnp
from jax import lax
from jax.experimental import pallas as pl
from jax.experimental.pallas import tpu as pltpu
from jax.sharding import PartitionSpec as P

ITERS = 3
BALANCE_SMOOTHING = 0.05
SOFTMAX_HEAT = 0.1
NORM_EPSILON = 1e-06
LANES = 128
CHUNK = 256
STREAMS = 4
OFFLOADED = 768
OWN_BLOCK = 128
MIB = 1 << 20
F32 = jnp.float32
BF16 = jnp.bfloat16


def params(mib=60):
    return pltpu.CompilerParams(vmem_limit_bytes=mib * MIB)


def cost(flops, moved, exps=0):
    return pl.CostEstimate(flops=flops, bytes_accessed=moved, transcendentals=exps)


def normalized(block):
    wide = block.astype(F32)
    inverse = 1.0 / jnp.sqrt(jnp.sum(wide * wide, axis=1, keepdims=True) + NORM_EPSILON)
    return wide * inverse


def lane_row_sums(values):
    columns = values.shape[1]
    part = values[:, 0:LANES]
    for start in range(LANES, columns, LANES):
        part = part + values[:, start : start + LANES]
    return jnp.sum(part.T, axis=0, keepdims=True)


def split_rows(row):
    high = row.astype(BF16).astype(F32)
    middle = (row - high).astype(BF16).astype(F32)
    low = row - high - middle
    place = lax.broadcasted_iota(jnp.int32, (16, row.shape[1]), 0)
    stacked = jnp.where(place == 0, high, jnp.where(place == 1, middle, jnp.where(place == 2, low, 0.0)))
    return stacked.astype(BF16)


def total_of(refs):
    total = refs[0][...]
    for ref in refs[1:]:
        total = total + ref[...]
    return total


def own_rows_kernel(index_ref, embeddings_ref, table_ref, stage_ref):
    del index_ref
    rows, columns = embeddings_ref.shape
    unit = normalized(embeddings_ref[...]).astype(BF16).astype(F32)
    groups = columns // LANES
    for k in range(groups):
        stage_ref[pl.ds(k, rows, stride=groups), :] = unit[:, k * LANES : (k + 1) * LANES]
    table_ref[...] = stage_ref[...].reshape(rows, groups, LANES).astype(BF16)


def own_rows(embeddings, index, block, count):
    columns = embeddings.shape[1]
    groups = columns // LANES
    return pl.pallas_call(
        own_rows_kernel,
        grid_spec=pltpu.PrefetchScalarGridSpec(
            num_scalar_prefetch=1,
            grid=(count,),
            in_specs=[pl.BlockSpec((block, columns), lambda i, index: (index[0] + i, 0))],
            out_specs=pl.BlockSpec((block, groups, LANES), lambda i, index: (i, 0, 0)),
            scratch_shapes=[pltpu.VMEM((block * groups, LANES), F32)],
        ),
        out_shape=jax.ShapeDtypeStruct((block * count, groups, LANES), BF16),
        compiler_params=params(),
        name="own_rows",
    )(index, embeddings)


def scores_kernel(embeddings_ref, prototypes_ref, unit_ref, wnorm_ref, scores_ref, expo_ref, zsum_ref, column_ref):
    step = pl.program_id(0)

    @pl.when(step == 0)
    def _():
        wnorm_ref[...] = normalized(prototypes_ref[...]).astype(BF16)

    unit = normalized(embeddings_ref[...]).astype(BF16)
    unit_ref[...] = unit
    scores = lax.dot_general(unit, wnorm_ref[...], (((1,), (1,)), ((), ())), preferred_element_type=F32)
    scores_ref[...] = scores
    soft = jnp.exp(scores * (1.0 / SOFTMAX_HEAT))
    zsum_ref[...] = lane_row_sums(soft)
    expo = soft * soft
    expo_ref[...] = expo.astype(BF16)
    sums = jnp.sum(expo, axis=0, keepdims=True)

    @pl.when(step == 0)
    def _():
        column_ref[...] = sums

    @pl.when(step > 0)
    def _():
        column_ref[...] += sums


def scores_of(embeddings, prototypes, share):
    rows, columns = embeddings.shape
    protos = prototypes.shape[0]
    return pl.pallas_call(
        scores_kernel,
        grid=(rows // share,),
        in_specs=[
            pl.BlockSpec((share, columns), lambda i: (i, 0)),
            pl.BlockSpec((protos, columns), lambda i: (0, 0), pipeline_mode=pl.Buffered(1)),
        ],
        out_specs=[
            pl.BlockSpec((share, columns), lambda i: (i, 0)),
            pl.BlockSpec((protos, columns), lambda i: (0, 0)),
            pl.BlockSpec((share, protos), lambda i: (i, 0)),
            pl.BlockSpec((share, protos), lambda i: (i, 0)),
            pl.BlockSpec((None, None, 1, share), lambda i: (i % 2, i // 2, 0, 0)),
            pl.BlockSpec((1, protos), lambda i: (0, 0)),
        ],
        out_shape=[
            jax.ShapeDtypeStruct((rows, columns), BF16),
            jax.ShapeDtypeStruct((protos, columns), BF16),
            jax.ShapeDtypeStruct((rows, protos), F32),
            jax.ShapeDtypeStruct((rows, protos), BF16),
            jax.ShapeDtypeStruct((2, rows // share // 2, 1, share), F32),
            jax.ShapeDtypeStruct((1, protos), F32),
        ],
        compiler_params=params(),
        cost_estimate=cost(2 * rows * columns * protos, 22 * MIB, rows * protos),
        name="scores",
    )(embeddings, prototypes)


def row_kernel(count, parts, *refs):
    column_refs, expo_refs, row_ref = refs[:parts], refs[parts:-1], refs[-1]
    scale = split_rows(1.0 / (count * total_of(column_refs)))
    block = expo_refs[0].shape[0]
    for k, expo_ref in enumerate(expo_refs):
        sums = lax.dot_general(scale, expo_ref[...], (((1,), (1,)), ((), ())), preferred_element_type=F32)
        row_ref[:, k * block : (k + 1) * block] = jnp.sum(sums, axis=0, keepdims=True)


def streams_of(shape):
    return [pl.BlockSpec(shape, functools.partial(lambda k, i: (STREAMS * i + k, 0), k)) for k in range(STREAMS)]


def row_pass(columns, expo, count):
    rows, protos = expo.shape
    block = rows // 8
    return pl.pallas_call(
        functools.partial(row_kernel, count, len(columns)),
        grid=(rows // block // STREAMS,),
        in_specs=[pl.BlockSpec((1, protos), lambda i: (0, 0)) for _ in columns] + streams_of((block, protos)),
        out_specs=pl.BlockSpec((1, STREAMS * block), lambda i: (0, i)),
        out_shape=jax.ShapeDtypeStruct((1, rows), F32),
        compiler_params=params(),
        cost_estimate=cost(2 * rows * protos, 4 * MIB),
        name="row_pass",
    )(*columns, *[expo] * STREAMS)


def column_kernel(count, parts, *refs):
    row_refs, expo_refs, column_ref = refs[:parts], refs[parts:-1], refs[-1]
    step = pl.program_id(0)
    scale = split_rows(1.0 / (count * total_of(row_refs)))
    block = expo_refs[0].shape[0]
    total = None
    for k, expo_ref in enumerate(expo_refs):
        sums = lax.dot_general(
            scale[:, k * block : (k + 1) * block], expo_ref[...], (((1,), (0,)), ((), ())), preferred_element_type=F32
        )
        total = sums if total is None else total + sums
    total = jnp.sum(total, axis=0, keepdims=True)

    @pl.when(step == 0)
    def _():
        column_ref[...] = total

    @pl.when(step > 0)
    def _():
        column_ref[...] += total


def column_pass(row_totals, expo, count):
    rows, protos = expo.shape
    block = rows // 8
    return pl.pallas_call(
        functools.partial(column_kernel, count, len(row_totals)),
        grid=(rows // block // STREAMS,),
        in_specs=[pl.BlockSpec((1, STREAMS * block), lambda i: (0, i)) for _ in row_totals]
        + streams_of((block, protos)),
        out_specs=pl.BlockSpec((1, protos), lambda i: (0, 0)),
        out_shape=jax.ShapeDtypeStruct((1, protos), F32),
        compiler_params=params(),
        cost_estimate=cost(2 * rows * protos, 4 * MIB),
        name="column_pass",
    )(*row_totals, *[expo] * STREAMS)


def partner_kernel(pieces, first_ref, second_ref, places_ref, *refs):
    piece_refs = refs[: len(pieces)]
    wnorm_ref, first_expo_ref, second_expo_ref, table_ref, semaphores, *stages = refs[len(pieces) :]
    step = pl.program_id(0)
    groups = table_ref.shape[1]

    @pl.when(step == 0)
    def _():
        copies, place = [], 0
        for piece_ref, (size, count) in zip(piece_refs, pieces):
            for k in range(count):
                copies.append(
                    pltpu.make_async_copy(
                        piece_ref.at[pl.ds(k * size, size)],
                        table_ref.at[pl.ds(places_ref[place], size)],
                        semaphores.at[place],
                    )
                )
                place += 1
        for copy in copies:
            copy.start()
        for copy in copies:
            copy.wait()

    rows = first_expo_ref.shape[0]
    wnorm = wnorm_ref[...]
    chunks = [
        (which_ref, out_ref, start)
        for start in range(0, rows, CHUNK)
        for which_ref, out_ref in ((first_ref, first_expo_ref), (second_ref, second_expo_ref))
    ]
    for (which_ref, out_ref, start), stage_ref in zip(chunks, stages):
        for row in range(CHUNK):
            place = which_ref[step * rows + start + row]
            stage_ref[row * groups : (row + 1) * groups, :] = table_ref[place].astype(F32)
        unit = jnp.concatenate(
            [stage_ref[pl.ds(k, CHUNK, stride=groups), :].astype(BF16) for k in range(groups)], axis=1
        )
        scores = lax.dot_general(unit, wnorm, (((1,), (1,)), ((), ())), preferred_element_type=F32)
        soft = jnp.exp(scores * (1.0 / SOFTMAX_HEAT))
        out_ref[start : start + CHUNK, :] = (soft * soft).astype(out_ref.dtype)


def partner_pass(first, second, pieces, wnorm, total_rows):
    rows = first.shape[0]
    protos, columns = wnorm.shape
    groups = columns // LANES
    block = 2 * CHUNK
    places = jnp.stack([place for _, _, at in pieces for place in at]).astype(jnp.int32)
    shapes = tuple((size, len(at)) for _, size, at in pieces)
    return pl.pallas_call(
        functools.partial(partner_kernel, shapes),
        grid_spec=pltpu.PrefetchScalarGridSpec(
            num_scalar_prefetch=3,
            grid=(rows // block,),
            in_specs=[pl.BlockSpec(memory_space=pl.ANY) for _ in pieces]
            + [pl.BlockSpec((protos, columns), lambda i, *_: (0, 0), pipeline_mode=pl.Buffered(1))],
            out_specs=[
                pl.BlockSpec((block, protos), lambda i, *_: (i, 0)),
                pl.BlockSpec((block, protos), lambda i, *_: (i, 0)),
            ],
            scratch_shapes=[
                pltpu.VMEM((total_rows, groups, LANES), BF16),
                pltpu.SemaphoreType.DMA((places.shape[0],)),
            ]
            + [pltpu.VMEM((CHUNK * groups, LANES), F32)] * 4,
        ),
        out_shape=[jax.ShapeDtypeStruct((rows, protos), BF16)] * 2,
        compiler_params=params(),
        cost_estimate=cost(4 * rows * columns * protos, 28 * MIB, 2 * rows * protos),
        name="partner_scores",
    )(first, second, places, *[piece for piece, _, _ in pieces], wnorm)


def partner_row_kernel(count, parts, *refs):
    column_refs, zsum_ref, row_ref = refs[:parts], refs[parts], refs[-1]
    first_refs, second_refs = refs[parts + 1 : parts + 1 + STREAMS], refs[parts + 1 + STREAMS : -1]
    scale = 1.0 / (count * total_of(column_refs))
    for k in range(STREAMS):
        at = (k % 2, k // 2)
        row_ref[at] = jnp.concatenate(
            [
                lane_row_sums(first_refs[k][...].astype(F32) * scale),
                lane_row_sums(second_refs[k][...].astype(F32) * scale),
                zsum_ref[at],
            ],
            axis=0,
        )


def partner_row_pass(columns, zsum, first, second, count):
    rows, protos = first.shape
    share = zsum.shape[-1]
    group = STREAMS // 2
    return pl.pallas_call(
        functools.partial(partner_row_kernel, count, len(columns)),
        grid=(rows // share // STREAMS,),
        in_specs=[pl.BlockSpec((1, protos), lambda i: (0, 0)) for _ in columns]
        + [pl.BlockSpec((2, group, 1, share), lambda i: (0, i, 0, 0))]
        + streams_of((share, protos)) * 2,
        out_specs=pl.BlockSpec((2, group, 3, share), lambda i: (0, i, 0, 0)),
        out_shape=jax.ShapeDtypeStruct((2, rows // share // 2, 3, share), F32),
        compiler_params=params(),
        cost_estimate=cost(4 * rows * protos, 8 * MIB),
        name="partner_row_pass",
    )(*columns, zsum, *[first] * STREAMS, *[second] * STREAMS)


def gradient_kernel(count, total, heat_scale, proto_size, parts, core_ref, *refs):
    del core_ref
    column_refs, row_refs = refs[: parts[0]], refs[parts[0] : parts[0] + parts[1]]
    first_ref, second_ref, scores_ref, wnorm_ref, gunit_ref, dscore_ref, loss_ref = refs[parts[0] + parts[1] :]
    step = pl.program_id(0)
    scale = 1.0 / (count * total_of(column_refs))
    totals = total_of(row_refs)
    share = totals.shape[-1]
    place = lax.broadcasted_iota(jnp.int32, (8, share), 0)
    loss = jnp.zeros((), F32)
    for group in range(totals.shape[0]):
        row_totals, zsum = totals[group, 0:2], totals[group, 2:3]
        weights = total * (1.0 / (total * row_totals))
        code_totals = 0.5 * jnp.sum(weights * row_totals, axis=0, keepdims=True)
        log_part = jnp.sum(code_totals * jnp.log(zsum)) * (1.0 / proto_size)
        stacked = jnp.where(
            place == 0,
            weights[0:1],
            jnp.where(place == 1, weights[1:2], jnp.where(place == 2, code_totals / zsum, 0.0)),
        ).T
        first = (stacked[:, 0:1] * first_ref[group].astype(F32) * scale).astype(BF16).astype(F32)
        second = (stacked[:, 1:2] * second_ref[group].astype(F32) * scale).astype(BF16).astype(F32)
        targets = 0.5 * (first + second)
        heated = scores_ref[group] * (1.0 / SOFTMAX_HEAT)
        loss = loss + (log_part - jnp.sum(targets * heated))
        dscore = ((jnp.exp(heated) * stacked[:, 2:3] - targets) * heat_scale).astype(BF16)
        dscore_ref[group] = dscore
        gunit = jnp.dot(dscore, wnorm_ref[...], preferred_element_type=F32)
        gunit_ref[group] = gunit.astype(gunit_ref.dtype)

    @pl.when(step == 0)
    def _():
        loss_ref[...] = jnp.full(loss_ref.shape, loss, F32)

    @pl.when(step > 0)
    def _():
        loss_ref[...] += loss


def gradients(core, columns, row_totals, first, second, scores, wnorm, count, total, proto_size, dtype):
    rows, protos = first.shape
    width = wnorm.shape[1]
    heat_scale = count / (32.0 * SOFTMAX_HEAT)
    _, places, _, share = row_totals[0].shape
    group = 2
    by_core = pl.BlockSpec((group, None, share, protos), lambda i, core: (i, core[0], 0, 0))
    first, second, scores = [value.reshape(places, 2, share, protos) for value in (first, second, scores)]
    return pl.pallas_call(
        functools.partial(
            gradient_kernel, count, total, heat_scale, proto_size, (len(columns), len(row_totals))
        ),
        grid_spec=pltpu.PrefetchScalarGridSpec(
            num_scalar_prefetch=1,
            grid=(places // group,),
            in_specs=[pl.BlockSpec((1, protos), lambda i, core: (0, 0)) for _ in columns]
            + [pl.BlockSpec((None, group, 3, share), lambda i, core: (core[0], i, 0, 0)) for _ in row_totals]
            + [
                by_core,
                by_core,
                by_core,
                pl.BlockSpec((protos, width), lambda i, core: (0, 0), pipeline_mode=pl.Buffered(1)),
            ],
            out_specs=[
                pl.BlockSpec((group, share, width), lambda i, core: (i, 0, 0)),
                pl.BlockSpec((group, share, protos), lambda i, core: (i, 0, 0)),
                pl.BlockSpec((1, LANES), lambda i, core: (0, 0)),
            ],
        ),
        out_shape=[
            jax.ShapeDtypeStruct((places, share, width), dtype),
            jax.ShapeDtypeStruct((places, share, protos), BF16),
            jax.ShapeDtypeStruct((1, LANES), F32),
        ],
        compiler_params=params(),
        cost_estimate=cost(rows * width * protos, 16 * MIB, rows * protos // 2),
        name="gradients",
    )(core, *columns, *row_totals, first, second, scores, wnorm)


def combine_kernel(bit_ref, own_kept_ref, own_received_ref, other_kept_ref, other_received_ref, own_ref, sent_ref):
    del bit_ref
    sent_ref[...] = (other_kept_ref[...] + other_received_ref[...].astype(F32)).astype(BF16)
    own_ref[...] = own_kept_ref[...] + own_received_ref[...].astype(F32)


def combine(bit, kept, received):
    count, share, width = kept.shape
    kept, received = [value.reshape(count // 2, 2, share, width) for value in (kept, received)]
    own_at = pl.BlockSpec((None, None, share, width), lambda i, bit: (i, bit[0], 0, 0))
    other_at = pl.BlockSpec((None, None, share, width), lambda i, bit: (i, 1 - bit[0], 0, 0))
    out_at = pl.BlockSpec((None, share, width), lambda i, bit: (i, 0, 0))
    return pl.pallas_call(
        combine_kernel,
        grid_spec=pltpu.PrefetchScalarGridSpec(
            num_scalar_prefetch=1,
            grid=(count // 2,),
            in_specs=[own_at, own_at, other_at, other_at],
            out_specs=[out_at, out_at],
        ),
        out_shape=[
            jax.ShapeDtypeStruct((count // 2, share, width), F32),
            jax.ShapeDtypeStruct((count // 2, share, width), BF16),
        ],
        compiler_params=params(),
        cost_estimate=cost(count * share * width, 9 * count * share * width),
        name="combine",
    )(bit, kept, received, kept, received)


def proto_gradient_kernel(index_ref, own_dscore_ref, other_dscore_ref, own_unit_ref, other_unit_ref, own_ref, sent_ref):
    del index_ref
    rows = own_dscore_ref.shape[0]
    part = own_unit_ref.shape[-1]
    both = (((0,), (0,)), ((), ()))
    total = lax.dot_general(
        own_dscore_ref[...], own_unit_ref[...].reshape(rows, part), both, preferred_element_type=F32
    ) + lax.dot_general(
        other_dscore_ref[...], other_unit_ref[...].reshape(rows, part), both, preferred_element_type=F32
    )
    sent_ref[...] = total.astype(BF16)
    own_ref[...] = total


def proto_gradient(index, own_dscore, other_dscore, unit, batch_size):
    places, share, protos = own_dscore.shape
    width = unit.shape[1]
    part = width // batch_size
    rows = places * share
    last = batch_size - 1
    unit = unit.reshape(places, 2, share, width)
    dscore_at = pl.BlockSpec((rows, protos), lambda i, index: (0, 0), pipeline_mode=pl.Buffered(1))
    return pl.pallas_call(
        proto_gradient_kernel,
        grid_spec=pltpu.PrefetchScalarGridSpec(
            num_scalar_prefetch=1,
            grid=(batch_size,),
            in_specs=[
                dscore_at,
                dscore_at,
                pl.BlockSpec((places, None, share, part), lambda i, index: (0, index[1], 0, index[0] ^ (last - i))),
                pl.BlockSpec((places, None, share, part), lambda i, index: (0, 1 - index[1], 0, index[0] ^ (last - i))),
            ],
            out_specs=[
                pl.BlockSpec((protos, part), lambda i, index: (0, 0)),
                pl.BlockSpec((None, protos, part), lambda i, index: (last - i, 0, 0)),
            ],
        ),
        out_shape=[
            jax.ShapeDtypeStruct((protos, part), F32),
            jax.ShapeDtypeStruct((batch_size, protos, part), BF16),
        ],
        compiler_params=params(),
        cost_estimate=cost(4 * rows * protos * width, 12 * MIB),
        name="proto_gradient",
    )(index, own_dscore.reshape(rows, protos), other_dscore.reshape(rows, protos), unit, unit)


def embed_gradient_kernel(index_ref, embeddings_ref, own_ref, received_ref, out_ref):
    del index_ref
    gunit = own_ref[...] + received_ref[...].astype(F32)
    hidden = embeddings_ref[...].astype(F32)
    inverse = 1.0 / jnp.sqrt(jnp.sum(hidden * hidden, axis=1, keepdims=True) + NORM_EPSILON)
    along = jnp.sum(hidden * gunit, axis=1, keepdims=True)
    out_ref[...] = inverse * gunit - hidden * (inverse * inverse * inverse * along)


def embed_gradient(index, embeddings, own, received):
    share, width = own.shape
    whole = pl.BlockSpec((share, width), lambda i, index: (0, 0))
    return pl.pallas_call(
        embed_gradient_kernel,
        grid_spec=pltpu.PrefetchScalarGridSpec(
            num_scalar_prefetch=1,
            grid=(1,),
            in_specs=[pl.BlockSpec((share, width), lambda i, index: (index[0], 0)), whole, whole],
            out_specs=whole,
        ),
        out_shape=jax.ShapeDtypeStruct((share, width), F32),
        compiler_params=params(),
        cost_estimate=cost(8 * share * width, 4 * MIB),
        name="embed_gradient",
    )(index, embeddings, own, received)


def swap(value, axis, distance):
    size = lax.axis_size(axis)
    return lax.ppermute(value, axis, [(i, i ^ distance) for i in range(size)])


def parts_of(value, axis):
    size = lax.axis_size(axis)
    if size > 8:
        return [lax.psum(value, axis)]
    return [value] + [swap(value, axis, distance) for distance in range(1, size)]


def scalar(value):
    return jnp.full((1,), value, jnp.int32)


def on_device(embeddings, prototypes, partners):
    row_count, width = embeddings.shape
    proto_count = prototypes.shape[0]
    batch_size = lax.axis_size("batch")
    proto_size = lax.axis_size("proto")
    total_rows = row_count * batch_size
    centroids = proto_count * proto_size
    share = row_count // proto_size
    places = proto_size // 2
    batch_index = lax.axis_index("batch")
    proto_index = lax.axis_index("proto")
    core = proto_index % 2
    place = proto_index // 2

    piece = OFFLOADED // proto_size
    own = own_rows(embeddings, scalar(proto_index), piece, 1)
    gathered = lax.all_gather(own, ("batch", "proto"), axis=0, tiled=True)
    rest = row_count - OFFLOADED
    half = rest // 2
    own = own_rows(embeddings, scalar(OFFLOADED // OWN_BLOCK), OWN_BLOCK, rest // OWN_BLOCK)
    own_half = lax.dynamic_slice_in_dim(own, core * half, half, 0)
    arrived_rows = [swap(own_half, "batch", distance) for distance in range(1, batch_size)]

    unit, wnorm, scores, expo, zsum, columns = scores_of(embeddings, prototypes, share)
    columns = parts_of(columns, "batch")
    for iteration in range(ITERS - 1):
        row_totals = parts_of(row_pass(columns, expo, centroids), "proto")
        columns = parts_of(column_pass(row_totals, expo, total_rows), "batch")
        if iteration == 0:
            columns, arrived_rows = lax.optimization_barrier((columns, arrived_rows))
            other_rows = [swap(rows, "proto", 1) for rows in arrived_rows]

    pieces = [
        (gathered, OFFLOADED, [jnp.int32(i * row_count) for i in range(batch_size)]),
        (own, rest, [batch_index * row_count + OFFLOADED]),
    ]
    for distance in range(1, batch_size):
        start = (batch_index ^ distance) * row_count + OFFLOADED
        pieces.append((arrived_rows[distance - 1], half, [start + core * half]))
        pieces.append((other_rows[distance - 1], half, [start + (1 - core) * half]))
    first, second = partner_pass(partners[:, 0], partners[:, 1], pieces, wnorm, total_rows)
    row_totals = parts_of(partner_row_pass(columns, zsum, first, second, centroids), "proto")
    shared = (columns, row_totals, first, second, scores, wnorm, centroids, total_rows, proto_size)
    other_gunit, other_dscore, other_loss = gradients(scalar(1 - core), *shared, BF16)
    received = swap(other_gunit, "proto", 1)
    kept, own_dscore, own_loss = gradients(scalar(core), *shared, F32)

    bit = 0
    while (2 << bit) <= places:
        kept, sent = combine(scalar((place >> bit) % 2), kept, received)
        if bit == 0:
            sent, own_dscore, other_dscore = lax.optimization_barrier((sent, own_dscore, other_dscore))
            received = swap(sent, "proto", 2)
            grad_proto, proto_sent = proto_gradient(
                jnp.stack([batch_index, core]).astype(jnp.int32), own_dscore, other_dscore, unit, batch_size
            )
            kept, grad_proto, proto_sent = lax.optimization_barrier((kept, grad_proto, proto_sent))
        else:
            received = swap(sent, "proto", 2 << bit)
        bit += 1
    grad_embed = embed_gradient(scalar(proto_index), embeddings, kept[0], received[0])

    loss, proto_sent = lax.optimization_barrier((own_loss + other_loss, proto_sent))
    for axis in ("batch", "proto"):
        loss = functools.reduce(jnp.add, parts_of(loss, axis))
    loss = loss[0, 0] / total_rows

    for distance in range(batch_size - 1, 0, -1):
        grad_proto = grad_proto + swap(proto_sent[distance], "batch", distance).astype(F32)

    return (loss, grad_proto, grad_embed)


def solution(mesh):
    return jax.shard_map(
        on_device,
        mesh=mesh,
        in_specs=(P("batch", None), P("proto", None), P("batch", None)),
        out_specs=(P(), P("proto", "batch"), P(("batch", "proto"), None)),
        check_vma=False,
    )
```

```python
import functools

import jax
import jax.numpy as jnp
from jax import lax
from jax.experimental import pallas as pl
from jax.experimental.pallas import tpu as pltpu
from jax.sharding import PartitionSpec as P

ITERS = 3
BALANCE_SMOOTHING = 0.05
SOFTMAX_HEAT = 0.1
NORM_EPSILON = 1e-06
LANES = 128
CHUNK = 256
STREAMS = 4
OWN_BLOCK = 256
MIB = 1 << 20
F32 = jnp.float32
BF16 = jnp.bfloat16


def params(mib=60):
    return pltpu.CompilerParams(vmem_limit_bytes=mib * MIB)


def cost(flops, moved, exps=0):
    return pl.CostEstimate(flops=flops, bytes_accessed=moved, transcendentals=exps)


def normalized(block):
    wide = block.astype(F32)
    inverse = 1.0 / jnp.sqrt(jnp.sum(wide * wide, axis=1, keepdims=True) + NORM_EPSILON)
    return wide * inverse


def lane_row_sums(values):
    columns = values.shape[1]
    part = values[:, 0:LANES]
    for start in range(LANES, columns, LANES):
        part = part + values[:, start : start + LANES]
    return jnp.sum(part.T, axis=0, keepdims=True)


def split_rows(row):
    high = row.astype(BF16).astype(F32)
    middle = (row - high).astype(BF16).astype(F32)
    low = row - high - middle
    place = lax.broadcasted_iota(jnp.int32, (16, row.shape[1]), 0)
    stacked = jnp.where(place == 0, high, jnp.where(place == 1, middle, jnp.where(place == 2, low, 0.0)))
    return stacked.astype(BF16)


def total_of(refs):
    total = refs[0][...]
    for ref in refs[1:]:
        total = total + ref[...]
    return total


def own_rows_kernel(index_ref, embeddings_ref, table_ref, stage_ref):
    del index_ref
    rows, columns = embeddings_ref.shape
    unit = normalized(embeddings_ref[...]).astype(BF16).astype(F32)
    groups = columns // LANES
    for k in range(groups):
        stage_ref[pl.ds(k, rows, stride=groups), :] = unit[:, k * LANES : (k + 1) * LANES]
    table_ref[...] = stage_ref[...].reshape(rows, groups, LANES).astype(BF16)


def own_rows(embeddings, index, block, count):
    columns = embeddings.shape[1]
    groups = columns // LANES
    return pl.pallas_call(
        own_rows_kernel,
        grid_spec=pltpu.PrefetchScalarGridSpec(
            num_scalar_prefetch=1,
            grid=(count,),
            in_specs=[pl.BlockSpec((block, columns), lambda i, index: (index[0] + i, 0))],
            out_specs=pl.BlockSpec((block, groups, LANES), lambda i, index: (i, 0, 0)),
            scratch_shapes=[pltpu.VMEM((block * groups, LANES), F32)],
        ),
        out_shape=jax.ShapeDtypeStruct((block * count, groups, LANES), BF16),
        compiler_params=params(),
        name="own_rows",
    )(index, embeddings)


def scores_kernel(embeddings_ref, prototypes_ref, unit_ref, wnorm_ref, scores_ref, expo_ref, zsum_ref, column_ref):
    step = pl.program_id(0)

    @pl.when(step == 0)
    def _():
        wnorm_ref[...] = normalized(prototypes_ref[...]).astype(BF16)

    unit = normalized(embeddings_ref[...]).astype(BF16)
    unit_ref[...] = unit
    scores = lax.dot_general(unit, wnorm_ref[...], (((1,), (1,)), ((), ())), preferred_element_type=F32)
    scores_ref[...] = scores
    soft = jnp.exp(scores * (1.0 / SOFTMAX_HEAT))
    zsum_ref[...] = lane_row_sums(soft)
    expo = soft * soft
    expo_ref[...] = expo.astype(BF16)
    sums = jnp.sum(expo, axis=0, keepdims=True)

    @pl.when(step == 0)
    def _():
        column_ref[...] = sums

    @pl.when(step > 0)
    def _():
        column_ref[...] += sums


def scores_of(embeddings, prototypes, share):
    rows, columns = embeddings.shape
    protos = prototypes.shape[0]
    return pl.pallas_call(
        scores_kernel,
        grid=(rows // share,),
        in_specs=[
            pl.BlockSpec((share, columns), lambda i: (i, 0)),
            pl.BlockSpec((protos, columns), lambda i: (0, 0), pipeline_mode=pl.Buffered(1)),
        ],
        out_specs=[
            pl.BlockSpec((share, columns), lambda i: (i, 0)),
            pl.BlockSpec((protos, columns), lambda i: (0, 0)),
            pl.BlockSpec((share, protos), lambda i: (i, 0)),
            pl.BlockSpec((share, protos), lambda i: (i, 0)),
            pl.BlockSpec((None, None, 1, share), lambda i: (i % 2, i // 2, 0, 0)),
            pl.BlockSpec((1, protos), lambda i: (0, 0)),
        ],
        out_shape=[
            jax.ShapeDtypeStruct((rows, columns), BF16),
            jax.ShapeDtypeStruct((protos, columns), BF16),
            jax.ShapeDtypeStruct((rows, protos), F32),
            jax.ShapeDtypeStruct((rows, protos), BF16),
            jax.ShapeDtypeStruct((2, rows // share // 2, 1, share), F32),
            jax.ShapeDtypeStruct((1, protos), F32),
        ],
        compiler_params=params(),
        cost_estimate=cost(2 * rows * columns * protos, 22 * MIB, rows * protos),
        name="scores",
    )(embeddings, prototypes)


def row_kernel(count, parts, *refs):
    column_refs, expo_refs, row_ref = refs[:parts], refs[parts:-1], refs[-1]
    scale = split_rows(1.0 / (count * total_of(column_refs)))
    block = expo_refs[0].shape[0]
    for k, expo_ref in enumerate(expo_refs):
        sums = lax.dot_general(scale, expo_ref[...], (((1,), (1,)), ((), ())), preferred_element_type=F32)
        row_ref[:, k * block : (k + 1) * block] = jnp.sum(sums, axis=0, keepdims=True)


def streams_of(shape):
    return [pl.BlockSpec(shape, functools.partial(lambda k, i: (STREAMS * i + k, 0), k)) for k in range(STREAMS)]


def row_pass(columns, expo, count):
    rows, protos = expo.shape
    block = rows // 8
    return pl.pallas_call(
        functools.partial(row_kernel, count, len(columns)),
        grid=(rows // block // STREAMS,),
        in_specs=[pl.BlockSpec((1, protos), lambda i: (0, 0)) for _ in columns] + streams_of((block, protos)),
        out_specs=pl.BlockSpec((1, STREAMS * block), lambda i: (0, i)),
        out_shape=jax.ShapeDtypeStruct((1, rows), F32),
        compiler_params=params(),
        cost_estimate=cost(2 * rows * protos, 4 * MIB),
        name="row_pass",
    )(*columns, *[expo] * STREAMS)


def column_kernel(count, parts, *refs):
    row_refs, expo_refs, column_ref = refs[:parts], refs[parts:-1], refs[-1]
    step = pl.program_id(0)
    scale = split_rows(1.0 / (count * total_of(row_refs)))
    block = expo_refs[0].shape[0]
    total = None
    for k, expo_ref in enumerate(expo_refs):
        sums = lax.dot_general(
            scale[:, k * block : (k + 1) * block], expo_ref[...], (((1,), (0,)), ((), ())), preferred_element_type=F32
        )
        total = sums if total is None else total + sums
    total = jnp.sum(total, axis=0, keepdims=True)

    @pl.when(step == 0)
    def _():
        column_ref[...] = total

    @pl.when(step > 0)
    def _():
        column_ref[...] += total


def column_pass(row_totals, expo, count):
    rows, protos = expo.shape
    block = rows // 8
    return pl.pallas_call(
        functools.partial(column_kernel, count, len(row_totals)),
        grid=(rows // block // STREAMS,),
        in_specs=[pl.BlockSpec((1, STREAMS * block), lambda i: (0, i)) for _ in row_totals]
        + streams_of((block, protos)),
        out_specs=pl.BlockSpec((1, protos), lambda i: (0, 0)),
        out_shape=jax.ShapeDtypeStruct((1, protos), F32),
        compiler_params=params(),
        cost_estimate=cost(2 * rows * protos, 4 * MIB),
        name="column_pass",
    )(*row_totals, *[expo] * STREAMS)


def partner_kernel(first_ref, second_ref, source_ref, wnorm_ref, first_expo_ref, second_expo_ref, table_ref, semaphores, *stages):
    step = pl.program_id(0)
    groups = table_ref.shape[1]

    @pl.when(step == 0)
    def _():
        parts = semaphores.shape[0]
        size = source_ref.shape[0] // parts
        copies = [
            pltpu.make_async_copy(
                source_ref.at[pl.ds(k * size, size)], table_ref.at[pl.ds(k * size, size)], semaphores.at[k]
            )
            for k in range(parts)
        ]
        for copy in copies:
            copy.start()
        for copy in copies:
            copy.wait()

    rows = first_expo_ref.shape[0]
    wnorm = wnorm_ref[...]
    chunks = [
        (which_ref, out_ref, start)
        for start in range(0, rows, CHUNK)
        for which_ref, out_ref in ((first_ref, first_expo_ref), (second_ref, second_expo_ref))
    ]
    for (which_ref, out_ref, start), stage_ref in zip(chunks, stages):
        for row in range(CHUNK):
            place = which_ref[step * rows + start + row]
            stage_ref[row * groups : (row + 1) * groups, :] = table_ref[place].astype(F32)
        unit = jnp.concatenate(
            [stage_ref[pl.ds(k, CHUNK, stride=groups), :].astype(BF16) for k in range(groups)], axis=1
        )
        scores = lax.dot_general(unit, wnorm, (((1,), (1,)), ((), ())), preferred_element_type=F32)
        soft = jnp.exp(scores * (1.0 / SOFTMAX_HEAT))
        out_ref[start : start + CHUNK, :] = (soft * soft).astype(out_ref.dtype)


def partner_pass(first, second, table, wnorm):
    rows = first.shape[0]
    protos, columns = wnorm.shape
    groups = columns // LANES
    block = 2 * CHUNK
    return pl.pallas_call(
        partner_kernel,
        grid_spec=pltpu.PrefetchScalarGridSpec(
            num_scalar_prefetch=2,
            grid=(rows // block,),
            in_specs=[
                pl.BlockSpec(memory_space=pl.ANY),
                pl.BlockSpec((protos, columns), lambda i, *_: (0, 0), pipeline_mode=pl.Buffered(1)),
            ],
            out_specs=[
                pl.BlockSpec((block, protos), lambda i, *_: (i, 0)),
                pl.BlockSpec((block, protos), lambda i, *_: (i, 0)),
            ],
            scratch_shapes=[
                pltpu.VMEM(table.shape, BF16),
                pltpu.SemaphoreType.DMA((STREAMS,)),
            ]
            + [pltpu.VMEM((CHUNK * groups, LANES), F32)] * 4,
        ),
        out_shape=[jax.ShapeDtypeStruct((rows, protos), BF16)] * 2,
        compiler_params=params(),
        cost_estimate=cost(4 * rows * columns * protos, 28 * MIB, 2 * rows * protos),
        name="partner_scores",
    )(first, second, table, wnorm)


def partner_row_kernel(count, parts, *refs):
    column_refs, zsum_ref, row_ref = refs[:parts], refs[parts], refs[-1]
    first_refs, second_refs = refs[parts + 1 : parts + 1 + STREAMS], refs[parts + 1 + STREAMS : -1]
    scale = 1.0 / (count * total_of(column_refs))
    for k in range(STREAMS):
        at = (k % 2, k // 2)
        row_ref[at] = jnp.concatenate(
            [
                lane_row_sums(first_refs[k][...].astype(F32) * scale),
                lane_row_sums(second_refs[k][...].astype(F32) * scale),
                zsum_ref[at],
            ],
            axis=0,
        )


def partner_row_pass(columns, zsum, first, second, count):
    rows, protos = first.shape
    share = zsum.shape[-1]
    group = STREAMS // 2
    return pl.pallas_call(
        functools.partial(partner_row_kernel, count, len(columns)),
        grid=(rows // share // STREAMS,),
        in_specs=[pl.BlockSpec((1, protos), lambda i: (0, 0)) for _ in columns]
        + [pl.BlockSpec((2, group, 1, share), lambda i: (0, i, 0, 0))]
        + streams_of((share, protos)) * 2,
        out_specs=pl.BlockSpec((2, group, 3, share), lambda i: (0, i, 0, 0)),
        out_shape=jax.ShapeDtypeStruct((2, rows // share // 2, 3, share), F32),
        compiler_params=params(),
        cost_estimate=cost(4 * rows * protos, 8 * MIB),
        name="partner_row_pass",
    )(*columns, zsum, *[first] * STREAMS, *[second] * STREAMS)


def gradient_kernel(count, total, heat_scale, proto_size, parts, core_ref, *refs):
    del core_ref
    column_refs, row_refs = refs[: parts[0]], refs[parts[0] : parts[0] + parts[1]]
    first_ref, second_ref, scores_ref, wnorm_ref, gunit_ref, dscore_ref, loss_ref = refs[parts[0] + parts[1] :]
    step = pl.program_id(0)
    scale = 1.0 / (count * total_of(column_refs))
    totals = total_of(row_refs)
    share = totals.shape[-1]
    place = lax.broadcasted_iota(jnp.int32, (8, share), 0)
    loss = jnp.zeros((), F32)
    for group in range(totals.shape[0]):
        row_totals, zsum = totals[group, 0:2], totals[group, 2:3]
        weights = total * (1.0 / (total * row_totals))
        code_totals = 0.5 * jnp.sum(weights * row_totals, axis=0, keepdims=True)
        log_part = jnp.sum(code_totals * jnp.log(zsum)) * (1.0 / proto_size)
        stacked = jnp.where(
            place == 0,
            weights[0:1],
            jnp.where(place == 1, weights[1:2], jnp.where(place == 2, code_totals / zsum, 0.0)),
        ).T
        first = (stacked[:, 0:1] * first_ref[group].astype(F32) * scale).astype(BF16).astype(F32)
        second = (stacked[:, 1:2] * second_ref[group].astype(F32) * scale).astype(BF16).astype(F32)
        targets = 0.5 * (first + second)
        heated = scores_ref[group] * (1.0 / SOFTMAX_HEAT)
        loss = loss + (log_part - jnp.sum(targets * heated))
        dscore = ((jnp.exp(heated) * stacked[:, 2:3] - targets) * heat_scale).astype(BF16)
        dscore_ref[group] = dscore
        gunit = jnp.dot(dscore, wnorm_ref[...], preferred_element_type=F32)
        gunit_ref[group] = gunit.astype(gunit_ref.dtype)

    @pl.when(step == 0)
    def _():
        loss_ref[...] = jnp.full(loss_ref.shape, loss, F32)

    @pl.when(step > 0)
    def _():
        loss_ref[...] += loss


def gradients(core, columns, row_totals, first, second, scores, wnorm, count, total, proto_size, dtype):
    rows, protos = first.shape
    width = wnorm.shape[1]
    heat_scale = count / (32.0 * SOFTMAX_HEAT)
    _, places, _, share = row_totals[0].shape
    group = 2
    by_core = pl.BlockSpec((group, None, share, protos), lambda i, core: (i, core[0], 0, 0))
    first, second, scores = [value.reshape(places, 2, share, protos) for value in (first, second, scores)]
    return pl.pallas_call(
        functools.partial(
            gradient_kernel, count, total, heat_scale, proto_size, (len(columns), len(row_totals))
        ),
        grid_spec=pltpu.PrefetchScalarGridSpec(
            num_scalar_prefetch=1,
            grid=(places // group,),
            in_specs=[pl.BlockSpec((1, protos), lambda i, core: (0, 0)) for _ in columns]
            + [pl.BlockSpec((None, group, 3, share), lambda i, core: (core[0], i, 0, 0)) for _ in row_totals]
            + [
                by_core,
                by_core,
                by_core,
                pl.BlockSpec((protos, width), lambda i, core: (0, 0), pipeline_mode=pl.Buffered(1)),
            ],
            out_specs=[
                pl.BlockSpec((group, share, width), lambda i, core: (i, 0, 0)),
                pl.BlockSpec((group, share, protos), lambda i, core: (i, 0, 0)),
                pl.BlockSpec((1, LANES), lambda i, core: (0, 0)),
            ],
        ),
        out_shape=[
            jax.ShapeDtypeStruct((places, share, width), dtype),
            jax.ShapeDtypeStruct((places, share, protos), BF16),
            jax.ShapeDtypeStruct((1, LANES), F32),
        ],
        compiler_params=params(),
        cost_estimate=cost(rows * width * protos, 16 * MIB, rows * protos // 2),
        name="gradients",
    )(core, *columns, *row_totals, first, second, scores, wnorm)


def combine_kernel(bit_ref, own_kept_ref, own_received_ref, other_kept_ref, other_received_ref, own_ref, sent_ref):
    del bit_ref
    sent_ref[...] = (other_kept_ref[...] + other_received_ref[...].astype(F32)).astype(BF16)
    own_ref[...] = own_kept_ref[...] + own_received_ref[...].astype(F32)


def combine(bit, kept, received):
    count, share, width = kept.shape
    kept, received = [value.reshape(count // 2, 2, share, width) for value in (kept, received)]
    own_at = pl.BlockSpec((None, None, share, width), lambda i, bit: (i, bit[0], 0, 0))
    other_at = pl.BlockSpec((None, None, share, width), lambda i, bit: (i, 1 - bit[0], 0, 0))
    out_at = pl.BlockSpec((None, share, width), lambda i, bit: (i, 0, 0))
    return pl.pallas_call(
        combine_kernel,
        grid_spec=pltpu.PrefetchScalarGridSpec(
            num_scalar_prefetch=1,
            grid=(count // 2,),
            in_specs=[own_at, own_at, other_at, other_at],
            out_specs=[out_at, out_at],
        ),
        out_shape=[
            jax.ShapeDtypeStruct((count // 2, share, width), F32),
            jax.ShapeDtypeStruct((count // 2, share, width), BF16),
        ],
        compiler_params=params(),
        cost_estimate=cost(count * share * width, 9 * count * share * width),
        name="combine",
    )(bit, kept, received, kept, received)


def proto_gradient_kernel(index_ref, own_dscore_ref, other_dscore_ref, own_unit_ref, other_unit_ref, own_ref, sent_ref):
    del index_ref
    rows = own_dscore_ref.shape[0]
    part = own_unit_ref.shape[-1]
    both = (((0,), (0,)), ((), ()))
    total = lax.dot_general(
        own_dscore_ref[...], own_unit_ref[...].reshape(rows, part), both, preferred_element_type=F32
    ) + lax.dot_general(
        other_dscore_ref[...], other_unit_ref[...].reshape(rows, part), both, preferred_element_type=F32
    )
    sent_ref[...] = total.astype(BF16)
    own_ref[...] = total


def proto_gradient(index, own_dscore, other_dscore, unit, batch_size):
    places, share, protos = own_dscore.shape
    width = unit.shape[1]
    part = width // batch_size
    rows = places * share
    last = batch_size - 1
    unit = unit.reshape(places, 2, share, width)
    dscore_at = pl.BlockSpec((rows, protos), lambda i, index: (0, 0), pipeline_mode=pl.Buffered(1))
    return pl.pallas_call(
        proto_gradient_kernel,
        grid_spec=pltpu.PrefetchScalarGridSpec(
            num_scalar_prefetch=1,
            grid=(batch_size,),
            in_specs=[
                dscore_at,
                dscore_at,
                pl.BlockSpec((places, None, share, part), lambda i, index: (0, index[1], 0, index[0] ^ (last - i))),
                pl.BlockSpec((places, None, share, part), lambda i, index: (0, 1 - index[1], 0, index[0] ^ (last - i))),
            ],
            out_specs=[
                pl.BlockSpec((protos, part), lambda i, index: (0, 0)),
                pl.BlockSpec((None, protos, part), lambda i, index: (last - i, 0, 0)),
            ],
        ),
        out_shape=[
            jax.ShapeDtypeStruct((protos, part), F32),
            jax.ShapeDtypeStruct((batch_size, protos, part), BF16),
        ],
        compiler_params=params(),
        cost_estimate=cost(4 * rows * protos * width, 12 * MIB),
        name="proto_gradient",
    )(index, own_dscore.reshape(rows, protos), other_dscore.reshape(rows, protos), unit, unit)


def embed_gradient_kernel(index_ref, embeddings_ref, own_ref, received_ref, out_ref):
    del index_ref
    gunit = own_ref[...] + received_ref[...].astype(F32)
    hidden = embeddings_ref[...].astype(F32)
    inverse = 1.0 / jnp.sqrt(jnp.sum(hidden * hidden, axis=1, keepdims=True) + NORM_EPSILON)
    along = jnp.sum(hidden * gunit, axis=1, keepdims=True)
    out_ref[...] = inverse * gunit - hidden * (inverse * inverse * inverse * along)


def embed_gradient(index, embeddings, own, received):
    share, width = own.shape
    whole = pl.BlockSpec((share, width), lambda i, index: (0, 0))
    return pl.pallas_call(
        embed_gradient_kernel,
        grid_spec=pltpu.PrefetchScalarGridSpec(
            num_scalar_prefetch=1,
            grid=(1,),
            in_specs=[pl.BlockSpec((share, width), lambda i, index: (index[0], 0)), whole, whole],
            out_specs=whole,
        ),
        out_shape=jax.ShapeDtypeStruct((share, width), F32),
        compiler_params=params(),
        cost_estimate=cost(8 * share * width, 4 * MIB),
        name="embed_gradient",
    )(index, embeddings, own, received)


def swap(value, axis, distance):
    size = lax.axis_size(axis)
    return lax.ppermute(value, axis, [(i, i ^ distance) for i in range(size)])


def parts_of(value, axis):
    size = lax.axis_size(axis)
    if size > 4:
        return [lax.psum(value, axis)]
    return [value] + [swap(value, axis, distance) for distance in range(1, size)]


def proto_parts_of(value):
    return parts_of(value + swap(value, "core", 1), "place")


def scalar(value):
    return jnp.full((1,), value, jnp.int32)


def on_device(embeddings, prototypes, partners):
    row_count, width = embeddings.shape
    proto_count = prototypes.shape[0]
    batch_size = lax.axis_size("batch")
    places = lax.axis_size("place")
    proto_size = 2 * places
    total_rows = row_count * batch_size
    centroids = proto_count * proto_size
    share = row_count // proto_size
    batch_index = lax.axis_index("batch")
    place = lax.axis_index("place")
    core = lax.axis_index("core")
    proto_index = 2 * place + core

    half = row_count // 2
    own = own_rows(embeddings, scalar(core * (half // OWN_BLOCK)), OWN_BLOCK, half // OWN_BLOCK)
    table = lax.all_gather(own, ("batch", "core"), axis=0, tiled=True)

    unit, wnorm, scores, expo, zsum, columns = scores_of(embeddings, prototypes, share)
    columns = parts_of(columns, "batch")
    for iteration in range(ITERS - 1):
        row_totals = proto_parts_of(row_pass(columns, expo, centroids))
        columns = parts_of(column_pass(row_totals, expo, total_rows), "batch")

    first, second = partner_pass(partners[:, 0], partners[:, 1], table, wnorm)
    row_totals = proto_parts_of(partner_row_pass(columns, zsum, first, second, centroids))
    shared = (columns, row_totals, first, second, scores, wnorm, centroids, total_rows, proto_size)
    other_gunit, other_dscore, other_loss = gradients(scalar(1 - core), *shared, BF16)
    received = swap(other_gunit, "core", 1)
    kept, own_dscore, own_loss = gradients(scalar(core), *shared, F32)
    loss = functools.reduce(jnp.add, parts_of(own_loss + other_loss, "batch"))

    bit = 0
    while (1 << bit) < places:
        kept, sent = combine(scalar((place >> bit) % 2), kept, received)
        if bit == 0:
            sent, own_dscore, other_dscore, loss = lax.optimization_barrier((sent, own_dscore, other_dscore, loss))
            received = swap(sent, "place", 1)
            grad_proto, proto_sent = proto_gradient(
                jnp.stack([batch_index, core]).astype(jnp.int32), own_dscore, other_dscore, unit, batch_size
            )
            kept, grad_proto, proto_sent = lax.optimization_barrier((kept, grad_proto, proto_sent))
            loss = loss + swap(loss, "core", 1)
        else:
            sent, loss = lax.optimization_barrier((sent, loss))
            received = swap(sent, "place", 1 << bit)
        loss = loss + swap(loss, "place", 1 << bit)
        bit += 1
    grad_embed = embed_gradient(scalar(proto_index), embeddings, kept[0], received[0])
    loss = loss[0, 0] / total_rows

    for distance in range(batch_size - 1, 0, -1):
        grad_proto = grad_proto + swap(proto_sent[distance], "batch", distance).astype(F32)

    return (loss, grad_proto, grad_embed)


def solution(mesh):
    batch_size, proto_size = mesh.shape["batch"], mesh.shape["proto"]
    devices = mesh.devices.reshape(batch_size, proto_size // 2, 2)
    proto = ("place", "core")
    return jax.shard_map(
        on_device,
        mesh=jax.sharding.Mesh(devices, ("batch", "place", "core")),
        in_specs=(P("batch", None), P(proto, None), P("batch", None)),
        out_specs=(P(), P(proto, "batch"), P(("batch", "place", "core"), None)),
        check_vma=False,
    )
```

```python
import functools

import jax
import jax.numpy as jnp
from jax import lax
from jax.experimental import pallas as pl
from jax.experimental.pallas import tpu as pltpu
from jax.sharding import PartitionSpec as P

ITERS = 3
BALANCE_SMOOTHING = 0.05
SOFTMAX_HEAT = 0.1
NORM_EPSILON = 1e-06
LANES = 128
CHUNK = 256
STREAMS = 4
OWN_BLOCK = 256
MIB = 1 << 20
F32 = jnp.float32
BF16 = jnp.bfloat16


def params(mib=60):
    return pltpu.CompilerParams(vmem_limit_bytes=mib * MIB)


def in_vmem(value):
    return pltpu.with_memory_space_constraint(value, pltpu.VMEM)


def cost(flops, moved, exps=0):
    return pl.CostEstimate(flops=flops, bytes_accessed=moved, transcendentals=exps)


def normalized(block):
    wide = block.astype(F32)
    inverse = 1.0 / jnp.sqrt(jnp.sum(wide * wide, axis=1, keepdims=True) + NORM_EPSILON)
    return wide * inverse


def lane_row_sums(values):
    columns = values.shape[1]
    part = values[:, 0:LANES]
    for start in range(LANES, columns, LANES):
        part = part + values[:, start : start + LANES]
    return jnp.sum(part.T, axis=0, keepdims=True)


def split_rows(row):
    high = row.astype(BF16).astype(F32)
    middle = (row - high).astype(BF16).astype(F32)
    low = row - high - middle
    place = lax.broadcasted_iota(jnp.int32, (16, row.shape[1]), 0)
    stacked = jnp.where(place == 0, high, jnp.where(place == 1, middle, jnp.where(place == 2, low, 0.0)))
    return stacked.astype(BF16)


def total_of(refs):
    total = refs[0][...]
    for ref in refs[1:]:
        total = total + ref[...]
    return total


def own_rows_kernel(index_ref, embeddings_ref, table_ref, stage_ref):
    del index_ref
    rows, columns = embeddings_ref.shape
    unit = normalized(embeddings_ref[...]).astype(BF16).astype(F32)
    groups = columns // LANES
    for k in range(groups):
        stage_ref[pl.ds(k, rows, stride=groups), :] = unit[:, k * LANES : (k + 1) * LANES]
    table_ref[...] = stage_ref[...].reshape(rows, groups, LANES).astype(BF16)


def own_rows(embeddings, index, block, count):
    columns = embeddings.shape[1]
    groups = columns // LANES
    return pl.pallas_call(
        own_rows_kernel,
        grid_spec=pltpu.PrefetchScalarGridSpec(
            num_scalar_prefetch=1,
            grid=(count,),
            in_specs=[pl.BlockSpec((block, columns), lambda i, index: (index[0] + i, 0))],
            out_specs=pl.BlockSpec((block, groups, LANES), lambda i, index: (i, 0, 0)),
            scratch_shapes=[pltpu.VMEM((block * groups, LANES), F32)],
        ),
        out_shape=jax.ShapeDtypeStruct((block * count, groups, LANES), BF16),
        compiler_params=params(),
        name="own_rows",
    )(index, embeddings)


def scores_kernel(embeddings_ref, prototypes_ref, unit_ref, wnorm_ref, scores_ref, expo_ref, zsum_ref, column_ref):
    step = pl.program_id(0)

    @pl.when(step == 0)
    def _():
        wnorm_ref[...] = normalized(prototypes_ref[...]).astype(BF16)

    share = zsum_ref.shape[-1]
    sums = None
    for k in range(2):
        at = slice(k * share, (k + 1) * share)
        unit = normalized(embeddings_ref[at]).astype(BF16)
        unit_ref[at] = unit
        scores = lax.dot_general(unit, wnorm_ref[...], (((1,), (1,)), ((), ())), preferred_element_type=F32)
        scores_ref[at] = scores
        soft = jnp.exp(scores * (1.0 / SOFTMAX_HEAT))
        zsum_ref[k, 0] = lane_row_sums(soft)
        expo = soft * soft
        expo_ref[at] = expo.astype(BF16)
        part = jnp.sum(expo, axis=0, keepdims=True)
        sums = part if sums is None else sums + part

    @pl.when(step == 0)
    def _():
        column_ref[...] = sums

    @pl.when(step > 0)
    def _():
        column_ref[...] += sums


def scores_of(embeddings, prototypes, share):
    rows, columns = embeddings.shape
    protos = prototypes.shape[0]
    return pl.pallas_call(
        scores_kernel,
        grid=(rows // share // 2,),
        in_specs=[
            pl.BlockSpec((2 * share, columns), lambda i: (i, 0)),
            pl.BlockSpec((protos, columns), lambda i: (0, 0), pipeline_mode=pl.Buffered(1)),
        ],
        out_specs=[
            pl.BlockSpec((2 * share, columns), lambda i: (i, 0)),
            pl.BlockSpec((protos, columns), lambda i: (0, 0)),
            pl.BlockSpec((2 * share, protos), lambda i: (i, 0)),
            pl.BlockSpec((2 * share, protos), lambda i: (i, 0)),
            pl.BlockSpec((2, 1, 1, share), lambda i: (0, i, 0, 0)),
            pl.BlockSpec((1, protos), lambda i: (0, 0)),
        ],
        out_shape=[
            jax.ShapeDtypeStruct((rows, columns), BF16),
            jax.ShapeDtypeStruct((protos, columns), BF16),
            jax.ShapeDtypeStruct((rows, protos), F32),
            jax.ShapeDtypeStruct((rows, protos), BF16),
            jax.ShapeDtypeStruct((2, rows // share // 2, 1, share), F32),
            jax.ShapeDtypeStruct((1, protos), F32),
        ],
        compiler_params=params(32),
        cost_estimate=cost(2 * rows * columns * protos, 22 * MIB, rows * protos),
        name="scores",
    )(embeddings, prototypes)


def row_kernel(count, parts, *refs):
    column_refs, expo_refs, row_ref = refs[:parts], refs[parts:-1], refs[-1]
    scale = split_rows(1.0 / (count * total_of(column_refs)))
    block = expo_refs[0].shape[0]
    for k, expo_ref in enumerate(expo_refs):
        sums = lax.dot_general(scale, expo_ref[...], (((1,), (1,)), ((), ())), preferred_element_type=F32)
        row_ref[:, k * block : (k + 1) * block] = jnp.sum(sums, axis=0, keepdims=True)


def streams_of(shape):
    return [pl.BlockSpec(shape, functools.partial(lambda k, i: (STREAMS * i + k, 0), k)) for k in range(STREAMS)]


def row_pass(columns, expo, count):
    rows, protos = expo.shape
    block = rows // 8
    return pl.pallas_call(
        functools.partial(row_kernel, count, len(columns)),
        grid=(rows // block // STREAMS,),
        in_specs=[pl.BlockSpec((1, protos), lambda i: (0, 0)) for _ in columns] + streams_of((block, protos)),
        out_specs=pl.BlockSpec((1, STREAMS * block), lambda i: (0, i)),
        out_shape=jax.ShapeDtypeStruct((1, rows), F32),
        compiler_params=params(16),
        cost_estimate=cost(2 * rows * protos, 4 * MIB),
        name="row_pass",
    )(*columns, *[in_vmem(expo)] * STREAMS)


def column_kernel(count, parts, *refs):
    row_refs, expo_refs, column_ref = refs[:parts], refs[parts:-1], refs[-1]
    step = pl.program_id(0)
    scale = split_rows(1.0 / (count * total_of(row_refs)))
    block = expo_refs[0].shape[0]
    total = None
    for k, expo_ref in enumerate(expo_refs):
        sums = lax.dot_general(
            scale[:, k * block : (k + 1) * block], expo_ref[...], (((1,), (0,)), ((), ())), preferred_element_type=F32
        )
        total = sums if total is None else total + sums
    total = jnp.sum(total, axis=0, keepdims=True)

    @pl.when(step == 0)
    def _():
        column_ref[...] = total

    @pl.when(step > 0)
    def _():
        column_ref[...] += total


def column_pass(row_totals, expo, count):
    rows, protos = expo.shape
    block = rows // 8
    return pl.pallas_call(
        functools.partial(column_kernel, count, len(row_totals)),
        grid=(rows // block // STREAMS,),
        in_specs=[pl.BlockSpec((1, STREAMS * block), lambda i: (0, i)) for _ in row_totals]
        + streams_of((block, protos)),
        out_specs=pl.BlockSpec((1, protos), lambda i: (0, 0)),
        out_shape=jax.ShapeDtypeStruct((1, protos), F32),
        compiler_params=params(16),
        cost_estimate=cost(2 * rows * protos, 4 * MIB),
        name="column_pass",
    )(*row_totals, *[in_vmem(expo)] * STREAMS)


def partner_kernel(first_ref, second_ref, source_ref, wnorm_ref, first_expo_ref, second_expo_ref, table_ref, semaphores, *stages):
    step = pl.program_id(0)
    groups = table_ref.shape[1]

    @pl.when(step == 0)
    def _():
        parts = semaphores.shape[0]
        size = source_ref.shape[0] // parts
        copies = [
            pltpu.make_async_copy(
                source_ref.at[pl.ds(k * size, size)], table_ref.at[pl.ds(k * size, size)], semaphores.at[k]
            )
            for k in range(parts)
        ]
        for copy in copies:
            copy.start()
        for copy in copies:
            copy.wait()

    rows = first_expo_ref.shape[0]
    wnorm = wnorm_ref[...]
    chunks = [
        (which_ref, out_ref, start)
        for start in range(0, rows, CHUNK)
        for which_ref, out_ref in ((first_ref, first_expo_ref), (second_ref, second_expo_ref))
    ]
    for (which_ref, out_ref, start), stage_ref in zip(chunks, stages):
        for row in range(CHUNK):
            place = which_ref[step * rows + start + row]
            stage_ref[row * groups : (row + 1) * groups, :] = table_ref[place].astype(F32)
        unit = jnp.concatenate(
            [stage_ref[pl.ds(k, CHUNK, stride=groups), :].astype(BF16) for k in range(groups)], axis=1
        )
        scores = lax.dot_general(unit, wnorm, (((1,), (1,)), ((), ())), preferred_element_type=F32)
        soft = jnp.exp(scores * (1.0 / SOFTMAX_HEAT))
        out_ref[start : start + CHUNK, :] = (soft * soft).astype(out_ref.dtype)


def partner_pass(first, second, table, wnorm):
    rows = first.shape[0]
    protos, columns = wnorm.shape
    groups = columns // LANES
    block = 2 * CHUNK
    return pl.pallas_call(
        partner_kernel,
        grid_spec=pltpu.PrefetchScalarGridSpec(
            num_scalar_prefetch=2,
            grid=(rows // block,),
            in_specs=[
                pl.BlockSpec(memory_space=pl.ANY),
                pl.BlockSpec((protos, columns), lambda i, *_: (0, 0), pipeline_mode=pl.Buffered(1)),
            ],
            out_specs=[
                pl.BlockSpec((block, protos), lambda i, *_: (i, 0)),
                pl.BlockSpec((block, protos), lambda i, *_: (i, 0)),
            ],
            scratch_shapes=[
                pltpu.VMEM(table.shape, BF16),
                pltpu.SemaphoreType.DMA((STREAMS,)),
            ]
            + [pltpu.VMEM((CHUNK * groups, LANES), F32)] * 4,
        ),
        out_shape=[jax.ShapeDtypeStruct((rows, protos), BF16)] * 2,
        compiler_params=params(32),
        cost_estimate=cost(4 * rows * columns * protos, 28 * MIB, 2 * rows * protos),
        name="partner_scores",
    )(first, second, table, wnorm)


def partner_row_kernel(count, parts, *refs):
    column_refs, zsum_ref, row_ref = refs[:parts], refs[parts], refs[-1]
    first_refs, second_refs = refs[parts + 1 : parts + 1 + STREAMS], refs[parts + 1 + STREAMS : -1]
    scale = 1.0 / (count * total_of(column_refs))
    for k in range(STREAMS):
        at = (k % 2, k // 2)
        row_ref[at] = jnp.concatenate(
            [
                lane_row_sums(first_refs[k][...].astype(F32) * scale),
                lane_row_sums(second_refs[k][...].astype(F32) * scale),
                zsum_ref[at],
            ],
            axis=0,
        )


def partner_row_pass(columns, zsum, first, second, count):
    rows, protos = first.shape
    share = zsum.shape[-1]
    group = STREAMS // 2
    return pl.pallas_call(
        functools.partial(partner_row_kernel, count, len(columns)),
        grid=(rows // share // STREAMS,),
        in_specs=[pl.BlockSpec((1, protos), lambda i: (0, 0)) for _ in columns]
        + [pl.BlockSpec((2, group, 1, share), lambda i: (0, i, 0, 0))]
        + streams_of((share, protos)) * 2,
        out_specs=pl.BlockSpec((2, group, 3, share), lambda i: (0, i, 0, 0)),
        out_shape=jax.ShapeDtypeStruct((2, rows // share // 2, 3, share), F32),
        compiler_params=params(16),
        cost_estimate=cost(4 * rows * protos, 8 * MIB),
        name="partner_row_pass",
    )(*columns, zsum, *[in_vmem(first)] * STREAMS, *[in_vmem(second)] * STREAMS)


def gradient_kernel(count, total, heat_scale, proto_size, parts, core_ref, *refs):
    del core_ref
    column_refs, row_refs = refs[: parts[0]], refs[parts[0] : parts[0] + parts[1]]
    first_ref, second_ref, scores_ref, wnorm_ref, gunit_ref, dscore_ref, loss_ref = refs[parts[0] + parts[1] :]
    step = pl.program_id(0)
    scale = 1.0 / (count * total_of(column_refs))
    totals = total_of(row_refs)
    share = totals.shape[-1]
    place = lax.broadcasted_iota(jnp.int32, (8, share), 0)
    loss = jnp.zeros((), F32)
    for group in range(totals.shape[0]):
        row_totals, zsum = totals[group, 0:2], totals[group, 2:3]
        weights = total * (1.0 / (total * row_totals))
        code_totals = 0.5 * jnp.sum(weights * row_totals, axis=0, keepdims=True)
        log_part = jnp.sum(code_totals * jnp.log(zsum)) * (1.0 / proto_size)
        stacked = jnp.where(
            place == 0,
            weights[0:1],
            jnp.where(place == 1, weights[1:2], jnp.where(place == 2, code_totals / zsum, 0.0)),
        ).T
        first = (stacked[:, 0:1] * first_ref[group].astype(F32) * scale).astype(BF16).astype(F32)
        second = (stacked[:, 1:2] * second_ref[group].astype(F32) * scale).astype(BF16).astype(F32)
        targets = 0.5 * (first + second)
        heated = scores_ref[group] * (1.0 / SOFTMAX_HEAT)
        loss = loss + (log_part - jnp.sum(targets * heated))
        dscore = ((jnp.exp(heated) * stacked[:, 2:3] - targets) * heat_scale).astype(BF16)
        dscore_ref[group] = dscore
        gunit = jnp.dot(dscore, wnorm_ref[...], preferred_element_type=F32)
        gunit_ref[group] = gunit.astype(gunit_ref.dtype)

    @pl.when(step == 0)
    def _():
        loss_ref[...] = jnp.full(loss_ref.shape, loss, F32)

    @pl.when(step > 0)
    def _():
        loss_ref[...] += loss


def gradients(where, columns, row_totals, first, second, scores, wnorm, count, total, proto_size, dtype):
    rows, protos = first.shape
    width = wnorm.shape[1]
    heat_scale = count / (32.0 * SOFTMAX_HEAT)
    _, places, _, share = row_totals[0].shape
    half = places // 2
    group = 2
    at = pl.BlockSpec((group, None, None, share, protos), lambda i, where: (i, where[0], where[1], 0, 0))
    first, second, scores = [in_vmem(value.reshape(half, 2, 2, share, protos)) for value in (first, second, scores)]
    row_totals = [value.reshape(2, half, 2, 3, share) for value in row_totals]
    return pl.pallas_call(
        functools.partial(
            gradient_kernel, count, total, heat_scale, proto_size, (len(columns), len(row_totals))
        ),
        grid_spec=pltpu.PrefetchScalarGridSpec(
            num_scalar_prefetch=1,
            grid=(half // group,),
            in_specs=[pl.BlockSpec((1, protos), lambda i, where: (0, 0)) for _ in columns]
            + [
                pl.BlockSpec((None, group, None, 3, share), lambda i, where: (where[1], i, where[0], 0, 0))
                for _ in row_totals
            ]
            + [at, at, at, pl.BlockSpec((protos, width), lambda i, where: (0, 0), pipeline_mode=pl.Buffered(1))],
            out_specs=[
                pl.BlockSpec((group, share, width), lambda i, where: (i, 0, 0)),
                pl.BlockSpec((group, share, protos), lambda i, where: (i, 0, 0)),
                pl.BlockSpec((1, LANES), lambda i, where: (0, 0)),
            ],
        ),
        out_shape=[
            jax.ShapeDtypeStruct((half, share, width), dtype),
            jax.ShapeDtypeStruct((half, share, protos), BF16),
            jax.ShapeDtypeStruct((1, LANES), F32),
        ],
        compiler_params=params(32),
        cost_estimate=cost(MIB, MIB),
        name="gradients",
    )(where, *columns, *row_totals, first, second, scores, in_vmem(wnorm))


def add_kernel(*refs):
    total = refs[0][...]
    for ref in refs[1:-1]:
        total = total + ref[...].astype(F32)
    refs[-1][...] = total.astype(refs[-1].dtype)


def add_blocks(values, dtype):
    count, share, width = values[0].shape
    at = pl.BlockSpec((1, share, width), lambda i: (i, 0, 0))
    return pl.pallas_call(
        add_kernel,
        grid=(count,),
        in_specs=[at for _ in values],
        out_specs=at,
        out_shape=jax.ShapeDtypeStruct(values[0].shape, dtype),
        compiler_params=params(16),
        cost_estimate=cost(count * share * width, 8 * count * share * width),
        name="add_blocks",
    )(*values)


def combine_kernel(parts, bit_ref, *refs):
    del bit_ref
    own_refs, other_refs, (own_ref, sent_ref) = refs[:parts], refs[parts : 2 * parts], refs[2 * parts :]
    add_kernel(*other_refs, sent_ref)
    add_kernel(*own_refs, own_ref)


def combine(bit, values):
    count, share, width = values[0].shape
    values = [value.reshape(count // 2, 2, share, width) for value in values]
    own_at = pl.BlockSpec((None, None, share, width), lambda i, bit: (i, bit[0], 0, 0))
    other_at = pl.BlockSpec((None, None, share, width), lambda i, bit: (i, 1 - bit[0], 0, 0))
    out_at = pl.BlockSpec((None, share, width), lambda i, bit: (i, 0, 0))
    return pl.pallas_call(
        functools.partial(combine_kernel, len(values)),
        grid_spec=pltpu.PrefetchScalarGridSpec(
            num_scalar_prefetch=1,
            grid=(count // 2,),
            in_specs=[own_at] * len(values) + [other_at] * len(values),
            out_specs=[out_at, out_at],
        ),
        out_shape=[
            jax.ShapeDtypeStruct((count // 2, share, width), F32),
            jax.ShapeDtypeStruct((count // 2, share, width), BF16),
        ],
        compiler_params=params(16),
        cost_estimate=cost(count * share * width, 9 * count * share * width),
        name="combine",
    )(bit, *values, *values)


def proto_gradient_kernel(index_ref, *refs):
    del index_ref
    dscore_refs, unit_refs, own_ref, sent_ref = refs[:4], refs[4:8], refs[8], refs[9]
    both = (((0,), (0,)), ((), ()))
    total = None
    for dscore_ref, unit_ref in zip(dscore_refs, unit_refs):
        rows, part = dscore_ref.shape[0], unit_ref.shape[-1]
        term = lax.dot_general(
            dscore_ref[...], unit_ref[...].reshape(rows, part), both, preferred_element_type=F32
        )
        total = term if total is None else total + term
    sent_ref[...] = total.astype(BF16)
    own_ref[...] = total


def proto_gradient(index, dscores, unit, batch_size):
    half, share, protos = dscores[0].shape
    width = unit.shape[1]
    part = width // batch_size
    rows = half * share
    last = batch_size - 1
    unit = unit.reshape(half, 2, 2, share, width)
    dscore_at = pl.BlockSpec((rows, protos), lambda i, index: (0, 0), pipeline_mode=pl.Buffered(1))

    def unit_at(low, core):
        return pl.BlockSpec(
            (half, None, None, share, part),
            lambda i, index: (0, index[1] ^ low, index[2] ^ core, 0, index[0] ^ (last - i)),
        )

    return pl.pallas_call(
        proto_gradient_kernel,
        grid_spec=pltpu.PrefetchScalarGridSpec(
            num_scalar_prefetch=1,
            grid=(batch_size,),
            in_specs=[dscore_at] * 4 + [unit_at(1, 1), unit_at(1, 0), unit_at(0, 1), unit_at(0, 0)],
            out_specs=[
                pl.BlockSpec((protos, part), lambda i, index: (0, 0)),
                pl.BlockSpec((None, protos, part), lambda i, index: (last - i, 0, 0)),
            ],
        ),
        out_shape=[
            jax.ShapeDtypeStruct((protos, part), F32),
            jax.ShapeDtypeStruct((batch_size, protos, part), BF16),
        ],
        compiler_params=params(32),
        cost_estimate=cost(MIB, MIB),
        name="proto_gradient",
    )(index, *[in_vmem(dscore.reshape(rows, protos)) for dscore in dscores], *[unit] * 4)


def embed_gradient_kernel(index_ref, embeddings_ref, own_ref, received_ref, out_ref):
    del index_ref
    gunit = own_ref[...] + received_ref[...].astype(F32)
    hidden = embeddings_ref[...].astype(F32)
    inverse = 1.0 / jnp.sqrt(jnp.sum(hidden * hidden, axis=1, keepdims=True) + NORM_EPSILON)
    along = jnp.sum(hidden * gunit, axis=1, keepdims=True)
    out_ref[...] = inverse * gunit - hidden * (inverse * inverse * inverse * along)


def embed_gradient(index, embeddings, own, received):
    share, width = own.shape
    whole = pl.BlockSpec((share, width), lambda i, index: (0, 0))
    return pl.pallas_call(
        embed_gradient_kernel,
        grid_spec=pltpu.PrefetchScalarGridSpec(
            num_scalar_prefetch=1,
            grid=(1,),
            in_specs=[pl.BlockSpec((share, width), lambda i, index: (index[0], 0)), whole, whole],
            out_specs=whole,
        ),
        out_shape=jax.ShapeDtypeStruct((share, width), F32),
        compiler_params=params(),
        cost_estimate=cost(8 * share * width, 4 * MIB),
        name="embed_gradient",
    )(index, embeddings, own, received)


PLACE = ("high", "low")


def swap(value, axis, distance):
    size = lax.axis_size(axis)
    return lax.ppermute(value, axis, [(i, i ^ distance) for i in range(size)])


def parts_of(value, axis):
    size = lax.axis_size(axis)
    if size > 4:
        return [lax.psum(value, axis)]
    return [value] + [swap(value, axis, distance) for distance in range(1, size)]


def proto_parts_of(value):
    return parts_of(value + swap(value, "core", 1), PLACE)


def scalar(value):
    return jnp.full((1,), value, jnp.int32)


def on_device(embeddings, prototypes, partners):
    row_count, width = embeddings.shape
    proto_count = prototypes.shape[0]
    batch_size = lax.axis_size("batch")
    places = lax.axis_size(PLACE)
    proto_size = 2 * places
    total_rows = row_count * batch_size
    centroids = proto_count * proto_size
    share = row_count // proto_size
    batch_index = lax.axis_index("batch")
    low = lax.axis_index("low")
    place = 2 * lax.axis_index("high") + low
    core = lax.axis_index("core")
    proto_index = 2 * place + core

    quarter = row_count // 4
    steps = quarter // OWN_BLOCK
    own = own_rows(embeddings, scalar((2 * low + core) * steps), OWN_BLOCK, steps)
    table = lax.all_gather(own, ("batch", "low", "core"), axis=0, tiled=True)

    unit, wnorm, scores, expo, zsum, columns = scores_of(embeddings, prototypes, share)
    columns = parts_of(columns, "batch")
    for iteration in range(ITERS - 1):
        row_totals = proto_parts_of(row_pass(columns, expo, centroids))
        columns = parts_of(column_pass(row_totals, expo, total_rows), "batch")

    first, second = partner_pass(partners[:, 0], partners[:, 1], table, wnorm)
    row_totals = proto_parts_of(partner_row_pass(columns, zsum, first, second, centroids))
    others = (scores, wnorm, centroids, total_rows, proto_size)

    def quarter_of(low_bit, core_bit, dtype):
        where = jnp.stack([low_bit, core_bit]).astype(jnp.int32)
        return gradients(where, columns, row_totals, first, second, *others, dtype)

    gunit, dscore_a, loss_a = quarter_of(1 - low, 1 - core, BF16)
    received = swap(gunit, "core", 1)
    kept, dscore_b, loss_b = quarter_of(1 - low, core, F32)
    sent = add_blocks([kept, received], BF16)
    sent, first, second = lax.optimization_barrier((sent, first, second))
    from_neighbor = swap(sent, PLACE, 1)

    gunit, dscore_c, loss_c = quarter_of(low, 1 - core, BF16)
    received = swap(gunit, "core", 1)
    kept, dscore_d, loss_d = quarter_of(low, core, F32)
    grad_proto, proto_sent = proto_gradient(
        jnp.stack([batch_index, low, core]).astype(jnp.int32),
        (dscore_a, dscore_b, dscore_c, dscore_d),
        unit,
        batch_size,
    )
    kept, grad_proto, proto_sent = lax.optimization_barrier((kept, grad_proto, proto_sent))

    loss = loss_a + loss_b + loss_c + loss_d
    values = [kept, received, from_neighbor]
    bit = 1
    while (1 << bit) < places:
        kept, sent = combine(scalar((place >> bit) % 2), values)
        if bit == 1:
            sent, loss = lax.optimization_barrier((sent, loss))
            loss = functools.reduce(jnp.add, parts_of(loss, "batch"))
            loss, proto_sent = lax.optimization_barrier((loss, proto_sent))
        values = [kept, swap(sent, PLACE, 1 << bit)]
        bit += 1
    grad_embed = embed_gradient(scalar(proto_index), embeddings, *[value[0] for value in values])
    loss = functools.reduce(jnp.add, proto_parts_of(loss))
    loss = loss[0, 0] / total_rows

    for distance in range(batch_size - 1, 0, -1):
        grad_proto = grad_proto + swap(proto_sent[distance], "batch", distance).astype(F32)

    return (loss, grad_proto, grad_embed)


def solution(mesh):
    batch_size, proto_size = mesh.shape["batch"], mesh.shape["proto"]
    devices = mesh.devices.reshape(batch_size, proto_size // 4, 2, 2)
    proto = ("high", "low", "core")
    return jax.shard_map(
        on_device,
        mesh=jax.sharding.Mesh(devices, ("batch",) + proto),
        in_specs=(P("batch", None), P(proto, None), P("batch", None)),
        out_specs=(P(), P(proto, "batch"), P(("batch",) + proto, None)),
        check_vma=False,
    )
```

```python
import functools

import jax
import jax.numpy as jnp
from jax import lax
from jax.experimental import pallas as pl
from jax.experimental.pallas import tpu as pltpu
from jax.sharding import PartitionSpec as P

ITERS = 3
BALANCE_SMOOTHING = 0.05
SOFTMAX_HEAT = 0.1
NORM_EPSILON = 1e-06
LANES = 128
CHUNK = 256
STREAMS = 4
OWN_BLOCK = 256
MIB = 1 << 20
F32 = jnp.float32
BF16 = jnp.bfloat16


def params(mib=60):
    return pltpu.CompilerParams(vmem_limit_bytes=mib * MIB)


def in_vmem(value):
    return pltpu.with_memory_space_constraint(value, pltpu.VMEM)


def cost(flops, moved, exps=0):
    return pl.CostEstimate(flops=flops, bytes_accessed=moved, transcendentals=exps)


def normalized(block):
    wide = block.astype(F32)
    inverse = 1.0 / jnp.sqrt(jnp.sum(wide * wide, axis=1, keepdims=True) + NORM_EPSILON)
    return wide * inverse


def lane_row_sums(values):
    columns = values.shape[1]
    part = values[:, 0:LANES]
    for start in range(LANES, columns, LANES):
        part = part + values[:, start : start + LANES]
    return jnp.sum(part.T, axis=0, keepdims=True)


def split_rows(row):
    high = row.astype(BF16).astype(F32)
    middle = (row - high).astype(BF16).astype(F32)
    low = row - high - middle
    place = lax.broadcasted_iota(jnp.int32, (16, row.shape[1]), 0)
    stacked = jnp.where(place == 0, high, jnp.where(place == 1, middle, jnp.where(place == 2, low, 0.0)))
    return stacked.astype(BF16)


def total_of(refs):
    total = refs[0][...]
    for ref in refs[1:]:
        total = total + ref[...]
    return total


def own_rows_kernel(index_ref, embeddings_ref, table_ref, stage_ref):
    del index_ref
    rows, columns = embeddings_ref.shape
    unit = normalized(embeddings_ref[...]).astype(BF16).astype(F32)
    groups = columns // LANES
    for k in range(groups):
        stage_ref[pl.ds(k, rows, stride=groups), :] = unit[:, k * LANES : (k + 1) * LANES]
    table_ref[...] = stage_ref[...].reshape(rows, groups, LANES).astype(BF16)


def own_rows(embeddings, index, block, count):
    columns = embeddings.shape[1]
    groups = columns // LANES
    return pl.pallas_call(
        own_rows_kernel,
        grid_spec=pltpu.PrefetchScalarGridSpec(
            num_scalar_prefetch=1,
            grid=(count,),
            in_specs=[pl.BlockSpec((block, columns), lambda i, index: (index[0] + i, 0))],
            out_specs=pl.BlockSpec((block, groups, LANES), lambda i, index: (i, 0, 0)),
            scratch_shapes=[pltpu.VMEM((block * groups, LANES), F32)],
        ),
        out_shape=jax.ShapeDtypeStruct((block * count, groups, LANES), BF16),
        compiler_params=params(16),
        name="own_rows",
    )(index, embeddings)


def scores_kernel(embeddings_ref, prototypes_ref, unit_ref, wnorm_ref, scores_ref, expo_ref, zsum_ref, column_ref):
    step = pl.program_id(0)

    @pl.when(step == 0)
    def _():
        wnorm_ref[...] = normalized(prototypes_ref[...]).astype(BF16)

    share = zsum_ref.shape[-1]
    sums = None
    for k in range(2):
        at = slice(k * share, (k + 1) * share)
        unit = normalized(embeddings_ref[at]).astype(BF16)
        unit_ref[at] = unit
        scores = lax.dot_general(unit, wnorm_ref[...], (((1,), (1,)), ((), ())), preferred_element_type=F32)
        scores_ref[at] = scores
        soft = jnp.exp(scores * (1.0 / SOFTMAX_HEAT))
        zsum_ref[k, 0] = lane_row_sums(soft)
        expo = soft * soft
        expo_ref[at] = expo.astype(BF16)
        part = jnp.sum(expo, axis=0, keepdims=True)
        sums = part if sums is None else sums + part

    @pl.when(step == 0)
    def _():
        column_ref[...] = sums

    @pl.when(step > 0)
    def _():
        column_ref[...] += sums


def scores_of(embeddings, prototypes, share):
    rows, columns = embeddings.shape
    protos = prototypes.shape[0]
    return pl.pallas_call(
        scores_kernel,
        grid=(rows // share // 2,),
        in_specs=[
            pl.BlockSpec((2 * share, columns), lambda i: (i, 0)),
            pl.BlockSpec((protos, columns), lambda i: (0, 0), pipeline_mode=pl.Buffered(1)),
        ],
        out_specs=[
            pl.BlockSpec((2 * share, columns), lambda i: (i, 0)),
            pl.BlockSpec((protos, columns), lambda i: (0, 0)),
            pl.BlockSpec((2 * share, protos), lambda i: (i, 0)),
            pl.BlockSpec((2 * share, protos), lambda i: (i, 0)),
            pl.BlockSpec((2, 1, 1, share), lambda i: (0, i, 0, 0)),
            pl.BlockSpec((1, protos), lambda i: (0, 0)),
        ],
        out_shape=[
            jax.ShapeDtypeStruct((rows, columns), BF16),
            jax.ShapeDtypeStruct((protos, columns), BF16),
            jax.ShapeDtypeStruct((rows, protos), F32),
            jax.ShapeDtypeStruct((rows, protos), BF16),
            jax.ShapeDtypeStruct((2, rows // share // 2, 1, share), F32),
            jax.ShapeDtypeStruct((1, protos), F32),
        ],
        compiler_params=params(28),
        cost_estimate=cost(2 * rows * columns * protos, 22 * MIB, rows * protos),
        name="scores",
    )(embeddings, prototypes)


def row_kernel(count, parts, *refs):
    column_refs, expo_refs, row_ref = refs[:parts], refs[parts:-1], refs[-1]
    scale = split_rows(1.0 / (count * total_of(column_refs)))
    block = expo_refs[0].shape[0]
    for k, expo_ref in enumerate(expo_refs):
        sums = lax.dot_general(scale, expo_ref[...], (((1,), (1,)), ((), ())), preferred_element_type=F32)
        row_ref[:, k * block : (k + 1) * block] = jnp.sum(sums, axis=0, keepdims=True)


def streams_of(shape):
    return [pl.BlockSpec(shape, functools.partial(lambda k, i: (STREAMS * i + k, 0), k)) for k in range(STREAMS)]


def row_pass(columns, expo, count):
    rows, protos = expo.shape
    block = rows // 8
    return pl.pallas_call(
        functools.partial(row_kernel, count, len(columns)),
        grid=(rows // block // STREAMS,),
        in_specs=[pl.BlockSpec((1, protos), lambda i: (0, 0)) for _ in columns] + streams_of((block, protos)),
        out_specs=pl.BlockSpec((1, STREAMS * block), lambda i: (0, i)),
        out_shape=jax.ShapeDtypeStruct((1, rows), F32),
        compiler_params=params(8),
        cost_estimate=cost(2 * rows * protos, 4 * MIB),
        name="row_pass",
    )(*columns, *[in_vmem(expo)] * STREAMS)


def column_kernel(count, parts, *refs):
    row_refs, expo_refs, column_ref = refs[:parts], refs[parts:-1], refs[-1]
    step = pl.program_id(0)
    scale = split_rows(1.0 / (count * total_of(row_refs)))
    block = expo_refs[0].shape[0]
    total = None
    for k, expo_ref in enumerate(expo_refs):
        sums = lax.dot_general(
            scale[:, k * block : (k + 1) * block], expo_ref[...], (((1,), (0,)), ((), ())), preferred_element_type=F32
        )
        total = sums if total is None else total + sums
    total = jnp.sum(total, axis=0, keepdims=True)

    @pl.when(step == 0)
    def _():
        column_ref[...] = total

    @pl.when(step > 0)
    def _():
        column_ref[...] += total


def column_pass(row_totals, expo, count):
    rows, protos = expo.shape
    block = rows // 8
    return pl.pallas_call(
        functools.partial(column_kernel, count, len(row_totals)),
        grid=(rows // block // STREAMS,),
        in_specs=[pl.BlockSpec((1, STREAMS * block), lambda i: (0, i)) for _ in row_totals]
        + streams_of((block, protos)),
        out_specs=pl.BlockSpec((1, protos), lambda i: (0, 0)),
        out_shape=jax.ShapeDtypeStruct((1, protos), F32),
        compiler_params=params(8),
        cost_estimate=cost(2 * rows * protos, 4 * MIB),
        name="column_pass",
    )(*row_totals, *[in_vmem(expo)] * STREAMS)


def partner_kernel(first_ref, second_ref, source_ref, wnorm_ref, first_expo_ref, second_expo_ref, table_ref, semaphores, *stages):
    step = pl.program_id(0)
    groups = table_ref.shape[1]

    @pl.when(step == 0)
    def _():
        parts = semaphores.shape[0]
        size = source_ref.shape[0] // parts
        copies = [
            pltpu.make_async_copy(
                source_ref.at[pl.ds(k * size, size)], table_ref.at[pl.ds(k * size, size)], semaphores.at[k]
            )
            for k in range(parts)
        ]
        for copy in copies:
            copy.start()
        for copy in copies:
            copy.wait()

    rows = first_expo_ref.shape[0]
    wnorm = wnorm_ref[...]
    chunks = [
        (which_ref, out_ref, start)
        for start in range(0, rows, CHUNK)
        for which_ref, out_ref in ((first_ref, first_expo_ref), (second_ref, second_expo_ref))
    ]
    for number, (which_ref, out_ref, start) in enumerate(chunks):
        stage_ref = stages[number % 2]
        for row in range(CHUNK):
            place = which_ref[step * rows + start + row]
            stage_ref[row * groups : (row + 1) * groups, :] = table_ref[place].astype(F32)
        unit = jnp.concatenate(
            [stage_ref[pl.ds(k, CHUNK, stride=groups), :].astype(BF16) for k in range(groups)], axis=1
        )
        scores = lax.dot_general(unit, wnorm, (((1,), (1,)), ((), ())), preferred_element_type=F32)
        soft = jnp.exp(scores * (1.0 / SOFTMAX_HEAT))
        out_ref[start : start + CHUNK, :] = (soft * soft).astype(out_ref.dtype)


def partner_pass(first, second, table, wnorm):
    rows = first.shape[0]
    protos, columns = wnorm.shape
    groups = columns // LANES
    block = 2 * CHUNK
    return pl.pallas_call(
        partner_kernel,
        grid_spec=pltpu.PrefetchScalarGridSpec(
            num_scalar_prefetch=2,
            grid=(rows // block,),
            in_specs=[
                pl.BlockSpec(memory_space=pl.ANY),
                pl.BlockSpec((protos, columns), lambda i, *_: (0, 0), pipeline_mode=pl.Buffered(1)),
            ],
            out_specs=[
                pl.BlockSpec((block, protos), lambda i, *_: (i, 0)),
                pl.BlockSpec((block, protos), lambda i, *_: (i, 0)),
            ],
            scratch_shapes=[
                pltpu.VMEM(table.shape, BF16),
                pltpu.SemaphoreType.DMA((STREAMS,)),
            ]
            + [pltpu.VMEM((CHUNK * groups, LANES), F32)] * 2,
        ),
        out_shape=[jax.ShapeDtypeStruct((rows, protos), BF16)] * 2,
        compiler_params=params(28),
        cost_estimate=cost(4 * rows * columns * protos, 28 * MIB, 2 * rows * protos),
        name="partner_scores",
    )(first, second, table, wnorm)


def partner_row_kernel(count, parts, *refs):
    column_refs, zsum_ref, row_ref = refs[:parts], refs[parts], refs[-1]
    first_refs, second_refs = refs[parts + 1 : parts + 1 + STREAMS], refs[parts + 1 + STREAMS : -1]
    scale = 1.0 / (count * total_of(column_refs))
    for k in range(STREAMS):
        at = (k % 2, k // 2)
        row_ref[at] = jnp.concatenate(
            [
                lane_row_sums(first_refs[k][...].astype(F32) * scale),
                lane_row_sums(second_refs[k][...].astype(F32) * scale),
                zsum_ref[at],
            ],
            axis=0,
        )


def partner_row_pass(columns, zsum, first, second, count):
    rows, protos = first.shape
    share = zsum.shape[-1]
    group = STREAMS // 2
    return pl.pallas_call(
        functools.partial(partner_row_kernel, count, len(columns)),
        grid=(rows // share // STREAMS,),
        in_specs=[pl.BlockSpec((1, protos), lambda i: (0, 0)) for _ in columns]
        + [pl.BlockSpec((2, group, 1, share), lambda i: (0, i, 0, 0))]
        + streams_of((share, protos)) * 2,
        out_specs=pl.BlockSpec((2, group, 3, share), lambda i: (0, i, 0, 0)),
        out_shape=jax.ShapeDtypeStruct((2, rows // share // 2, 3, share), F32),
        compiler_params=params(16),
        cost_estimate=cost(4 * rows * protos, 8 * MIB),
        name="partner_row_pass",
    )(*columns, zsum, *[in_vmem(first)] * STREAMS, *[in_vmem(second)] * STREAMS)


def gradient_kernel(count, total, heat_scale, proto_size, parts, core_ref, *refs):
    del core_ref
    column_refs, row_refs = refs[: parts[0]], refs[parts[0] : parts[0] + parts[1]]
    first_ref, second_ref, scores_ref, wnorm_ref, gunit_ref, dscore_ref, loss_ref = refs[parts[0] + parts[1] :]
    step = pl.program_id(0)
    scale = 1.0 / (count * total_of(column_refs))
    totals = total_of(row_refs)
    share = totals.shape[-1]
    place = lax.broadcasted_iota(jnp.int32, (8, share), 0)
    loss = jnp.zeros((), F32)
    for group in range(totals.shape[0]):
        row_totals, zsum = totals[group, 0:2], totals[group, 2:3]
        weights = total * (1.0 / (total * row_totals))
        code_totals = 0.5 * jnp.sum(weights * row_totals, axis=0, keepdims=True)
        log_part = jnp.sum(code_totals * jnp.log(zsum)) * (1.0 / proto_size)
        stacked = jnp.where(
            place == 0,
            weights[0:1],
            jnp.where(place == 1, weights[1:2], jnp.where(place == 2, code_totals / zsum, 0.0)),
        ).T
        first = (stacked[:, 0:1] * first_ref[group].astype(F32) * scale).astype(BF16).astype(F32)
        second = (stacked[:, 1:2] * second_ref[group].astype(F32) * scale).astype(BF16).astype(F32)
        targets = 0.5 * (first + second)
        heated = scores_ref[group] * (1.0 / SOFTMAX_HEAT)
        loss = loss + (log_part - jnp.sum(targets * heated))
        dscore = ((jnp.exp(heated) * stacked[:, 2:3] - targets) * heat_scale).astype(BF16)
        dscore_ref[group] = dscore
        gunit = jnp.dot(dscore, wnorm_ref[...], preferred_element_type=F32)
        gunit_ref[group] = gunit.astype(gunit_ref.dtype)

    @pl.when(step == 0)
    def _():
        loss_ref[...] = jnp.full(loss_ref.shape, loss, F32)

    @pl.when(step > 0)
    def _():
        loss_ref[...] += loss


def gradients(where, columns, row_totals, first, second, scores, wnorm, count, total, proto_size, dtype):
    rows, protos = first.shape
    width = wnorm.shape[1]
    heat_scale = count / (32.0 * SOFTMAX_HEAT)
    _, places, _, share = row_totals[0].shape
    top = places // 4
    at = pl.BlockSpec((1, None, None, None, share, protos), lambda i, where: (i, where[0], where[1], where[2], 0, 0))
    first, second, scores = [in_vmem(value.reshape(top, 2, 2, 2, share, protos)) for value in (first, second, scores)]
    row_totals = [value.reshape(2, top, 2, 2, 3, share) for value in row_totals]
    return pl.pallas_call(
        functools.partial(
            gradient_kernel, count, total, heat_scale, proto_size, (len(columns), len(row_totals))
        ),
        grid_spec=pltpu.PrefetchScalarGridSpec(
            num_scalar_prefetch=1,
            grid=(top,),
            in_specs=[pl.BlockSpec((1, protos), lambda i, where: (0, 0)) for _ in columns]
            + [
                pl.BlockSpec(
                    (None, 1, None, None, 3, share), lambda i, where: (where[2], i, where[0], where[1], 0, 0)
                )
                for _ in row_totals
            ]
            + [at, at, at, pl.BlockSpec((protos, width), lambda i, where: (0, 0), pipeline_mode=pl.Buffered(1))],
            out_specs=[
                pl.BlockSpec((1, share, width), lambda i, where: (i, 0, 0)),
                pl.BlockSpec((1, share, protos), lambda i, where: (i, 0, 0)),
                pl.BlockSpec((1, LANES), lambda i, where: (0, 0)),
            ],
        ),
        out_shape=[
            jax.ShapeDtypeStruct((top, share, width), dtype),
            jax.ShapeDtypeStruct((top, share, protos), BF16),
            jax.ShapeDtypeStruct((1, LANES), F32),
        ],
        compiler_params=params(16),
        cost_estimate=cost(MIB, MIB),
        name="gradients",
    )(where, *columns, *row_totals, first, second, scores, in_vmem(wnorm))


def add_kernel(*refs):
    total = refs[0][...]
    for ref in refs[1:-1]:
        total = total + ref[...].astype(F32)
    refs[-1][...] = total.astype(refs[-1].dtype)


def add_blocks(values, dtype):
    count, share, width = values[0].shape
    at = pl.BlockSpec((1, share, width), lambda i: (i, 0, 0))
    return pl.pallas_call(
        add_kernel,
        grid=(count,),
        in_specs=[at for _ in values],
        out_specs=at,
        out_shape=jax.ShapeDtypeStruct(values[0].shape, dtype),
        compiler_params=params(12),
        cost_estimate=cost(count * share * width, 8 * count * share * width),
        name="add_blocks",
    )(*values)


def combine_kernel(parts, bit_ref, *refs):
    del bit_ref
    own_refs, other_refs, (own_ref, sent_ref) = refs[:parts], refs[parts : 2 * parts], refs[2 * parts :]
    add_kernel(*other_refs, sent_ref)
    add_kernel(*own_refs, own_ref)


def combine(bit, values):
    count, share, width = values[0].shape
    values = [value.reshape(count // 2, 2, share, width) for value in values]
    own_at = pl.BlockSpec((None, None, share, width), lambda i, bit: (i, bit[0], 0, 0))
    other_at = pl.BlockSpec((None, None, share, width), lambda i, bit: (i, 1 - bit[0], 0, 0))
    out_at = pl.BlockSpec((None, share, width), lambda i, bit: (i, 0, 0))
    return pl.pallas_call(
        functools.partial(combine_kernel, len(values)),
        grid_spec=pltpu.PrefetchScalarGridSpec(
            num_scalar_prefetch=1,
            grid=(count // 2,),
            in_specs=[own_at] * len(values) + [other_at] * len(values),
            out_specs=[out_at, out_at],
        ),
        out_shape=[
            jax.ShapeDtypeStruct((count // 2, share, width), F32),
            jax.ShapeDtypeStruct((count // 2, share, width), BF16),
        ],
        compiler_params=params(16),
        cost_estimate=cost(count * share * width, 9 * count * share * width),
        name="combine",
    )(bit, *values, *values)


def proto_gradient_kernel(index_ref, *refs):
    del index_ref
    dscore_refs, unit_refs, own_ref, sent_ref = refs[:8], refs[8:16], refs[16], refs[17]
    both = (((0,), (0,)), ((), ()))
    total = None
    for dscore_ref, unit_ref in zip(dscore_refs, unit_refs):
        rows, part = dscore_ref.shape[0], unit_ref.shape[-1]
        term = lax.dot_general(
            dscore_ref[...], unit_ref[...].reshape(rows, part), both, preferred_element_type=F32
        )
        total = term if total is None else total + term
    sent_ref[...] = total.astype(BF16)
    own_ref[...] = total


def proto_gradient(index, dscores, unit, batch_size):
    top, share, protos = dscores[0].shape
    width = unit.shape[1]
    part = width // batch_size
    rows = top * share
    last = batch_size - 1
    unit = unit.reshape(top, 2, 2, 2, share, width)
    dscore_at = pl.BlockSpec((rows, protos), lambda i, index: (0, 0), pipeline_mode=pl.Buffered(1))

    def unit_at(number):
        return pl.BlockSpec(
            (top, None, None, None, share, part),
            lambda i, index: (
                0, index[1] ^ (number >> 2), index[2] ^ (number >> 1 & 1), index[3] ^ (number & 1), 0, index[0] ^ (last - i),
            ),
        )

    return pl.pallas_call(
        proto_gradient_kernel,
        grid_spec=pltpu.PrefetchScalarGridSpec(
            num_scalar_prefetch=1,
            grid=(batch_size,),
            in_specs=[dscore_at] * 8 + [unit_at(number) for number in range(8)],
            out_specs=[
                pl.BlockSpec((protos, part), lambda i, index: (0, 0)),
                pl.BlockSpec((None, protos, part), lambda i, index: (last - i, 0, 0)),
            ],
        ),
        out_shape=[
            jax.ShapeDtypeStruct((protos, part), F32),
            jax.ShapeDtypeStruct((batch_size, protos, part), BF16),
        ],
        compiler_params=params(20),
        cost_estimate=cost(MIB, MIB),
        name="proto_gradient",
    )(index, *[in_vmem(dscore.reshape(rows, protos)) for dscore in dscores], *[unit] * 8)


def embed_gradient_kernel(index_ref, embeddings_ref, *refs):
    del index_ref
    *part_refs, out_ref = refs
    gunit = part_refs[0][...]
    for ref in part_refs[1:]:
        gunit = gunit + ref[...].astype(F32)
    hidden = embeddings_ref[...].astype(F32)
    inverse = 1.0 / jnp.sqrt(jnp.sum(hidden * hidden, axis=1, keepdims=True) + NORM_EPSILON)
    along = jnp.sum(hidden * gunit, axis=1, keepdims=True)
    out_ref[...] = inverse * gunit - hidden * (inverse * inverse * inverse * along)


def embed_gradient(index, embeddings, values):
    share, width = values[0].shape
    whole = pl.BlockSpec((share, width), lambda i, index: (0, 0))
    return pl.pallas_call(
        embed_gradient_kernel,
        grid_spec=pltpu.PrefetchScalarGridSpec(
            num_scalar_prefetch=1,
            grid=(1,),
            in_specs=[pl.BlockSpec((share, width), lambda i, index: (index[0], 0))] + [whole for _ in values],
            out_specs=whole,
        ),
        out_shape=jax.ShapeDtypeStruct((share, width), F32),
        compiler_params=params(12),
        cost_estimate=cost(8 * share * width, 4 * MIB),
        name="embed_gradient",
    )(index, embeddings, *values)


PLACE = ("top", "middle", "low")


def swap(value, axis, distance):
    size = lax.axis_size(axis)
    return lax.ppermute(value, axis, [(i, i ^ distance) for i in range(size)])


def parts_of(value, axis):
    size = lax.axis_size(axis)
    if size > 4:
        return [lax.psum(value, axis)]
    return [value] + [swap(value, axis, distance) for distance in range(1, size)]


def proto_parts_of(value):
    return parts_of(value + swap(value, "core", 1), PLACE)


def scalar(value):
    return jnp.full((1,), value, jnp.int32)


def on_device(embeddings, prototypes, partners):
    row_count, width = embeddings.shape
    proto_count = prototypes.shape[0]
    batch_size = lax.axis_size("batch")
    places = lax.axis_size(PLACE)
    proto_size = 2 * places
    total_rows = row_count * batch_size
    centroids = proto_count * proto_size
    share = row_count // proto_size
    batch_index = lax.axis_index("batch")
    low = lax.axis_index("low")
    middle = lax.axis_index("middle")
    place = lax.axis_index(PLACE)
    core = lax.axis_index("core")
    proto_index = 2 * place + core

    quarter = row_count // 4
    steps = quarter // OWN_BLOCK
    own = own_rows(embeddings, scalar((2 * low + core) * steps), OWN_BLOCK, steps)
    table = lax.all_gather(own, ("batch", "low", "core"), axis=0, tiled=True)

    unit, wnorm, scores, expo, zsum, columns = scores_of(embeddings, prototypes, share)
    columns = parts_of(columns, "batch")
    for iteration in range(ITERS - 1):
        row_totals = proto_parts_of(row_pass(columns, expo, centroids))
        columns = parts_of(column_pass(row_totals, expo, total_rows), "batch")

    first, second = partner_pass(partners[:, 0], partners[:, 1], table, wnorm)
    row_totals = proto_parts_of(partner_row_pass(columns, zsum, first, second, centroids))
    others = (scores, wnorm, centroids, total_rows, proto_size)

    def after(value, *earlier):
        return lax.optimization_barrier((value, *earlier))[0]

    losses, dscores = [], {}

    def part_of(number, *earlier):
        place_bits = [middle ^ (number >> 1), low ^ (number & 1)]

        def run(other, dtype):
            where = after(jnp.stack(place_bits + [core ^ other]).astype(jnp.int32), *earlier)
            gunit, dscores[2 * number + other], loss = gradients(
                where, columns, row_totals, first, second, *others, dtype
            )
            losses.append(loss)
            return gunit

        gunit = run(1, BF16)
        return [run(0, F32), swap(gunit, "core", 1)]

    forwarded = add_blocks(part_of(3), BF16)
    from_forwarder = swap(forwarded, PLACE, 1)
    near = add_blocks(part_of(1, forwarded), BF16)
    from_near = swap(near, PLACE, 1)
    across = part_of(2, near)
    values = part_of(0, near)

    loss = functools.reduce(jnp.add, losses)
    loss = functools.reduce(jnp.add, parts_of(loss, "batch"))
    index = jnp.stack([batch_index, middle, low, core]).astype(jnp.int32)
    grad_proto, proto_sent = proto_gradient(index, [dscores[number] for number in range(8)], unit, batch_size)
    from_forwarder = after(from_forwarder, proto_sent)
    across = add_blocks(across + [from_forwarder], BF16)
    values += [from_near, swap(across, PLACE, 2)]
    proto_sent = after(proto_sent, loss, across, from_near)

    bit = 2
    while (1 << bit) < places:
        kept, sent = combine(scalar((place >> bit) % 2), values)
        values = [kept, swap(sent, PLACE, 1 << bit)]
        bit += 1
    grad_embed = embed_gradient(scalar(proto_index), embeddings, [value[0] for value in values])
    loss = loss + swap(loss, "core", 1)
    arrived = [swap(proto_sent[distance], "batch", distance) for distance in range(batch_size - 1, 0, -1)]
    loss = functools.reduce(jnp.add, parts_of(after(loss, *arrived), PLACE))
    loss = loss[0, 0] / total_rows
    for block in arrived:
        grad_proto = grad_proto + block.astype(F32)

    return (loss, grad_proto, grad_embed)


def solution(mesh):
    batch_size, proto_size = mesh.shape["batch"], mesh.shape["proto"]
    devices = mesh.devices.reshape(batch_size, proto_size // 8, 2, 2, 2)
    proto = PLACE + ("core",)
    return jax.shard_map(
        on_device,
        mesh=jax.sharding.Mesh(devices, ("batch",) + proto),
        in_specs=(P("batch", None), P(proto, None), P("batch", None)),
        out_specs=(P(), P(proto, "batch"), P(("batch",) + proto, None)),
        check_vma=False,
    )
```

```python
import functools

import jax
import jax.numpy as jnp
from jax import lax
from jax.experimental import pallas as pl
from jax.experimental.pallas import tpu as pltpu
from jax.sharding import PartitionSpec as P

ITERS = 3
BALANCE_SMOOTHING = 0.05
SOFTMAX_HEAT = 0.1
NORM_EPSILON = 1e-06
LANES = 128
CHUNK = 256
STREAMS = 4
OWN_BLOCK = 256
MIB = 1 << 20
F32 = jnp.float32
BF16 = jnp.bfloat16


def params(mib=60):
    return pltpu.CompilerParams(vmem_limit_bytes=mib * MIB)


def in_vmem(value):
    return pltpu.with_memory_space_constraint(value, pltpu.VMEM)


def cost(flops, moved, exps=0):
    return pl.CostEstimate(flops=flops, bytes_accessed=moved, transcendentals=exps)


def normalized(block):
    wide = block.astype(F32)
    inverse = 1.0 / jnp.sqrt(jnp.sum(wide * wide, axis=1, keepdims=True) + NORM_EPSILON)
    return wide * inverse


def lane_row_sums(values):
    columns = values.shape[1]
    part = values[:, 0:LANES]
    for start in range(LANES, columns, LANES):
        part = part + values[:, start : start + LANES]
    return jnp.sum(part.T, axis=0, keepdims=True)


def split_rows(row):
    high = row.astype(BF16).astype(F32)
    middle = (row - high).astype(BF16).astype(F32)
    low = row - high - middle
    place = lax.broadcasted_iota(jnp.int32, (16, row.shape[1]), 0)
    stacked = jnp.where(place == 0, high, jnp.where(place == 1, middle, jnp.where(place == 2, low, 0.0)))
    return stacked.astype(BF16)


def total_of(refs):
    total = refs[0][...]
    for ref in refs[1:]:
        total = total + ref[...]
    return total


def own_rows_kernel(index_ref, embeddings_ref, table_ref, stage_ref):
    del index_ref
    rows, columns = embeddings_ref.shape
    unit = normalized(embeddings_ref[...]).astype(BF16).astype(F32)
    groups = columns // LANES
    for k in range(groups):
        stage_ref[pl.ds(k, rows, stride=groups), :] = unit[:, k * LANES : (k + 1) * LANES]
    table_ref[...] = stage_ref[...].reshape(rows, groups, LANES).astype(BF16)


def own_rows(embeddings, index, block, count):
    columns = embeddings.shape[1]
    groups = columns // LANES
    return pl.pallas_call(
        own_rows_kernel,
        grid_spec=pltpu.PrefetchScalarGridSpec(
            num_scalar_prefetch=1,
            grid=(count,),
            in_specs=[pl.BlockSpec((block, columns), lambda i, index: (index[0] + i, 0))],
            out_specs=pl.BlockSpec((block, groups, LANES), lambda i, index: (i, 0, 0)),
            scratch_shapes=[pltpu.VMEM((block * groups, LANES), F32)],
        ),
        out_shape=jax.ShapeDtypeStruct((block * count, groups, LANES), BF16),
        compiler_params=params(60),
        name="own_rows",
    )(index, embeddings)


def scores_kernel(embeddings_ref, prototypes_ref, unit_ref, wnorm_ref, scores_ref, expo_ref, zsum_ref, column_ref):
    step = pl.program_id(0)

    @pl.when(step == 0)
    def _():
        wnorm_ref[...] = normalized(prototypes_ref[...]).astype(BF16)

    share = embeddings_ref.shape[0] // 2
    sums = None
    for k in range(2):
        at = slice(k * share, (k + 1) * share)
        unit = normalized(embeddings_ref[at]).astype(BF16)
        unit_ref[at] = unit
        scores = lax.dot_general(unit, wnorm_ref[...], (((1,), (1,)), ((), ())), preferred_element_type=F32)
        scores_ref[at] = scores
        soft = jnp.exp(scores * (1.0 / SOFTMAX_HEAT))
        zsum_ref[:, at] = lane_row_sums(soft)
        expo = soft * soft
        expo_ref[at] = expo.astype(BF16)
        part = jnp.sum(expo, axis=0, keepdims=True)
        sums = part if sums is None else sums + part

    @pl.when(step == 0)
    def _():
        column_ref[...] = sums

    @pl.when(step > 0)
    def _():
        column_ref[...] += sums


def scores_of(embeddings, prototypes, share):
    rows, columns = embeddings.shape
    protos = prototypes.shape[0]
    return pl.pallas_call(
        scores_kernel,
        grid=(rows // share // 2,),
        in_specs=[
            pl.BlockSpec((2 * share, columns), lambda i: (i, 0)),
            pl.BlockSpec((protos, columns), lambda i: (0, 0), pipeline_mode=pl.Buffered(1)),
        ],
        out_specs=[
            pl.BlockSpec((2 * share, columns), lambda i: (i, 0)),
            pl.BlockSpec((protos, columns), lambda i: (0, 0)),
            pl.BlockSpec((2 * share, protos), lambda i: (i, 0)),
            pl.BlockSpec((2 * share, protos), lambda i: (i, 0)),
            pl.BlockSpec((1, 2 * share), lambda i: (0, i)),
            pl.BlockSpec((1, protos), lambda i: (0, 0)),
        ],
        out_shape=[
            jax.ShapeDtypeStruct((rows, columns), BF16),
            jax.ShapeDtypeStruct((protos, columns), BF16),
            jax.ShapeDtypeStruct((rows, protos), F32),
            jax.ShapeDtypeStruct((rows, protos), BF16),
            jax.ShapeDtypeStruct((1, rows), F32),
            jax.ShapeDtypeStruct((1, protos), F32),
        ],
        compiler_params=params(50),
        cost_estimate=cost(2 * rows * columns * protos, 22 * MIB, rows * protos),
        name="scores",
    )(embeddings, prototypes)


def row_kernel(count, parts, *refs):
    column_refs, expo_refs, row_ref = refs[:parts], refs[parts:-1], refs[-1]
    scale = split_rows(1.0 / (count * total_of(column_refs)))
    block = expo_refs[0].shape[0]
    for k, expo_ref in enumerate(expo_refs):
        sums = lax.dot_general(scale, expo_ref[...], (((1,), (1,)), ((), ())), preferred_element_type=F32)
        row_ref[:, k * block : (k + 1) * block] = jnp.sum(sums, axis=0, keepdims=True)


def streams_of(shape):
    return [pl.BlockSpec(shape, functools.partial(lambda k, i: (STREAMS * i + k, 0), k)) for k in range(STREAMS)]


def row_pass(columns, expo, count):
    rows, protos = expo.shape
    block = rows // 8
    return pl.pallas_call(
        functools.partial(row_kernel, count, len(columns)),
        grid=(rows // block // STREAMS,),
        in_specs=[pl.BlockSpec((1, protos), lambda i: (0, 0)) for _ in columns] + streams_of((block, protos)),
        out_specs=pl.BlockSpec((1, STREAMS * block), lambda i: (0, i)),
        out_shape=jax.ShapeDtypeStruct((1, rows), F32),
        compiler_params=params(8),
        cost_estimate=cost(2 * rows * protos, 4 * MIB),
        name="row_pass",
    )(*columns, *[in_vmem(expo)] * STREAMS)


def column_kernel(count, parts, *refs):
    row_refs, expo_refs, column_ref = refs[:parts], refs[parts:-1], refs[-1]
    step = pl.program_id(0)
    scale = split_rows(1.0 / (count * total_of(row_refs)))
    block = expo_refs[0].shape[0]
    total = None
    for k, expo_ref in enumerate(expo_refs):
        sums = lax.dot_general(
            scale[:, k * block : (k + 1) * block], expo_ref[...], (((1,), (0,)), ((), ())), preferred_element_type=F32
        )
        total = sums if total is None else total + sums
    total = jnp.sum(total, axis=0, keepdims=True)

    @pl.when(step == 0)
    def _():
        column_ref[...] = total

    @pl.when(step > 0)
    def _():
        column_ref[...] += total


def column_pass(row_totals, expo, count):
    rows, protos = expo.shape
    block = rows // 8
    return pl.pallas_call(
        functools.partial(column_kernel, count, len(row_totals)),
        grid=(rows // block // STREAMS,),
        in_specs=[pl.BlockSpec((1, STREAMS * block), lambda i: (0, i)) for _ in row_totals]
        + streams_of((block, protos)),
        out_specs=pl.BlockSpec((1, protos), lambda i: (0, 0)),
        out_shape=jax.ShapeDtypeStruct((1, protos), F32),
        compiler_params=params(8),
        cost_estimate=cost(2 * rows * protos, 4 * MIB),
        name="column_pass",
    )(*row_totals, *[in_vmem(expo)] * STREAMS)


def partner_kernel(first_ref, second_ref, source_ref, wnorm_ref, first_expo_ref, second_expo_ref, table_ref, semaphores, *stages):
    step = pl.program_id(0)
    groups = table_ref.shape[1]

    @pl.when(step == 0)
    def _():
        parts = semaphores.shape[0]
        size = source_ref.shape[0] // parts
        copies = [
            pltpu.make_async_copy(
                source_ref.at[pl.ds(k * size, size)], table_ref.at[pl.ds(k * size, size)], semaphores.at[k]
            )
            for k in range(parts)
        ]
        for copy in copies:
            copy.start()
        for copy in copies:
            copy.wait()

    rows = first_expo_ref.shape[0]
    wnorm = wnorm_ref[...]
    chunks = [
        (which_ref, out_ref, start)
        for start in range(0, rows, CHUNK)
        for which_ref, out_ref in ((first_ref, first_expo_ref), (second_ref, second_expo_ref))
    ]
    for number, (which_ref, out_ref, start) in enumerate(chunks):
        stage_ref = stages[number % 2]
        for row in range(CHUNK):
            place = which_ref[step * rows + start + row]
            stage_ref[row * groups : (row + 1) * groups, :] = table_ref[place].astype(F32)
        unit = jnp.concatenate(
            [stage_ref[pl.ds(k, CHUNK, stride=groups), :].astype(BF16) for k in range(groups)], axis=1
        )
        scores = lax.dot_general(unit, wnorm, (((1,), (1,)), ((), ())), preferred_element_type=F32)
        soft = jnp.exp(scores * (1.0 / SOFTMAX_HEAT))
        out_ref[start : start + CHUNK, :] = (soft * soft).astype(out_ref.dtype)


def partner_pass(first, second, table, wnorm):
    rows = first.shape[0]
    protos, columns = wnorm.shape
    groups = columns // LANES
    block = 2 * CHUNK
    return pl.pallas_call(
        partner_kernel,
        grid_spec=pltpu.PrefetchScalarGridSpec(
            num_scalar_prefetch=2,
            grid=(rows // block,),
            in_specs=[
                pl.BlockSpec(memory_space=pl.ANY),
                pl.BlockSpec((protos, columns), lambda i, *_: (0, 0), pipeline_mode=pl.Buffered(1)),
            ],
            out_specs=[
                pl.BlockSpec((block, protos), lambda i, *_: (i, 0)),
                pl.BlockSpec((block, protos), lambda i, *_: (i, 0)),
            ],
            scratch_shapes=[
                pltpu.VMEM(table.shape, BF16),
                pltpu.SemaphoreType.DMA((STREAMS,)),
            ]
            + [pltpu.VMEM((CHUNK * groups, LANES), F32)] * 2,
        ),
        out_shape=[jax.ShapeDtypeStruct((rows, protos), BF16)] * 2,
        compiler_params=params(40),
        cost_estimate=cost(4 * rows * columns * protos, 28 * MIB, 2 * rows * protos),
        name="partner_scores",
    )(first, second, table, wnorm)


def lookup_kernel(first_ref, second_ref, totals_ref, out_ref):
    rows = first_ref.shape[0]
    for number, which_ref in enumerate((first_ref, second_ref)):

        @pl.loop(0, rows // 16)
        def _(i):
            for j in range(16):
                row = i * 16 + j
                out_ref[number * rows + row] = totals_ref[which_ref[row]]


def lookup(first, second, totals):
    return pl.pallas_call(
        lookup_kernel,
        grid_spec=pltpu.PrefetchScalarGridSpec(
            num_scalar_prefetch=2,
            grid=(1,),
            in_specs=[pl.BlockSpec(memory_space=pltpu.SMEM)],
            out_specs=pl.BlockSpec(memory_space=pltpu.SMEM),
        ),
        out_shape=jax.ShapeDtypeStruct((2 * first.shape[0],), F32),
        compiler_params=params(8),
        cost_estimate=cost(MIB, MIB),
        name="lookup",
    )(first, second, totals)


def gradient_kernel(count, total, heat_scale, proto_size, parts, core_ref, *refs):
    del core_ref
    column_refs, row_refs = refs[: parts[0]], refs[parts[0] : parts[0] + parts[1]]
    first_ref, second_ref, scores_ref, wnorm_ref, gunit_ref, dscore_ref, loss_ref = refs[parts[0] + parts[1] :]
    step = pl.program_id(0)
    scale = 1.0 / (count * total_of(column_refs))
    totals = total_of(row_refs)
    share = totals.shape[-1]
    place = lax.broadcasted_iota(jnp.int32, (8, share), 0)
    loss = jnp.zeros((), F32)
    for group in range(totals.shape[0]):
        row_totals, zsum = totals[group, 0:2], totals[group, 2:3]
        weights = total * (1.0 / (total * row_totals))
        code_totals = 0.5 * jnp.sum(weights * row_totals, axis=0, keepdims=True)
        log_part = jnp.sum(code_totals * jnp.log(zsum)) * (1.0 / proto_size)
        stacked = jnp.where(
            place == 0,
            weights[0:1],
            jnp.where(place == 1, weights[1:2], jnp.where(place == 2, code_totals / zsum, 0.0)),
        ).T
        first = (stacked[:, 0:1] * first_ref[group].astype(F32) * scale).astype(BF16).astype(F32)
        second = (stacked[:, 1:2] * second_ref[group].astype(F32) * scale).astype(BF16).astype(F32)
        targets = 0.5 * (first + second)
        heated = scores_ref[group] * (1.0 / SOFTMAX_HEAT)
        loss = loss + (log_part - jnp.sum(targets * heated))
        dscore = ((jnp.exp(heated) * stacked[:, 2:3] - targets) * heat_scale).astype(BF16)
        dscore_ref[group] = dscore
        gunit = jnp.dot(dscore, wnorm_ref[...], preferred_element_type=F32)
        gunit_ref[group] = gunit.astype(gunit_ref.dtype)

    @pl.when(step == 0)
    def _():
        loss_ref[...] = jnp.full(loss_ref.shape, loss, F32)

    @pl.when(step > 0)
    def _():
        loss_ref[...] += loss


def gradients(where, columns, row_totals, first, second, scores, wnorm, count, total, proto_size, dtype):
    rows, protos = first.shape
    width = wnorm.shape[1]
    heat_scale = count / (32.0 * SOFTMAX_HEAT)
    _, places, _, share = row_totals[0].shape
    top = places // 4
    at = pl.BlockSpec((1, None, None, None, share, protos), lambda i, where: (i, where[0], where[1], where[2], 0, 0))
    first, second, scores = [value.reshape(top, 2, 2, 2, share, protos) for value in (first, second, scores)]
    row_totals = [value.reshape(2, top, 2, 2, 3, share) for value in row_totals]
    return pl.pallas_call(
        functools.partial(
            gradient_kernel, count, total, heat_scale, proto_size, (len(columns), len(row_totals))
        ),
        grid_spec=pltpu.PrefetchScalarGridSpec(
            num_scalar_prefetch=1,
            grid=(top,),
            in_specs=[pl.BlockSpec((1, protos), lambda i, where: (0, 0)) for _ in columns]
            + [
                pl.BlockSpec(
                    (None, 1, None, None, 3, share), lambda i, where: (where[2], i, where[0], where[1], 0, 0)
                )
                for _ in row_totals
            ]
            + [at, at, at, pl.BlockSpec((protos, width), lambda i, where: (0, 0), pipeline_mode=pl.Buffered(1))],
            out_specs=[
                pl.BlockSpec((1, share, width), lambda i, where: (i, 0, 0)),
                pl.BlockSpec((1, share, protos), lambda i, where: (i, 0, 0)),
                pl.BlockSpec((1, LANES), lambda i, where: (0, 0)),
            ],
        ),
        out_shape=[
            jax.ShapeDtypeStruct((top, share, width), dtype),
            jax.ShapeDtypeStruct((top, share, protos), BF16),
            jax.ShapeDtypeStruct((1, LANES), F32),
        ],
        compiler_params=params(44),
        cost_estimate=cost(MIB, MIB),
        name="gradients",
    )(where, *columns, *row_totals, in_vmem(first), in_vmem(second), scores, in_vmem(wnorm))


def add_kernel(*refs):
    total = refs[0][...]
    for ref in refs[1:-1]:
        total = total + ref[...].astype(F32)
    refs[-1][...] = total.astype(refs[-1].dtype)


def add_blocks(values, dtype):
    count, share, width = values[0].shape
    at = pl.BlockSpec((1, share, width), lambda i: (i, 0, 0))
    return pl.pallas_call(
        add_kernel,
        grid=(count,),
        in_specs=[at for _ in values],
        out_specs=at,
        out_shape=jax.ShapeDtypeStruct(values[0].shape, dtype),
        compiler_params=params(12),
        cost_estimate=cost(count * share * width, 8 * count * share * width),
        name="add_blocks",
    )(*values)


def combine_kernel(parts, bit_ref, *refs):
    del bit_ref
    own_refs, other_refs, (own_ref, sent_ref) = refs[:parts], refs[parts : 2 * parts], refs[2 * parts :]
    add_kernel(*other_refs, sent_ref)
    add_kernel(*own_refs, own_ref)


def combine(bit, values):
    count, share, width = values[0].shape
    values = [value.reshape(count // 2, 2, share, width) for value in values]
    own_at = pl.BlockSpec((None, None, share, width), lambda i, bit: (i, bit[0], 0, 0))
    other_at = pl.BlockSpec((None, None, share, width), lambda i, bit: (i, 1 - bit[0], 0, 0))
    out_at = pl.BlockSpec((None, share, width), lambda i, bit: (i, 0, 0))
    return pl.pallas_call(
        functools.partial(combine_kernel, len(values)),
        grid_spec=pltpu.PrefetchScalarGridSpec(
            num_scalar_prefetch=1,
            grid=(count // 2,),
            in_specs=[own_at] * len(values) + [other_at] * len(values),
            out_specs=[out_at, out_at],
        ),
        out_shape=[
            jax.ShapeDtypeStruct((count // 2, share, width), F32),
            jax.ShapeDtypeStruct((count // 2, share, width), BF16),
        ],
        compiler_params=params(16),
        cost_estimate=cost(count * share * width, 9 * count * share * width),
        name="combine",
    )(bit, *values, *values)


def proto_gradient_kernel(index_ref, *refs):
    del index_ref
    dscore_refs, unit_refs, own_ref, sent_ref = refs[:8], refs[8:16], refs[16], refs[17]
    both = (((0,), (0,)), ((), ()))
    total = None
    for dscore_ref, unit_ref in zip(dscore_refs, unit_refs):
        rows, part = dscore_ref.shape[0], unit_ref.shape[-1]
        term = lax.dot_general(
            dscore_ref[...], unit_ref[...].reshape(rows, part), both, preferred_element_type=F32
        )
        total = term if total is None else total + term
    sent_ref[...] = total.astype(BF16)
    own_ref[...] = total


def proto_gradient(index, dscores, unit, batch_size):
    top, share, protos = dscores[0].shape
    width = unit.shape[1]
    part = width // batch_size
    rows = top * share
    last = batch_size - 1
    unit = unit.reshape(top, 2, 2, 2, share, width)
    dscore_at = pl.BlockSpec((rows, protos), lambda i, index: (0, 0), pipeline_mode=pl.Buffered(1))

    def unit_at(number):
        return pl.BlockSpec(
            (top, None, None, None, share, part),
            lambda i, index: (
                0, index[1] ^ (number >> 2), index[2] ^ (number >> 1 & 1), index[3] ^ (number & 1), 0, index[0] ^ (last - i),
            ),
        )

    return pl.pallas_call(
        proto_gradient_kernel,
        grid_spec=pltpu.PrefetchScalarGridSpec(
            num_scalar_prefetch=1,
            grid=(batch_size,),
            in_specs=[dscore_at] * 8 + [unit_at(number) for number in range(8)],
            out_specs=[
                pl.BlockSpec((protos, part), lambda i, index: (0, 0)),
                pl.BlockSpec((None, protos, part), lambda i, index: (last - i, 0, 0)),
            ],
        ),
        out_shape=[
            jax.ShapeDtypeStruct((protos, part), F32),
            jax.ShapeDtypeStruct((batch_size, protos, part), BF16),
        ],
        compiler_params=params(20),
        cost_estimate=cost(MIB, MIB),
        name="proto_gradient",
    )(index, *[in_vmem(dscore.reshape(rows, protos)) for dscore in dscores], *[unit] * 8)


def embed_gradient_kernel(index_ref, embeddings_ref, *refs):
    del index_ref
    *part_refs, out_ref = refs
    gunit = part_refs[0][...]
    for ref in part_refs[1:]:
        gunit = gunit + ref[...].astype(F32)
    hidden = embeddings_ref[...].astype(F32)
    inverse = 1.0 / jnp.sqrt(jnp.sum(hidden * hidden, axis=1, keepdims=True) + NORM_EPSILON)
    along = jnp.sum(hidden * gunit, axis=1, keepdims=True)
    out_ref[...] = inverse * gunit - hidden * (inverse * inverse * inverse * along)


def embed_gradient(index, embeddings, values):
    share, width = values[0].shape
    whole = pl.BlockSpec((share, width), lambda i, index: (0, 0))
    return pl.pallas_call(
        embed_gradient_kernel,
        grid_spec=pltpu.PrefetchScalarGridSpec(
            num_scalar_prefetch=1,
            grid=(1,),
            in_specs=[pl.BlockSpec((share, width), lambda i, index: (index[0], 0))] + [whole for _ in values],
            out_specs=whole,
        ),
        out_shape=jax.ShapeDtypeStruct((share, width), F32),
        compiler_params=params(60),
        cost_estimate=cost(8 * share * width, 4 * MIB),
        name="embed_gradient",
    )(index, embeddings, *values)


PLACE = ("top", "middle", "low")


def swap(value, axis, distance):
    size = lax.axis_size(axis)
    return lax.ppermute(value, axis, [(i, i ^ distance) for i in range(size)])


def parts_of(value, axis):
    size = lax.axis_size(axis)
    if size > 4:
        return [lax.psum(value, axis)]
    return [value] + [swap(value, axis, distance) for distance in range(1, size)]


def proto_parts_of(value):
    return parts_of(value + swap(value, "core", 1), PLACE)


def scalar(value):
    return jnp.full((1,), value, jnp.int32)


def on_device(embeddings, prototypes, partners):
    row_count, width = embeddings.shape
    proto_count = prototypes.shape[0]
    batch_size = lax.axis_size("batch")
    places = lax.axis_size(PLACE)
    proto_size = 2 * places
    total_rows = row_count * batch_size
    centroids = proto_count * proto_size
    share = row_count // proto_size
    batch_index = lax.axis_index("batch")
    low = lax.axis_index("low")
    middle = lax.axis_index("middle")
    place = lax.axis_index(PLACE)
    core = lax.axis_index("core")
    proto_index = 2 * place + core

    quarter = row_count // 4
    steps = quarter // OWN_BLOCK
    own = own_rows(embeddings, scalar((2 * low + core) * steps), OWN_BLOCK, steps)
    table = lax.all_gather(own, ("batch", "low", "core"), axis=0, tiled=True)

    unit, wnorm, scores, expo, zsum, columns = scores_of(embeddings, prototypes, share)
    columns = parts_of(columns, "batch")
    for iteration in range(ITERS - 1):
        row_totals = proto_parts_of(row_pass(columns, expo, centroids))
        columns = parts_of(column_pass(row_totals, expo, total_rows), "batch")

    row_part = row_pass(columns, expo, centroids)
    row_totals = functools.reduce(jnp.add, proto_parts_of(jnp.concatenate([row_part, zsum], axis=0)))
    own_totals, zsum = row_totals[0], row_totals[1]
    all_totals = jnp.concatenate([own_totals] + [swap(own_totals, "batch", distance) for distance in range(1, batch_size)])
    away = (partners // row_count ^ batch_index) * row_count + partners % row_count
    partner_totals = lookup(away[:, 0], away[:, 1], all_totals).reshape(2, row_count)
    row_totals = jnp.concatenate([partner_totals, zsum[None]], axis=0)
    row_totals = [row_totals.reshape(3, places, 2, share).transpose(2, 1, 0, 3)]

    first, second = partner_pass(partners[:, 0], partners[:, 1], table, wnorm)
    others = (scores, wnorm, centroids, total_rows, proto_size)

    def after(value, *earlier):
        return lax.optimization_barrier((value, *earlier))[0]

    losses, dscores = [], {}

    def part_of(number, *earlier):
        place_bits = [middle ^ (number >> 1), low ^ (number & 1)]

        def run(other, dtype):
            where = after(jnp.stack(place_bits + [core ^ other]).astype(jnp.int32), *earlier)
            gunit, dscores[2 * number + other], loss = gradients(
                where, columns, row_totals, first, second, *others, dtype
            )
            losses.append(loss)
            return gunit

        gunit = run(1, BF16)
        return [run(0, F32), swap(gunit, "core", 1)]

    forwarded = add_blocks(part_of(3), BF16)
    from_forwarder = swap(forwarded, PLACE, 1)
    near = add_blocks(part_of(1, forwarded), BF16)
    from_near = swap(near, PLACE, 1)
    across = part_of(2, near)
    values = part_of(0, near)

    loss = functools.reduce(jnp.add, losses)
    loss = functools.reduce(jnp.add, parts_of(loss, "batch"))
    index = jnp.stack([batch_index, middle, low, core]).astype(jnp.int32)
    grad_proto, proto_sent = proto_gradient(index, [dscores[number] for number in range(8)], unit, batch_size)
    from_forwarder = after(from_forwarder, proto_sent)
    across = add_blocks(across + [from_forwarder], BF16)
    values += [from_near, swap(across, PLACE, 2)]
    proto_sent = after(proto_sent, loss, across, from_near)

    bit = 2
    while (1 << bit) < places:
        kept, sent = combine(scalar((place >> bit) % 2), values)
        values = [kept, swap(sent, PLACE, 1 << bit)]
        bit += 1
    grad_embed = embed_gradient(scalar(proto_index), embeddings, [value[0] for value in values])
    loss = loss + swap(loss, "core", 1)
    arrived = [swap(proto_sent[distance], "batch", distance) for distance in range(batch_size - 1, 0, -1)]
    loss = functools.reduce(jnp.add, parts_of(after(loss, *arrived), PLACE))
    loss = loss[0, 0] / total_rows
    for block in arrived:
        grad_proto = grad_proto + block.astype(F32)

    return (loss, grad_proto, grad_embed)


def solution(mesh):
    batch_size, proto_size = mesh.shape["batch"], mesh.shape["proto"]
    devices = mesh.devices.reshape(batch_size, proto_size // 8, 2, 2, 2)
    proto = PLACE + ("core",)
    return jax.shard_map(
        on_device,
        mesh=jax.sharding.Mesh(devices, ("batch",) + proto),
        in_specs=(P("batch", None), P(proto, None), P("batch", None)),
        out_specs=(P(), P(proto, "batch"), P(("batch",) + proto, None)),
        check_vma=False,
    )
```

```python
import functools

import jax
import jax.numpy as jnp
from jax import lax
from jax.experimental import pallas as pl
from jax.experimental.pallas import tpu as pltpu
from jax.sharding import PartitionSpec as P

ITERS = 3
BALANCE_SMOOTHING = 0.05
SOFTMAX_HEAT = 0.1
NORM_EPSILON = 1e-06
LANES = 128
CHUNK = 256
STREAMS = 4
OWN_BLOCK = 256
MIB = 1 << 20
F32 = jnp.float32
BF16 = jnp.bfloat16


def params(mib=60):
    return pltpu.CompilerParams(vmem_limit_bytes=mib * MIB)


def in_vmem(value):
    return pltpu.with_memory_space_constraint(value, pltpu.VMEM)


def cost(flops, moved, exps=0):
    return pl.CostEstimate(flops=flops, bytes_accessed=moved, transcendentals=exps)


def normalized(block):
    wide = block.astype(F32)
    inverse = 1.0 / jnp.sqrt(jnp.sum(wide * wide, axis=1, keepdims=True) + NORM_EPSILON)
    return wide * inverse


def lane_row_sums(values):
    columns = values.shape[1]
    part = values[:, 0:LANES]
    for start in range(LANES, columns, LANES):
        part = part + values[:, start : start + LANES]
    return jnp.sum(part.T, axis=0, keepdims=True)


def split_rows(row):
    high = row.astype(BF16).astype(F32)
    middle = (row - high).astype(BF16).astype(F32)
    low = row - high - middle
    place = lax.broadcasted_iota(jnp.int32, (16, row.shape[1]), 0)
    stacked = jnp.where(place == 0, high, jnp.where(place == 1, middle, jnp.where(place == 2, low, 0.0)))
    return stacked.astype(BF16)


def total_of(refs):
    total = refs[0][...]
    for ref in refs[1:]:
        total = total + ref[...]
    return total


def own_rows_kernel(index_ref, embeddings_ref, table_ref, stage_ref):
    del index_ref
    rows, columns = embeddings_ref.shape
    unit = normalized(embeddings_ref[...]).astype(BF16).astype(F32)
    groups = columns // LANES
    for k in range(groups):
        stage_ref[pl.ds(k, rows, stride=groups), :] = unit[:, k * LANES : (k + 1) * LANES]
    table_ref[...] = stage_ref[...].reshape(rows, groups, LANES).astype(BF16)


def own_rows(embeddings, index, block, count):
    columns = embeddings.shape[1]
    groups = columns // LANES
    return pl.pallas_call(
        own_rows_kernel,
        grid_spec=pltpu.PrefetchScalarGridSpec(
            num_scalar_prefetch=1,
            grid=(count,),
            in_specs=[pl.BlockSpec((block, columns), lambda i, index: (index[0] + i, 0))],
            out_specs=pl.BlockSpec((block, groups, LANES), lambda i, index: (i, 0, 0)),
            scratch_shapes=[pltpu.VMEM((block * groups, LANES), F32)],
        ),
        out_shape=jax.ShapeDtypeStruct((block * count, groups, LANES), BF16),
        compiler_params=params(60),
        name="own_rows",
    )(index, embeddings)


def scores_kernel(embeddings_ref, prototypes_ref, unit_ref, wnorm_ref, scores_ref, expo_ref, zsum_ref, column_ref):
    step = pl.program_id(0)

    @pl.when(step == 0)
    def _():
        wnorm_ref[...] = normalized(prototypes_ref[...]).astype(BF16)

    share = embeddings_ref.shape[0] // 2
    sums = None
    for k in range(2):
        at = slice(k * share, (k + 1) * share)
        unit = normalized(embeddings_ref[at]).astype(BF16)
        unit_ref[at] = unit
        scores = lax.dot_general(unit, wnorm_ref[...], (((1,), (1,)), ((), ())), preferred_element_type=F32)
        scores_ref[at] = scores
        soft = jnp.exp(scores * (1.0 / SOFTMAX_HEAT))
        zsum_ref[:, at] = lane_row_sums(soft)
        expo = soft * soft
        expo_ref[at] = expo.astype(BF16)
        part = jnp.sum(expo, axis=0, keepdims=True)
        sums = part if sums is None else sums + part

    @pl.when(step == 0)
    def _():
        column_ref[...] = sums

    @pl.when(step > 0)
    def _():
        column_ref[...] += sums


def scores_of(embeddings, prototypes, share):
    rows, columns = embeddings.shape
    protos = prototypes.shape[0]
    return pl.pallas_call(
        scores_kernel,
        grid=(rows // share // 2,),
        in_specs=[
            pl.BlockSpec((2 * share, columns), lambda i: (i, 0)),
            pl.BlockSpec((protos, columns), lambda i: (0, 0), pipeline_mode=pl.Buffered(1)),
        ],
        out_specs=[
            pl.BlockSpec((2 * share, columns), lambda i: (i, 0)),
            pl.BlockSpec((protos, columns), lambda i: (0, 0)),
            pl.BlockSpec((2 * share, protos), lambda i: (i, 0)),
            pl.BlockSpec((2 * share, protos), lambda i: (i, 0)),
            pl.BlockSpec((1, 2 * share), lambda i: (0, i)),
            pl.BlockSpec((1, protos), lambda i: (0, 0)),
        ],
        out_shape=[
            jax.ShapeDtypeStruct((rows, columns), BF16),
            jax.ShapeDtypeStruct((protos, columns), BF16),
            jax.ShapeDtypeStruct((rows, protos), F32),
            jax.ShapeDtypeStruct((rows, protos), BF16),
            jax.ShapeDtypeStruct((1, rows), F32),
            jax.ShapeDtypeStruct((1, protos), F32),
        ],
        compiler_params=params(28),
        cost_estimate=cost(2 * rows * columns * protos, 22 * MIB, rows * protos),
        name="scores",
    )(embeddings, prototypes)


def row_kernel(count, parts, *refs):
    column_refs, expo_refs, row_ref = refs[:parts], refs[parts:-1], refs[-1]
    scale = split_rows(1.0 / (count * total_of(column_refs)))
    block = expo_refs[0].shape[0]
    for k, expo_ref in enumerate(expo_refs):
        sums = lax.dot_general(scale, expo_ref[...], (((1,), (1,)), ((), ())), preferred_element_type=F32)
        row_ref[:, k * block : (k + 1) * block] = jnp.sum(sums, axis=0, keepdims=True)


def streams_of(shape):
    return [pl.BlockSpec(shape, functools.partial(lambda k, i: (STREAMS * i + k, 0), k)) for k in range(STREAMS)]


def row_pass(columns, expo, count):
    rows, protos = expo.shape
    block = rows // 8
    return pl.pallas_call(
        functools.partial(row_kernel, count, len(columns)),
        grid=(rows // block // STREAMS,),
        in_specs=[pl.BlockSpec((1, protos), lambda i: (0, 0)) for _ in columns] + streams_of((block, protos)),
        out_specs=pl.BlockSpec((1, STREAMS * block), lambda i: (0, i)),
        out_shape=jax.ShapeDtypeStruct((1, rows), F32),
        compiler_params=params(8),
        cost_estimate=cost(2 * rows * protos, 4 * MIB),
        name="row_pass",
    )(*columns, *[in_vmem(expo)] * STREAMS)


def column_kernel(count, parts, *refs):
    row_refs, expo_refs, column_ref = refs[:parts], refs[parts:-1], refs[-1]
    step = pl.program_id(0)
    scale = split_rows(1.0 / (count * total_of(row_refs)))
    block = expo_refs[0].shape[0]
    total = None
    for k, expo_ref in enumerate(expo_refs):
        sums = lax.dot_general(
            scale[:, k * block : (k + 1) * block], expo_ref[...], (((1,), (0,)), ((), ())), preferred_element_type=F32
        )
        total = sums if total is None else total + sums
    total = jnp.sum(total, axis=0, keepdims=True)

    @pl.when(step == 0)
    def _():
        column_ref[...] = total

    @pl.when(step > 0)
    def _():
        column_ref[...] += total


def column_pass(row_totals, expo, count):
    rows, protos = expo.shape
    block = rows // 8
    return pl.pallas_call(
        functools.partial(column_kernel, count, len(row_totals)),
        grid=(rows // block // STREAMS,),
        in_specs=[pl.BlockSpec((1, STREAMS * block), lambda i: (0, i)) for _ in row_totals]
        + streams_of((block, protos)),
        out_specs=pl.BlockSpec((1, protos), lambda i: (0, 0)),
        out_shape=jax.ShapeDtypeStruct((1, protos), F32),
        compiler_params=params(8),
        cost_estimate=cost(2 * rows * protos, 4 * MIB),
        name="column_pass",
    )(*row_totals, *[in_vmem(expo)] * STREAMS)


def partner_kernel(count, total, heat_scale, proto_size, parts, first_ref, second_ref, *refs):
    column_refs = refs[:parts]
    totals_ref, source_ref, wnorm_ref, scores_ref, dscore_ref, loss_ref, table_ref, semaphores, *stages = refs[parts:]
    step = pl.program_id(0)
    groups = table_ref.shape[1]

    @pl.when(step == 0)
    def _():
        parts = semaphores.shape[0]
        size = source_ref.shape[0] // parts
        copies = [
            pltpu.make_async_copy(
                source_ref.at[pl.ds(k * size, size)], table_ref.at[pl.ds(k * size, size)], semaphores.at[k]
            )
            for k in range(parts)
        ]
        for copy in copies:
            copy.start()
        for copy in copies:
            copy.wait()

    rows = dscore_ref.shape[0]
    wnorm = wnorm_ref[...]
    scale = 1.0 / (count * total_of(column_refs))
    place_in = lax.broadcasted_iota(jnp.int32, (8, CHUNK), 0)
    loss = jnp.zeros((), F32)
    for start in range(0, rows, CHUNK):
        at = slice(start, start + CHUNK)
        row_totals, zsum = totals_ref[0:2, at], totals_ref[2:3, at]
        weights = total * (1.0 / (total * row_totals))
        code_totals = 0.5 * jnp.sum(weights * row_totals, axis=0, keepdims=True)
        log_part = jnp.sum(code_totals * jnp.log(zsum)) * (1.0 / proto_size)
        stacked = jnp.where(
            place_in == 0,
            weights[0:1],
            jnp.where(place_in == 1, weights[1:2], jnp.where(place_in == 2, code_totals / zsum, 0.0)),
        ).T
        codes = []
        for number, which_ref in enumerate((first_ref, second_ref)):
            stage_ref = stages[number]
            for row in range(CHUNK):
                place = which_ref[step * rows + start + row]
                stage_ref[row * groups : (row + 1) * groups, :] = table_ref[place].astype(F32)
            unit = jnp.concatenate(
                [stage_ref[pl.ds(k, CHUNK, stride=groups), :].astype(BF16) for k in range(groups)], axis=1
            )
            scores = lax.dot_general(unit, wnorm, (((1,), (1,)), ((), ())), preferred_element_type=F32)
            soft = jnp.exp(scores * (1.0 / SOFTMAX_HEAT))
            expo = soft * soft
            codes.append((stacked[:, number : number + 1] * expo * scale).astype(BF16).astype(F32))
        targets = 0.5 * (codes[0] + codes[1])
        heated = scores_ref[at] * (1.0 / SOFTMAX_HEAT)
        loss = loss + (log_part - jnp.sum(targets * heated))
        dscore_ref[at] = ((jnp.exp(heated) * stacked[:, 2:3] - targets) * heat_scale).astype(BF16)

    @pl.when(step == 0)
    def _():
        loss_ref[...] = jnp.full(loss_ref.shape, loss, F32)

    @pl.when(step > 0)
    def _():
        loss_ref[...] += loss


def partner_pass(first, second, columns, totals, table, wnorm, scores, count, total, proto_size):
    rows = first.shape[0]
    protos, columns_of_table = wnorm.shape
    groups = columns_of_table // LANES
    block = 2 * CHUNK
    heat_scale = count / (32.0 * SOFTMAX_HEAT)
    return pl.pallas_call(
        functools.partial(partner_kernel, count, total, heat_scale, proto_size, len(columns)),
        grid_spec=pltpu.PrefetchScalarGridSpec(
            num_scalar_prefetch=2,
            grid=(rows // block,),
            in_specs=[pl.BlockSpec((1, protos), lambda i, *_: (0, 0)) for _ in columns]
            + [
                pl.BlockSpec((3, block), lambda i, *_: (0, i)),
                pl.BlockSpec(memory_space=pl.ANY),
                pl.BlockSpec(wnorm.shape, lambda i, *_: (0, 0), pipeline_mode=pl.Buffered(1)),
                pl.BlockSpec((block, protos), lambda i, *_: (i, 0)),
            ],
            out_specs=[
                pl.BlockSpec((block, protos), lambda i, *_: (i, 0)),
                pl.BlockSpec((1, LANES), lambda i, *_: (0, 0)),
            ],
            scratch_shapes=[
                pltpu.VMEM(table.shape, BF16),
                pltpu.SemaphoreType.DMA((STREAMS,)),
            ]
            + [pltpu.VMEM((CHUNK * groups, LANES), F32)] * 2,
        ),
        out_shape=[jax.ShapeDtypeStruct((rows, protos), BF16), jax.ShapeDtypeStruct((1, LANES), F32)],
        compiler_params=params(46),
        cost_estimate=cost(4 * rows * columns_of_table * protos, 32 * MIB, 3 * rows * protos),
        name="partner_scores",
    )(first, second, *columns, totals, table, wnorm, scores)


def lookup_kernel(first_ref, second_ref, totals_ref, out_ref):
    rows = first_ref.shape[0]
    for number, which_ref in enumerate((first_ref, second_ref)):

        @pl.loop(0, rows // 16)
        def _(i):
            for j in range(16):
                row = i * 16 + j
                out_ref[number * rows + row] = totals_ref[which_ref[row]]


def lookup(first, second, totals):
    return pl.pallas_call(
        lookup_kernel,
        grid_spec=pltpu.PrefetchScalarGridSpec(
            num_scalar_prefetch=2,
            grid=(1,),
            in_specs=[pl.BlockSpec(memory_space=pltpu.SMEM)],
            out_specs=pl.BlockSpec(memory_space=pltpu.SMEM),
        ),
        out_shape=jax.ShapeDtypeStruct((2 * first.shape[0],), F32),
        compiler_params=params(8),
        cost_estimate=cost(MIB, MIB),
        name="lookup",
    )(first, second, totals)


def gradient_kernel(where_ref, dscore_ref, wnorm_ref, gunit_ref):
    del where_ref
    gunit_ref[0] = jnp.dot(dscore_ref[0], wnorm_ref[...], preferred_element_type=F32).astype(gunit_ref.dtype)


def gradients(where, dscore, wnorm, dtype):
    top, share, protos = dscore.shape[0], *dscore.shape[4:]
    width = wnorm.shape[1]
    return pl.pallas_call(
        gradient_kernel,
        grid_spec=pltpu.PrefetchScalarGridSpec(
            num_scalar_prefetch=1,
            grid=(top,),
            in_specs=[
                pl.BlockSpec(
                    (1, None, None, None, share, protos), lambda i, where: (i, where[0], where[1], where[2], 0, 0)
                ),
                pl.BlockSpec((protos, width), lambda i, where: (0, 0), pipeline_mode=pl.Buffered(1)),
            ],
            out_specs=pl.BlockSpec((1, share, width), lambda i, where: (i, 0, 0)),
        ),
        out_shape=jax.ShapeDtypeStruct((top, share, width), dtype),
        compiler_params=params(16),
        cost_estimate=cost(MIB, MIB),
        name="gradients",
    )(where, in_vmem(dscore), in_vmem(wnorm))


def add_kernel(*refs):
    total = refs[0][...]
    for ref in refs[1:-1]:
        total = total + ref[...].astype(F32)
    refs[-1][...] = total.astype(refs[-1].dtype)


def add_blocks(values, dtype):
    count, share, width = values[0].shape
    at = pl.BlockSpec((1, share, width), lambda i: (i, 0, 0))
    return pl.pallas_call(
        add_kernel,
        grid=(count,),
        in_specs=[at for _ in values],
        out_specs=at,
        out_shape=jax.ShapeDtypeStruct(values[0].shape, dtype),
        compiler_params=params(12),
        cost_estimate=cost(count * share * width, 8 * count * share * width),
        name="add_blocks",
    )(*values)


def combine_kernel(parts, bit_ref, *refs):
    del bit_ref
    own_refs, other_refs, (own_ref, sent_ref) = refs[:parts], refs[parts : 2 * parts], refs[2 * parts :]
    add_kernel(*other_refs, sent_ref)
    add_kernel(*own_refs, own_ref)


def combine(bit, values):
    count, share, width = values[0].shape
    values = [value.reshape(count // 2, 2, share, width) for value in values]
    own_at = pl.BlockSpec((None, None, share, width), lambda i, bit: (i, bit[0], 0, 0))
    other_at = pl.BlockSpec((None, None, share, width), lambda i, bit: (i, 1 - bit[0], 0, 0))
    out_at = pl.BlockSpec((None, share, width), lambda i, bit: (i, 0, 0))
    return pl.pallas_call(
        functools.partial(combine_kernel, len(values)),
        grid_spec=pltpu.PrefetchScalarGridSpec(
            num_scalar_prefetch=1,
            grid=(count // 2,),
            in_specs=[own_at] * len(values) + [other_at] * len(values),
            out_specs=[out_at, out_at],
        ),
        out_shape=[
            jax.ShapeDtypeStruct((count // 2, share, width), F32),
            jax.ShapeDtypeStruct((count // 2, share, width), BF16),
        ],
        compiler_params=params(16),
        cost_estimate=cost(count * share * width, 9 * count * share * width),
        name="combine",
    )(bit, *values, *values)


def proto_gradient_kernel(index_ref, *refs):
    del index_ref
    dscore_refs, unit_refs, own_ref, sent_ref = refs[:8], refs[8:16], refs[16], refs[17]
    both = (((0,), (0,)), ((), ()))
    total = None
    for dscore_ref, unit_ref in zip(dscore_refs, unit_refs):
        rows, protos, part = dscore_ref.shape[0] * dscore_ref.shape[1], dscore_ref.shape[2], unit_ref.shape[-1]
        term = lax.dot_general(
            dscore_ref[...].reshape(rows, protos), unit_ref[...].reshape(rows, part), both, preferred_element_type=F32
        )
        total = term if total is None else total + term
    sent_ref[...] = total.astype(BF16)
    own_ref[...] = total


def proto_gradient(dscore, unit, index, batch_size):
    top, share, protos = dscore.shape[0], *dscore.shape[4:]
    width = unit.shape[1]
    part = width // batch_size
    rows = top * share
    last = batch_size - 1
    unit = unit.reshape(top, 2, 2, 2, share, width)

    def dscore_at(number):
        return pl.BlockSpec(
            (top, None, None, None, share, protos),
            lambda i, index: (0, number >> 2, number >> 1 & 1, number & 1, 0, 0),
            pipeline_mode=pl.Buffered(1),
        )

    def unit_at(number):
        return pl.BlockSpec(
            (top, None, None, None, share, part),
            lambda i, index: (
                0, number >> 2, number >> 1 & 1, number & 1, 0, index[0] ^ (last - i),
            ),
        )

    return pl.pallas_call(
        proto_gradient_kernel,
        grid_spec=pltpu.PrefetchScalarGridSpec(
            num_scalar_prefetch=1,
            grid=(batch_size,),
            in_specs=[dscore_at(number) for number in range(8)] + [unit_at(number) for number in range(8)],
            out_specs=[
                pl.BlockSpec((protos, part), lambda i, index: (0, 0)),
                pl.BlockSpec((None, protos, part), lambda i, index: (last - i, 0, 0)),
            ],
        ),
        out_shape=[
            jax.ShapeDtypeStruct((protos, part), F32),
            jax.ShapeDtypeStruct((batch_size, protos, part), BF16),
        ],
        compiler_params=params(20),
        cost_estimate=cost(MIB, MIB),
        name="proto_gradient",
    )(index, *[in_vmem(dscore)] * 8, *[unit] * 8)


def embed_gradient_kernel(index_ref, embeddings_ref, *refs):
    del index_ref
    *part_refs, out_ref = refs
    gunit = part_refs[0][...]
    for ref in part_refs[1:]:
        gunit = gunit + ref[...].astype(F32)
    hidden = embeddings_ref[...].astype(F32)
    inverse = 1.0 / jnp.sqrt(jnp.sum(hidden * hidden, axis=1, keepdims=True) + NORM_EPSILON)
    along = jnp.sum(hidden * gunit, axis=1, keepdims=True)
    out_ref[...] = inverse * gunit - hidden * (inverse * inverse * inverse * along)


def embed_gradient(index, embeddings, values):
    share, width = values[0].shape
    whole = pl.BlockSpec((share, width), lambda i, index: (0, 0))
    return pl.pallas_call(
        embed_gradient_kernel,
        grid_spec=pltpu.PrefetchScalarGridSpec(
            num_scalar_prefetch=1,
            grid=(1,),
            in_specs=[pl.BlockSpec((share, width), lambda i, index: (index[0], 0))] + [whole for _ in values],
            out_specs=whole,
        ),
        out_shape=jax.ShapeDtypeStruct((share, width), F32),
        compiler_params=params(60),
        cost_estimate=cost(8 * share * width, 4 * MIB),
        name="embed_gradient",
    )(index, embeddings, *values)


PLACE = ("top", "middle", "low")


def swap(value, axis, distance):
    size = lax.axis_size(axis)
    return lax.ppermute(value, axis, [(i, i ^ distance) for i in range(size)])


def parts_of(value, axis):
    size = lax.axis_size(axis)
    if size > 4:
        return [lax.psum(value, axis)]
    return [value] + [swap(value, axis, distance) for distance in range(1, size)]


def proto_parts_of(value):
    return parts_of(value + swap(value, "core", 1), PLACE)


def scalar(value):
    return jnp.full((1,), value, jnp.int32)


def on_device(embeddings, prototypes, partners):
    row_count, width = embeddings.shape
    proto_count = prototypes.shape[0]
    batch_size = lax.axis_size("batch")
    places = lax.axis_size(PLACE)
    proto_size = 2 * places
    total_rows = row_count * batch_size
    centroids = proto_count * proto_size
    share = row_count // proto_size
    batch_index = lax.axis_index("batch")
    low = lax.axis_index("low")
    middle = lax.axis_index("middle")
    place = lax.axis_index(PLACE)
    core = lax.axis_index("core")
    proto_index = 2 * place + core

    quarter = row_count // 4
    steps = quarter // OWN_BLOCK
    own = own_rows(embeddings, scalar((2 * low + core) * steps), OWN_BLOCK, steps)
    table = lax.all_gather(own, ("batch", "low", "core"), axis=0, tiled=True)

    unit, wnorm, scores, expo, zsum, columns = scores_of(embeddings, prototypes, share)
    columns = parts_of(columns, "batch")
    for iteration in range(ITERS - 1):
        row_totals = proto_parts_of(row_pass(columns, expo, centroids))
        columns = parts_of(column_pass(row_totals, expo, total_rows), "batch")

    row_part = row_pass(columns, expo, centroids)
    row_totals = functools.reduce(jnp.add, proto_parts_of(jnp.concatenate([row_part, zsum], axis=0)))
    own_totals, zsum = row_totals[0], row_totals[1]
    all_totals = jnp.concatenate([own_totals] + [swap(own_totals, "batch", distance) for distance in range(1, batch_size)])
    away = (partners // row_count ^ batch_index) * row_count + partners % row_count
    partner_totals = lookup(away[:, 0], away[:, 1], all_totals).reshape(2, row_count)
    row_totals = jnp.concatenate([partner_totals, zsum[None]], axis=0)
    dscore, loss = partner_pass(
        partners[:, 0], partners[:, 1], columns, row_totals, table, wnorm, scores, centroids, total_rows, proto_size
    )
    dscore = dscore.reshape(places // 4, 2, 2, 2, share, proto_count)

    def after(value, *earlier):
        return lax.optimization_barrier((value, *earlier))[0]

    def part_of(number, *earlier):
        place_bits = [middle ^ (number >> 1), low ^ (number & 1)]

        def run(other, dtype):
            where = after(jnp.stack(place_bits + [core ^ other]).astype(jnp.int32), *earlier)
            return gradients(where, dscore, wnorm, dtype)

        gunit = run(1, BF16)
        return [run(0, F32), swap(gunit, "core", 1)]

    forwarded = add_blocks(part_of(3), BF16)
    from_forwarder = swap(forwarded, PLACE, 1)
    near = add_blocks(part_of(1, forwarded), BF16)
    from_near = swap(near, PLACE, 1)
    across = part_of(2, near)
    values = part_of(0, near)

    loss = functools.reduce(jnp.add, parts_of(loss, "batch"))
    grad_proto, proto_sent = proto_gradient(dscore, unit, scalar(batch_index), batch_size)
    from_forwarder = after(from_forwarder, proto_sent)
    across = add_blocks(across + [from_forwarder], BF16)
    values += [from_near, swap(across, PLACE, 2)]
    proto_sent = after(proto_sent, loss, across, from_near)

    bit = 2
    while (1 << bit) < places:
        kept, sent = combine(scalar((place >> bit) % 2), values)
        values = [kept, swap(sent, PLACE, 1 << bit)]
        bit += 1
    grad_embed = embed_gradient(scalar(proto_index), embeddings, [value[0] for value in values])
    loss = loss + swap(loss, "core", 1)
    arrived = [swap(proto_sent[distance], "batch", distance) for distance in range(batch_size - 1, 0, -1)]
    loss = functools.reduce(jnp.add, parts_of(after(loss, *arrived), PLACE))
    loss = loss[0, 0] / total_rows
    for block in arrived:
        grad_proto = grad_proto + block.astype(F32)

    return (loss, grad_proto, grad_embed)


def solution(mesh):
    batch_size, proto_size = mesh.shape["batch"], mesh.shape["proto"]
    devices = mesh.devices.reshape(batch_size, proto_size // 8, 2, 2, 2)
    proto = PLACE + ("core",)
    return jax.shard_map(
        on_device,
        mesh=jax.sharding.Mesh(devices, ("batch",) + proto),
        in_specs=(P("batch", None), P(proto, None), P("batch", None)),
        out_specs=(P(), P(proto, "batch"), P(("batch",) + proto, None)),
        check_vma=False,
    )
```

```python
import functools

import jax
import jax.numpy as jnp
from jax import lax
from jax.experimental import pallas as pl
from jax.experimental.pallas import tpu as pltpu
from jax.sharding import PartitionSpec as P

ITERS = 3
BALANCE_SMOOTHING = 0.05
SOFTMAX_HEAT = 0.1
NORM_EPSILON = 1e-06
LANES = 128
CHUNK = 256
STREAMS = 4
OWN_BLOCK = 256
MIB = 1 << 20
F32 = jnp.float32
BF16 = jnp.bfloat16


def params(mib=60):
    return pltpu.CompilerParams(vmem_limit_bytes=mib * MIB)


def in_vmem(value):
    return pltpu.with_memory_space_constraint(value, pltpu.VMEM)


def cost(flops, moved, exps=0):
    return pl.CostEstimate(flops=flops, bytes_accessed=moved, transcendentals=exps)


def normalized(block):
    wide = block.astype(F32)
    inverse = 1.0 / jnp.sqrt(jnp.sum(wide * wide, axis=1, keepdims=True) + NORM_EPSILON)
    return wide * inverse


def lane_row_sums(values):
    columns = values.shape[1]
    part = values[:, 0:LANES]
    for start in range(LANES, columns, LANES):
        part = part + values[:, start : start + LANES]
    return jnp.sum(part.T, axis=0, keepdims=True)


def split_rows(row):
    high = row.astype(BF16).astype(F32)
    middle = (row - high).astype(BF16).astype(F32)
    low = row - high - middle
    place = lax.broadcasted_iota(jnp.int32, (16, row.shape[1]), 0)
    stacked = jnp.where(place == 0, high, jnp.where(place == 1, middle, jnp.where(place == 2, low, 0.0)))
    return stacked.astype(BF16)


def total_of(refs):
    total = refs[0][...]
    for ref in refs[1:]:
        total = total + ref[...]
    return total


def own_rows_kernel(index_ref, embeddings_ref, table_ref, stage_ref):
    del index_ref
    rows, columns = embeddings_ref.shape
    unit = normalized(embeddings_ref[...]).astype(BF16).astype(F32)
    groups = columns // LANES
    for k in range(groups):
        stage_ref[pl.ds(k, rows, stride=groups), :] = unit[:, k * LANES : (k + 1) * LANES]
    table_ref[...] = stage_ref[...].reshape(rows, groups, LANES).astype(BF16)


def own_rows(embeddings, index, block, count):
    columns = embeddings.shape[1]
    groups = columns // LANES
    return pl.pallas_call(
        own_rows_kernel,
        grid_spec=pltpu.PrefetchScalarGridSpec(
            num_scalar_prefetch=1,
            grid=(count,),
            in_specs=[pl.BlockSpec((block, columns), lambda i, index: (index[0] + i, 0))],
            out_specs=pl.BlockSpec((block, groups, LANES), lambda i, index: (i, 0, 0)),
            scratch_shapes=[pltpu.VMEM((block * groups, LANES), F32)],
        ),
        out_shape=jax.ShapeDtypeStruct((block * count, groups, LANES), BF16),
        compiler_params=params(60),
        name="own_rows",
    )(index, embeddings)


def scores_kernel(embeddings_ref, prototypes_ref, unit_ref, wnorm_ref, scores_ref, expo_ref, zsum_ref, column_ref):
    step = pl.program_id(0)

    @pl.when(step == 0)
    def _():
        wnorm_ref[...] = normalized(prototypes_ref[...]).astype(BF16)

    share = embeddings_ref.shape[0] // 2
    sums = None
    for k in range(2):
        at = slice(k * share, (k + 1) * share)
        unit = normalized(embeddings_ref[at]).astype(BF16)
        unit_ref[at] = unit
        scores = lax.dot_general(unit, wnorm_ref[...], (((1,), (1,)), ((), ())), preferred_element_type=F32)
        scores_ref[at] = scores
        soft = jnp.exp(scores * (1.0 / SOFTMAX_HEAT))
        zsum_ref[:, at] = lane_row_sums(soft)
        expo = soft * soft
        expo_ref[at] = expo.astype(BF16)
        part = jnp.sum(expo, axis=0, keepdims=True)
        sums = part if sums is None else sums + part

    @pl.when(step == 0)
    def _():
        column_ref[...] = sums

    @pl.when(step > 0)
    def _():
        column_ref[...] += sums


def scores_of(embeddings, prototypes, share):
    rows, columns = embeddings.shape
    protos = prototypes.shape[0]
    return pl.pallas_call(
        scores_kernel,
        grid=(rows // share // 2,),
        in_specs=[
            pl.BlockSpec((2 * share, columns), lambda i: (i, 0)),
            pl.BlockSpec((protos, columns), lambda i: (0, 0), pipeline_mode=pl.Buffered(1)),
        ],
        out_specs=[
            pl.BlockSpec((2 * share, columns), lambda i: (i, 0)),
            pl.BlockSpec((protos, columns), lambda i: (0, 0)),
            pl.BlockSpec((2 * share, protos), lambda i: (i, 0)),
            pl.BlockSpec((2 * share, protos), lambda i: (i, 0)),
            pl.BlockSpec((1, 2 * share), lambda i: (0, i)),
            pl.BlockSpec((1, protos), lambda i: (0, 0)),
        ],
        out_shape=[
            jax.ShapeDtypeStruct((rows, columns), BF16),
            jax.ShapeDtypeStruct((protos, columns), BF16),
            jax.ShapeDtypeStruct((rows, protos), F32),
            jax.ShapeDtypeStruct((rows, protos), BF16),
            jax.ShapeDtypeStruct((1, rows), F32),
            jax.ShapeDtypeStruct((1, protos), F32),
        ],
        compiler_params=params(28),
        cost_estimate=cost(2 * rows * columns * protos, 22 * MIB, rows * protos),
        name="scores",
    )(embeddings, prototypes)


def row_kernel(count, parts, *refs):
    column_refs, expo_refs, row_ref = refs[:parts], refs[parts:-1], refs[-1]
    scale = split_rows(1.0 / (count * total_of(column_refs)))
    block = expo_refs[0].shape[0]
    for k, expo_ref in enumerate(expo_refs):
        sums = lax.dot_general(scale, expo_ref[...], (((1,), (1,)), ((), ())), preferred_element_type=F32)
        row_ref[:, k * block : (k + 1) * block] = jnp.sum(sums, axis=0, keepdims=True)


def streams_of(shape):
    return [pl.BlockSpec(shape, functools.partial(lambda k, i: (STREAMS * i + k, 0), k)) for k in range(STREAMS)]


def row_pass(columns, expo, count):
    rows, protos = expo.shape
    block = rows // 8
    return pl.pallas_call(
        functools.partial(row_kernel, count, len(columns)),
        grid=(rows // block // STREAMS,),
        in_specs=[pl.BlockSpec((1, protos), lambda i: (0, 0)) for _ in columns] + streams_of((block, protos)),
        out_specs=pl.BlockSpec((1, STREAMS * block), lambda i: (0, i)),
        out_shape=jax.ShapeDtypeStruct((1, rows), F32),
        compiler_params=params(8),
        cost_estimate=cost(2 * rows * protos, 4 * MIB),
        name="row_pass",
    )(*columns, *[in_vmem(expo)] * STREAMS)


def column_kernel(count, parts, *refs):
    row_refs, expo_refs, column_ref = refs[:parts], refs[parts:-1], refs[-1]
    step = pl.program_id(0)
    scale = split_rows(1.0 / (count * total_of(row_refs)))
    block = expo_refs[0].shape[0]
    total = None
    for k, expo_ref in enumerate(expo_refs):
        sums = lax.dot_general(
            scale[:, k * block : (k + 1) * block], expo_ref[...], (((1,), (0,)), ((), ())), preferred_element_type=F32
        )
        total = sums if total is None else total + sums
    total = jnp.sum(total, axis=0, keepdims=True)

    @pl.when(step == 0)
    def _():
        column_ref[...] = total

    @pl.when(step > 0)
    def _():
        column_ref[...] += total


def column_pass(row_totals, expo, count):
    rows, protos = expo.shape
    block = rows // 8
    return pl.pallas_call(
        functools.partial(column_kernel, count, len(row_totals)),
        grid=(rows // block // STREAMS,),
        in_specs=[pl.BlockSpec((1, STREAMS * block), lambda i: (0, i)) for _ in row_totals]
        + streams_of((block, protos)),
        out_specs=pl.BlockSpec((1, protos), lambda i: (0, 0)),
        out_shape=jax.ShapeDtypeStruct((1, protos), F32),
        compiler_params=params(8),
        cost_estimate=cost(2 * rows * protos, 4 * MIB),
        name="column_pass",
    )(*row_totals, *[in_vmem(expo)] * STREAMS)


def partner_kernel(count, total, heat_scale, proto_size, parts, first_ref, second_ref, *refs):
    column_refs = refs[:parts]
    totals_ref, source_ref, wnorm_ref, scores_ref, dscore_ref, loss_ref, table_ref, semaphores, *stages = refs[parts:]
    step = pl.program_id(0)
    groups = table_ref.shape[1]

    @pl.when(step == 0)
    def _():
        parts = semaphores.shape[0]
        size = source_ref.shape[0] // parts
        copies = [
            pltpu.make_async_copy(
                source_ref.at[pl.ds(k * size, size)], table_ref.at[pl.ds(k * size, size)], semaphores.at[k]
            )
            for k in range(parts)
        ]
        for copy in copies:
            copy.start()
        for copy in copies:
            copy.wait()

    rows = dscore_ref.shape[0]
    wnorm = wnorm_ref[...]
    scale = 1.0 / (count * total_of(column_refs))
    place_in = lax.broadcasted_iota(jnp.int32, (8, CHUNK), 0)
    loss = jnp.zeros((), F32)
    for start in range(0, rows, CHUNK):
        at = slice(start, start + CHUNK)
        row_totals, zsum = totals_ref[0:2, at], totals_ref[2:3, at]
        weights = total * (1.0 / (total * row_totals))
        code_totals = 0.5 * jnp.sum(weights * row_totals, axis=0, keepdims=True)
        log_part = jnp.sum(code_totals * jnp.log(zsum)) * (1.0 / proto_size)
        stacked = jnp.where(
            place_in == 0,
            weights[0:1],
            jnp.where(place_in == 1, weights[1:2], jnp.where(place_in == 2, code_totals / zsum, 0.0)),
        ).T
        codes = []
        for number, which_ref in enumerate((first_ref, second_ref)):
            stage_ref = stages[number]
            for row in range(CHUNK):
                place = which_ref[step * rows + start + row]
                stage_ref[row * groups : (row + 1) * groups, :] = table_ref[place].astype(F32)
            unit = jnp.concatenate(
                [stage_ref[pl.ds(k, CHUNK, stride=groups), :].astype(BF16) for k in range(groups)], axis=1
            )
            scores = lax.dot_general(unit, wnorm, (((1,), (1,)), ((), ())), preferred_element_type=F32)
            soft = jnp.exp(scores * (1.0 / SOFTMAX_HEAT))
            expo = soft * soft
            codes.append((stacked[:, number : number + 1] * expo * scale).astype(BF16).astype(F32))
        targets = 0.5 * (codes[0] + codes[1])
        heated = scores_ref[at] * (1.0 / SOFTMAX_HEAT)
        loss = loss + (log_part - jnp.sum(targets * heated))
        dscore_ref[at] = ((jnp.exp(heated) * stacked[:, 2:3] - targets) * heat_scale).astype(BF16)

    @pl.when(step == 0)
    def _():
        loss_ref[...] = jnp.full(loss_ref.shape, loss, F32)

    @pl.when(step > 0)
    def _():
        loss_ref[...] += loss


def partner_pass(first, second, columns, totals, table, wnorm, scores, count, total, proto_size):
    rows = first.shape[0]
    protos, columns_of_table = wnorm.shape
    groups = columns_of_table // LANES
    block = 2 * CHUNK
    heat_scale = count / (32.0 * SOFTMAX_HEAT)
    return pl.pallas_call(
        functools.partial(partner_kernel, count, total, heat_scale, proto_size, len(columns)),
        grid_spec=pltpu.PrefetchScalarGridSpec(
            num_scalar_prefetch=2,
            grid=(rows // block,),
            in_specs=[pl.BlockSpec((1, protos), lambda i, *_: (0, 0)) for _ in columns]
            + [
                pl.BlockSpec((3, block), lambda i, *_: (0, i)),
                pl.BlockSpec(memory_space=pl.ANY),
                pl.BlockSpec(wnorm.shape, lambda i, *_: (0, 0), pipeline_mode=pl.Buffered(1)),
                pl.BlockSpec((block, protos), lambda i, *_: (i, 0)),
            ],
            out_specs=[
                pl.BlockSpec((block, protos), lambda i, *_: (i, 0)),
                pl.BlockSpec((1, LANES), lambda i, *_: (0, 0)),
            ],
            scratch_shapes=[
                pltpu.VMEM(table.shape, BF16),
                pltpu.SemaphoreType.DMA((STREAMS,)),
            ]
            + [pltpu.VMEM((CHUNK * groups, LANES), F32)] * 2,
        ),
        out_shape=[jax.ShapeDtypeStruct((rows, protos), BF16), jax.ShapeDtypeStruct((1, LANES), F32)],
        compiler_params=params(46),
        cost_estimate=cost(4 * rows * columns_of_table * protos, 32 * MIB, 3 * rows * protos),
        name="partner_scores",
    )(first, second, *columns, totals, table, wnorm, scores)


def lookup_kernel(first_ref, second_ref, totals_ref, out_ref):
    rows = first_ref.shape[0]
    for number, which_ref in enumerate((first_ref, second_ref)):

        @pl.loop(0, rows // 16)
        def _(i):
            for j in range(16):
                row = i * 16 + j
                out_ref[number * rows + row] = totals_ref[which_ref[row]]


def lookup(first, second, totals):
    return pl.pallas_call(
        lookup_kernel,
        grid_spec=pltpu.PrefetchScalarGridSpec(
            num_scalar_prefetch=2,
            grid=(1,),
            in_specs=[pl.BlockSpec(memory_space=pltpu.SMEM)],
            out_specs=pl.BlockSpec(memory_space=pltpu.SMEM),
        ),
        out_shape=jax.ShapeDtypeStruct((2 * first.shape[0],), F32),
        compiler_params=params(8),
        cost_estimate=cost(MIB, MIB),
        name="lookup",
    )(first, second, totals)


def gradient_kernel(where_ref, dscore_ref, wnorm_ref, gunit_ref):
    del where_ref
    gunit_ref[0] = jnp.dot(dscore_ref[0], wnorm_ref[...], preferred_element_type=F32).astype(gunit_ref.dtype)


def gradients(where, dscore, wnorm, dtype):
    top, share, protos = dscore.shape[0], *dscore.shape[4:]
    width = wnorm.shape[1]
    return pl.pallas_call(
        gradient_kernel,
        grid_spec=pltpu.PrefetchScalarGridSpec(
            num_scalar_prefetch=1,
            grid=(top,),
            in_specs=[
                pl.BlockSpec(
                    (1, None, None, None, share, protos), lambda i, where: (i, where[0], where[1], where[2], 0, 0)
                ),
                pl.BlockSpec((protos, width), lambda i, where: (0, 0), pipeline_mode=pl.Buffered(1)),
            ],
            out_specs=pl.BlockSpec((1, share, width), lambda i, where: (i, 0, 0)),
        ),
        out_shape=jax.ShapeDtypeStruct((top, share, width), dtype),
        compiler_params=params(16),
        cost_estimate=cost(MIB, MIB),
        name="gradients",
    )(where, in_vmem(dscore), in_vmem(wnorm))


def add_kernel(*refs):
    total = refs[0][...]
    for ref in refs[1:-1]:
        total = total + ref[...].astype(F32)
    refs[-1][...] = total.astype(refs[-1].dtype)


def add_blocks(values, dtype):
    count, share, width = values[0].shape
    at = pl.BlockSpec((1, share, width), lambda i: (i, 0, 0))
    return pl.pallas_call(
        add_kernel,
        grid=(count,),
        in_specs=[at for _ in values],
        out_specs=at,
        out_shape=jax.ShapeDtypeStruct(values[0].shape, dtype),
        compiler_params=params(12),
        cost_estimate=cost(count * share * width, 8 * count * share * width),
        name="add_blocks",
    )(*values)


def combine_kernel(parts, bit_ref, *refs):
    del bit_ref
    own_refs, other_refs, (own_ref, sent_ref) = refs[:parts], refs[parts : 2 * parts], refs[2 * parts :]
    add_kernel(*other_refs, sent_ref)
    add_kernel(*own_refs, own_ref)


def combine(bit, values):
    count, share, width = values[0].shape
    values = [value.reshape(count // 2, 2, share, width) for value in values]
    own_at = pl.BlockSpec((None, None, share, width), lambda i, bit: (i, bit[0], 0, 0))
    other_at = pl.BlockSpec((None, None, share, width), lambda i, bit: (i, 1 - bit[0], 0, 0))
    out_at = pl.BlockSpec((None, share, width), lambda i, bit: (i, 0, 0))
    return pl.pallas_call(
        functools.partial(combine_kernel, len(values)),
        grid_spec=pltpu.PrefetchScalarGridSpec(
            num_scalar_prefetch=1,
            grid=(count // 2,),
            in_specs=[own_at] * len(values) + [other_at] * len(values),
            out_specs=[out_at, out_at],
        ),
        out_shape=[
            jax.ShapeDtypeStruct((count // 2, share, width), F32),
            jax.ShapeDtypeStruct((count // 2, share, width), BF16),
        ],
        compiler_params=params(16),
        cost_estimate=cost(count * share * width, 9 * count * share * width),
        name="combine",
    )(bit, *values, *values)


def proto_gradient_kernel(index_ref, *refs):
    del index_ref
    dscore_refs, unit_refs, own_ref, sent_ref = refs[:8], refs[8:16], refs[16], refs[17]
    both = (((0,), (0,)), ((), ()))
    total = None
    for dscore_ref, unit_ref in zip(dscore_refs, unit_refs):
        rows, protos, part = dscore_ref.shape[0] * dscore_ref.shape[1], dscore_ref.shape[2], unit_ref.shape[-1]
        term = lax.dot_general(
            dscore_ref[...].reshape(rows, protos), unit_ref[...].reshape(rows, part), both, preferred_element_type=F32
        )
        total = term if total is None else total + term
    sent_ref[...] = total.astype(BF16)
    own_ref[...] = total


def proto_gradient(dscore, unit, index, batch_size):
    top, share, protos = dscore.shape[0], *dscore.shape[4:]
    width = unit.shape[1]
    part = width // batch_size
    rows = top * share
    last = batch_size - 1
    unit = unit.reshape(top, 2, 2, 2, share, width)

    def dscore_at(number):
        return pl.BlockSpec(
            (top, None, None, None, share, protos),
            lambda i, index: (0, number >> 2, number >> 1 & 1, number & 1, 0, 0),
            pipeline_mode=pl.Buffered(1),
        )

    def unit_at(number):
        return pl.BlockSpec(
            (top, None, None, None, share, part),
            lambda i, index: (
                0, number >> 2, number >> 1 & 1, number & 1, 0, index[0] ^ (last - i),
            ),
        )

    return pl.pallas_call(
        proto_gradient_kernel,
        grid_spec=pltpu.PrefetchScalarGridSpec(
            num_scalar_prefetch=1,
            grid=(batch_size,),
            in_specs=[dscore_at(number) for number in range(8)] + [unit_at(number) for number in range(8)],
            out_specs=[
                pl.BlockSpec((protos, part), lambda i, index: (0, 0)),
                pl.BlockSpec((None, protos, part), lambda i, index: (last - i, 0, 0)),
            ],
        ),
        out_shape=[
            jax.ShapeDtypeStruct((protos, part), F32),
            jax.ShapeDtypeStruct((batch_size, protos, part), BF16),
        ],
        compiler_params=params(20),
        cost_estimate=cost(MIB, MIB),
        name="proto_gradient",
    )(index, *[in_vmem(dscore)] * 8, *[unit] * 8)


def embed_gradient_kernel(index_ref, embeddings_ref, *refs):
    del index_ref
    *part_refs, out_ref = refs
    gunit = part_refs[0][...]
    for ref in part_refs[1:]:
        gunit = gunit + ref[...].astype(F32)
    hidden = embeddings_ref[...].astype(F32)
    inverse = 1.0 / jnp.sqrt(jnp.sum(hidden * hidden, axis=1, keepdims=True) + NORM_EPSILON)
    along = jnp.sum(hidden * gunit, axis=1, keepdims=True)
    out_ref[...] = inverse * gunit - hidden * (inverse * inverse * inverse * along)


def embed_gradient(index, embeddings, values):
    share, width = values[0].shape
    whole = pl.BlockSpec((share, width), lambda i, index: (0, 0))
    return pl.pallas_call(
        embed_gradient_kernel,
        grid_spec=pltpu.PrefetchScalarGridSpec(
            num_scalar_prefetch=1,
            grid=(1,),
            in_specs=[pl.BlockSpec((share, width), lambda i, index: (index[0], 0))] + [whole for _ in values],
            out_specs=whole,
        ),
        out_shape=jax.ShapeDtypeStruct((share, width), F32),
        compiler_params=params(60),
        cost_estimate=cost(8 * share * width, 4 * MIB),
        name="embed_gradient",
    )(index, embeddings, *values)


PLACE = ("top", "middle", "low")


def swap(value, axis, distance):
    size = lax.axis_size(axis)
    return lax.ppermute(value, axis, [(i, i ^ distance) for i in range(size)])


def parts_of(value, axis):
    size = lax.axis_size(axis)
    if size > 4:
        return [lax.psum(value, axis)]
    return [value] + [swap(value, axis, distance) for distance in range(1, size)]


def proto_parts_of(value):
    return parts_of(value + swap(value, "core", 1), PLACE)


def scalar(value):
    return jnp.full((1,), value, jnp.int32)


def on_device(embeddings, prototypes, partners):
    row_count, width = embeddings.shape
    proto_count = prototypes.shape[0]
    batch_size = lax.axis_size("batch")
    places = lax.axis_size(PLACE)
    proto_size = 2 * places
    total_rows = row_count * batch_size
    centroids = proto_count * proto_size
    share = row_count // proto_size
    batch_index = lax.axis_index("batch")
    low = lax.axis_index("low")
    middle = lax.axis_index("middle")
    place = lax.axis_index(PLACE)
    core = lax.axis_index("core")
    proto_index = 2 * place + core

    quarter = row_count // 4
    steps = quarter // OWN_BLOCK
    own = own_rows(embeddings, scalar((2 * low + core) * steps), OWN_BLOCK, steps)
    table = lax.all_gather(own, ("batch", "low", "core"), axis=0, tiled=True)

    unit, wnorm, scores, expo, zsum, columns = scores_of(embeddings, prototypes, share)
    columns = parts_of(columns, "batch")
    for iteration in range(ITERS - 1):
        row_totals = proto_parts_of(row_pass(columns, expo, centroids))
        columns = parts_of(column_pass(row_totals, expo, total_rows), "batch")

    row_part = row_pass(columns, expo, centroids)
    row_totals = functools.reduce(jnp.add, proto_parts_of(jnp.concatenate([row_part, zsum], axis=0)))
    own_totals, zsum = row_totals[0], row_totals[1]
    all_totals = jnp.concatenate([own_totals] + [swap(own_totals, "batch", distance) for distance in range(1, batch_size)])
    away = (partners // row_count ^ batch_index) * row_count + partners % row_count
    partner_totals = lookup(away[:, 0], away[:, 1], all_totals).reshape(2, row_count)
    row_totals = jnp.concatenate([partner_totals, zsum[None]], axis=0)
    dscore, loss = partner_pass(
        partners[:, 0], partners[:, 1], columns, row_totals, table, wnorm, scores, centroids, total_rows, proto_size
    )
    dscore = dscore.reshape(places // 4, 2, 2, 2, share, proto_count)

    def after(value, *earlier):
        return lax.optimization_barrier((value, *earlier))[0]

    def part_of(number, other_after=(), own_after=()):
        place_bits = [middle ^ (number >> 1), low ^ (number & 1)]

        def run(other, dtype, earlier):
            where = after(jnp.stack(place_bits + [core ^ other]).astype(jnp.int32), *earlier)
            return gradients(where, dscore, wnorm, dtype)

        gunit = run(1, BF16, other_after)
        return [run(0, F32, own_after), swap(gunit, "core", 1)]

    loss = functools.reduce(jnp.add, parts_of(loss, PLACE))
    forwarded = after(add_blocks(part_of(3), BF16), loss)
    from_forwarder = swap(forwarded, PLACE, 1)
    near = add_blocks(part_of(1, [forwarded], [forwarded]), BF16)
    from_near = swap(near, PLACE, 1)
    across = part_of(2, [near], [near])
    values = part_of(0, [near], [from_near])

    loss = loss + swap(loss, "core", 1)
    loss = functools.reduce(jnp.add, parts_of(loss, "batch"))
    grad_proto, proto_sent = proto_gradient(dscore, unit, after(scalar(batch_index), values[1]), batch_size)
    from_forwarder = after(from_forwarder, proto_sent)
    across = add_blocks(across + [from_forwarder], BF16)
    values += [from_near, swap(across, PLACE, 2)]
    proto_sent = after(proto_sent, loss, across)

    bit = 2
    while (1 << bit) < places:
        kept, sent = combine(scalar((place >> bit) % 2), values)
        values = [kept, swap(sent, PLACE, 1 << bit)]
        bit += 1
    grad_embed = embed_gradient(scalar(proto_index), embeddings, [value[0] for value in values])
    arrived = [swap(proto_sent[distance], "batch", distance) for distance in range(batch_size - 1, 0, -1)]
    loss = loss[0, 0] / total_rows
    for block in arrived:
        grad_proto = grad_proto + block.astype(F32)

    return (loss, grad_proto, grad_embed)


def solution(mesh):
    batch_size, proto_size = mesh.shape["batch"], mesh.shape["proto"]
    devices = mesh.devices.reshape(batch_size, proto_size // 8, 2, 2, 2)
    proto = PLACE + ("core",)
    return jax.shard_map(
        on_device,
        mesh=jax.sharding.Mesh(devices, ("batch",) + proto),
        in_specs=(P("batch", None), P(proto, None), P("batch", None)),
        out_specs=(P(), P(proto, "batch"), P(("batch",) + proto, None)),
        check_vma=False,
    )
```

```python
import functools

import jax
import jax.numpy as jnp
from jax import lax
from jax.experimental import pallas as pl
from jax.experimental.pallas import tpu as pltpu
from jax.sharding import PartitionSpec as P

ITERS = 3
BALANCE_SMOOTHING = 0.05
SOFTMAX_HEAT = 0.1
NORM_EPSILON = 1e-06
LANES = 128
CHUNK = 256
STREAMS = 4
OWN_BLOCK = 256
MIB = 1 << 20
F32 = jnp.float32
BF16 = jnp.bfloat16


def params(mib=60):
    return pltpu.CompilerParams(vmem_limit_bytes=mib * MIB)


def in_vmem(value):
    return pltpu.with_memory_space_constraint(value, pltpu.VMEM)


def cost(flops, moved, exps=0):
    return pl.CostEstimate(flops=flops, bytes_accessed=moved, transcendentals=exps)


def normalized(block):
    wide = block.astype(F32)
    inverse = 1.0 / jnp.sqrt(jnp.sum(wide * wide, axis=1, keepdims=True) + NORM_EPSILON)
    return wide * inverse


def lane_row_sums(values):
    columns = values.shape[1]
    part = values[:, 0:LANES]
    for start in range(LANES, columns, LANES):
        part = part + values[:, start : start + LANES]
    return jnp.sum(part.T, axis=0, keepdims=True)


def split_rows(row):
    high = row.astype(BF16).astype(F32)
    middle = (row - high).astype(BF16).astype(F32)
    low = row - high - middle
    place = lax.broadcasted_iota(jnp.int32, (16, row.shape[1]), 0)
    stacked = jnp.where(place == 0, high, jnp.where(place == 1, middle, jnp.where(place == 2, low, 0.0)))
    return stacked.astype(BF16)


def total_of(refs):
    total = refs[0][...]
    for ref in refs[1:]:
        total = total + ref[...]
    return total


def own_rows_kernel(index_ref, embeddings_ref, table_ref, stage_ref):
    del index_ref
    rows, columns = embeddings_ref.shape
    unit = normalized(embeddings_ref[...]).astype(BF16).astype(F32)
    groups = columns // LANES
    for k in range(groups):
        stage_ref[pl.ds(k, rows, stride=groups), :] = unit[:, k * LANES : (k + 1) * LANES]
    table_ref[...] = stage_ref[...].reshape(rows, groups, LANES).astype(BF16)


def own_rows(embeddings, index, block, count):
    columns = embeddings.shape[1]
    groups = columns // LANES
    return pl.pallas_call(
        own_rows_kernel,
        grid_spec=pltpu.PrefetchScalarGridSpec(
            num_scalar_prefetch=1,
            grid=(count,),
            in_specs=[pl.BlockSpec((block, columns), lambda i, index: (index[0] + i, 0))],
            out_specs=pl.BlockSpec((block, groups, LANES), lambda i, index: (i, 0, 0)),
            scratch_shapes=[pltpu.VMEM((block * groups, LANES), F32)],
        ),
        out_shape=jax.ShapeDtypeStruct((block * count, groups, LANES), BF16),
        compiler_params=params(60),
        name="own_rows",
    )(index, embeddings)


def scores_kernel(embeddings_ref, prototypes_ref, unit_ref, wnorm_ref, scores_ref, expo_ref, zsum_ref, column_ref):
    step = pl.program_id(0)

    @pl.when(step == 0)
    def _():
        wnorm_ref[...] = normalized(prototypes_ref[...]).astype(BF16)

    share = embeddings_ref.shape[0] // 2
    sums = None
    for k in range(2):
        at = slice(k * share, (k + 1) * share)
        unit = normalized(embeddings_ref[at]).astype(BF16)
        unit_ref[at] = unit
        scores = lax.dot_general(unit, wnorm_ref[...], (((1,), (1,)), ((), ())), preferred_element_type=F32)
        scores_ref[at] = scores
        soft = jnp.exp(scores * (1.0 / SOFTMAX_HEAT))
        zsum_ref[:, at] = lane_row_sums(soft)
        expo = soft * soft
        expo_ref[at] = expo.astype(BF16)
        part = jnp.sum(expo, axis=0, keepdims=True)
        sums = part if sums is None else sums + part

    @pl.when(step == 0)
    def _():
        column_ref[...] = sums

    @pl.when(step > 0)
    def _():
        column_ref[...] += sums


def scores_of(embeddings, prototypes, share):
    rows, columns = embeddings.shape
    protos = prototypes.shape[0]
    return pl.pallas_call(
        scores_kernel,
        grid=(rows // share // 2,),
        in_specs=[
            pl.BlockSpec((2 * share, columns), lambda i: (i, 0)),
            pl.BlockSpec((protos, columns), lambda i: (0, 0), pipeline_mode=pl.Buffered(1)),
        ],
        out_specs=[
            pl.BlockSpec((2 * share, columns), lambda i: (i, 0)),
            pl.BlockSpec((protos, columns), lambda i: (0, 0)),
            pl.BlockSpec((2 * share, protos), lambda i: (i, 0)),
            pl.BlockSpec((2 * share, protos), lambda i: (i, 0)),
            pl.BlockSpec((1, 2 * share), lambda i: (0, i)),
            pl.BlockSpec((1, protos), lambda i: (0, 0)),
        ],
        out_shape=[
            jax.ShapeDtypeStruct((rows, columns), BF16),
            jax.ShapeDtypeStruct((protos, columns), BF16),
            jax.ShapeDtypeStruct((rows, protos), F32),
            jax.ShapeDtypeStruct((rows, protos), BF16),
            jax.ShapeDtypeStruct((1, rows), F32),
            jax.ShapeDtypeStruct((1, protos), F32),
        ],
        compiler_params=params(28),
        cost_estimate=cost(2 * rows * columns * protos, 22 * MIB, rows * protos),
        name="scores",
    )(embeddings, prototypes)


def row_kernel(count, parts, *refs):
    column_refs, expo_refs, row_ref = refs[:parts], refs[parts:-1], refs[-1]
    scale = split_rows(1.0 / (count * total_of(column_refs)))
    block = expo_refs[0].shape[0]
    for k, expo_ref in enumerate(expo_refs):
        sums = lax.dot_general(scale, expo_ref[...], (((1,), (1,)), ((), ())), preferred_element_type=F32)
        row_ref[:, k * block : (k + 1) * block] = jnp.sum(sums, axis=0, keepdims=True)


def streams_of(shape):
    return [pl.BlockSpec(shape, functools.partial(lambda k, i: (STREAMS * i + k, 0), k)) for k in range(STREAMS)]


def row_pass(columns, expo, count):
    rows, protos = expo.shape
    block = rows // 8
    return pl.pallas_call(
        functools.partial(row_kernel, count, len(columns)),
        grid=(rows // block // STREAMS,),
        in_specs=[pl.BlockSpec((1, protos), lambda i: (0, 0)) for _ in columns] + streams_of((block, protos)),
        out_specs=pl.BlockSpec((1, STREAMS * block), lambda i: (0, i)),
        out_shape=jax.ShapeDtypeStruct((1, rows), F32),
        compiler_params=params(8),
        cost_estimate=cost(2 * rows * protos, 4 * MIB),
        name="row_pass",
    )(*columns, *[in_vmem(expo)] * STREAMS)


def column_kernel(count, parts, *refs):
    row_refs, expo_refs, column_ref = refs[:parts], refs[parts:-1], refs[-1]
    step = pl.program_id(0)
    scale = split_rows(1.0 / (count * total_of(row_refs)))
    block = expo_refs[0].shape[0]
    total = None
    for k, expo_ref in enumerate(expo_refs):
        sums = lax.dot_general(
            scale[:, k * block : (k + 1) * block], expo_ref[...], (((1,), (0,)), ((), ())), preferred_element_type=F32
        )
        total = sums if total is None else total + sums
    total = jnp.sum(total, axis=0, keepdims=True)

    @pl.when(step == 0)
    def _():
        column_ref[...] = total

    @pl.when(step > 0)
    def _():
        column_ref[...] += total


def column_pass(row_totals, expo, count):
    rows, protos = expo.shape
    block = rows // 8
    return pl.pallas_call(
        functools.partial(column_kernel, count, len(row_totals)),
        grid=(rows // block // STREAMS,),
        in_specs=[pl.BlockSpec((1, STREAMS * block), lambda i: (0, i)) for _ in row_totals]
        + streams_of((block, protos)),
        out_specs=pl.BlockSpec((1, protos), lambda i: (0, 0)),
        out_shape=jax.ShapeDtypeStruct((1, protos), F32),
        compiler_params=params(8),
        cost_estimate=cost(2 * rows * protos, 4 * MIB),
        name="column_pass",
    )(*row_totals, *[in_vmem(expo)] * STREAMS)


def partner_kernel(count, total, heat_scale, proto_size, parts, first_ref, second_ref, *refs):
    column_refs = refs[:parts]
    totals_ref, source_ref, wnorm_ref, scores_ref, dscore_ref, loss_ref, table_ref, semaphores, *stages = refs[parts:]
    step = pl.program_id(0)
    groups = table_ref.shape[1]

    @pl.when(step == 0)
    def _():
        parts = semaphores.shape[0]
        size = source_ref.shape[0] // parts
        copies = [
            pltpu.make_async_copy(
                source_ref.at[pl.ds(k * size, size)], table_ref.at[pl.ds(k * size, size)], semaphores.at[k]
            )
            for k in range(parts)
        ]
        for copy in copies:
            copy.start()
        for copy in copies:
            copy.wait()

    rows = dscore_ref.shape[0]
    wnorm = wnorm_ref[...]
    scale = 1.0 / (count * total_of(column_refs))
    place_in = lax.broadcasted_iota(jnp.int32, (8, CHUNK), 0)
    loss = jnp.zeros((), F32)
    for start in range(0, rows, CHUNK):
        at = slice(start, start + CHUNK)
        row_totals, zsum = totals_ref[0:2, at], totals_ref[2:3, at]
        weights = total * (1.0 / (total * row_totals))
        code_totals = 0.5 * jnp.sum(weights * row_totals, axis=0, keepdims=True)
        log_part = jnp.sum(code_totals * jnp.log(zsum)) * (1.0 / proto_size)
        stacked = jnp.where(
            place_in == 0,
            weights[0:1],
            jnp.where(place_in == 1, weights[1:2], jnp.where(place_in == 2, code_totals / zsum, 0.0)),
        ).T
        codes = []
        for number, which_ref in enumerate((first_ref, second_ref)):
            stage_ref = stages[number]
            for row in range(CHUNK):
                place = which_ref[step * rows + start + row]
                stage_ref[row * groups : (row + 1) * groups, :] = table_ref[place].astype(F32)
            unit = jnp.concatenate(
                [stage_ref[pl.ds(k, CHUNK, stride=groups), :].astype(BF16) for k in range(groups)], axis=1
            )
            scores = lax.dot_general(unit, wnorm, (((1,), (1,)), ((), ())), preferred_element_type=F32)
            soft = jnp.exp(scores * (1.0 / SOFTMAX_HEAT))
            expo = soft * soft
            codes.append((stacked[:, number : number + 1] * expo * scale).astype(BF16).astype(F32))
        targets = 0.5 * (codes[0] + codes[1])
        heated = scores_ref[at] * (1.0 / SOFTMAX_HEAT)
        loss = loss + (log_part - jnp.sum(targets * heated))
        dscore_ref[at] = ((jnp.exp(heated) * stacked[:, 2:3] - targets) * heat_scale).astype(BF16)

    @pl.when(step == 0)
    def _():
        loss_ref[...] = jnp.full(loss_ref.shape, loss, F32)

    @pl.when(step > 0)
    def _():
        loss_ref[...] += loss


def partner_pass(first, second, columns, totals, table, wnorm, scores, count, total, proto_size):
    rows = first.shape[0]
    protos, columns_of_table = wnorm.shape
    groups = columns_of_table // LANES
    block = 2 * CHUNK
    heat_scale = count / (32.0 * SOFTMAX_HEAT)
    return pl.pallas_call(
        functools.partial(partner_kernel, count, total, heat_scale, proto_size, len(columns)),
        grid_spec=pltpu.PrefetchScalarGridSpec(
            num_scalar_prefetch=2,
            grid=(rows // block,),
            in_specs=[pl.BlockSpec((1, protos), lambda i, *_: (0, 0)) for _ in columns]
            + [
                pl.BlockSpec((3, block), lambda i, *_: (0, i)),
                pl.BlockSpec(memory_space=pl.ANY),
                pl.BlockSpec(wnorm.shape, lambda i, *_: (0, 0), pipeline_mode=pl.Buffered(1)),
                pl.BlockSpec((block, protos), lambda i, *_: (i, 0)),
            ],
            out_specs=[
                pl.BlockSpec((block, protos), lambda i, *_: (i, 0)),
                pl.BlockSpec((1, LANES), lambda i, *_: (0, 0)),
            ],
            scratch_shapes=[
                pltpu.VMEM(table.shape, BF16),
                pltpu.SemaphoreType.DMA((STREAMS,)),
            ]
            + [pltpu.VMEM((CHUNK * groups, LANES), F32)] * 2,
        ),
        out_shape=[jax.ShapeDtypeStruct((rows, protos), BF16), jax.ShapeDtypeStruct((1, LANES), F32)],
        compiler_params=params(46),
        cost_estimate=cost(4 * rows * columns_of_table * protos, 32 * MIB, 3 * rows * protos),
        name="partner_scores",
    )(first, second, *columns, totals, table, wnorm, scores)


def lookup_kernel(first_ref, second_ref, totals_ref, out_ref):
    rows = first_ref.shape[0]
    for number, which_ref in enumerate((first_ref, second_ref)):

        @pl.loop(0, rows // 16)
        def _(i):
            for j in range(16):
                row = i * 16 + j
                out_ref[number * rows + row] = totals_ref[which_ref[row]]


def lookup(first, second, totals):
    return pl.pallas_call(
        lookup_kernel,
        grid_spec=pltpu.PrefetchScalarGridSpec(
            num_scalar_prefetch=2,
            grid=(1,),
            in_specs=[pl.BlockSpec(memory_space=pltpu.SMEM)],
            out_specs=pl.BlockSpec(memory_space=pltpu.SMEM),
        ),
        out_shape=jax.ShapeDtypeStruct((2 * first.shape[0],), F32),
        compiler_params=params(8),
        cost_estimate=cost(MIB, MIB),
        name="lookup",
    )(first, second, totals)


def gradient_kernel(where_ref, dscore_ref, wnorm_ref, gunit_ref):
    del where_ref
    gunit_ref[0] = jnp.dot(dscore_ref[0], wnorm_ref[...], preferred_element_type=F32).astype(gunit_ref.dtype)


def gradients(where, dscore, wnorm, dtype):
    top, share, protos = dscore.shape[0], *dscore.shape[4:]
    width = wnorm.shape[1]
    return pl.pallas_call(
        gradient_kernel,
        grid_spec=pltpu.PrefetchScalarGridSpec(
            num_scalar_prefetch=1,
            grid=(top,),
            in_specs=[
                pl.BlockSpec(
                    (1, None, None, None, share, protos), lambda i, where: (i, where[0], where[1], where[2], 0, 0)
                ),
                pl.BlockSpec((protos, width), lambda i, where: (0, 0), pipeline_mode=pl.Buffered(1)),
            ],
            out_specs=pl.BlockSpec((1, share, width), lambda i, where: (i, 0, 0)),
        ),
        out_shape=jax.ShapeDtypeStruct((top, share, width), dtype),
        compiler_params=params(16),
        cost_estimate=cost(MIB, MIB),
        name="gradients",
    )(where, in_vmem(dscore), in_vmem(wnorm))


def add_kernel(*refs):
    total = refs[0][...]
    for ref in refs[1:-1]:
        total = total + ref[...].astype(F32)
    refs[-1][...] = total.astype(refs[-1].dtype)


def add_blocks(values, dtype):
    count, share, width = values[0].shape
    at = pl.BlockSpec((1, share, width), lambda i: (i, 0, 0))
    return pl.pallas_call(
        add_kernel,
        grid=(count,),
        in_specs=[at for _ in values],
        out_specs=at,
        out_shape=jax.ShapeDtypeStruct(values[0].shape, dtype),
        compiler_params=params(12),
        cost_estimate=cost(count * share * width, 8 * count * share * width),
        name="add_blocks",
    )(*values)


def combine_kernel(parts, bit_ref, *refs):
    del bit_ref
    own_refs, other_refs, (own_ref, sent_ref) = refs[:parts], refs[parts : 2 * parts], refs[2 * parts :]
    add_kernel(*other_refs, sent_ref)
    add_kernel(*own_refs, own_ref)


def combine(bit, values):
    count, share, width = values[0].shape
    values = [value.reshape(count // 2, 2, share, width) for value in values]
    own_at = pl.BlockSpec((None, None, share, width), lambda i, bit: (i, bit[0], 0, 0))
    other_at = pl.BlockSpec((None, None, share, width), lambda i, bit: (i, 1 - bit[0], 0, 0))
    out_at = pl.BlockSpec((None, share, width), lambda i, bit: (i, 0, 0))
    return pl.pallas_call(
        functools.partial(combine_kernel, len(values)),
        grid_spec=pltpu.PrefetchScalarGridSpec(
            num_scalar_prefetch=1,
            grid=(count // 2,),
            in_specs=[own_at] * len(values) + [other_at] * len(values),
            out_specs=[out_at, out_at],
        ),
        out_shape=[
            jax.ShapeDtypeStruct((count // 2, share, width), F32),
            jax.ShapeDtypeStruct((count // 2, share, width), BF16),
        ],
        compiler_params=params(16),
        cost_estimate=cost(count * share * width, 9 * count * share * width),
        name="combine",
    )(bit, *values, *values)


def proto_gradient_kernel(index_ref, *refs):
    del index_ref
    dscore_refs, unit_refs, loss_ref, own_ref, sent_ref = refs[:8], refs[8:16], *refs[16:]
    both = (((0,), (0,)), ((), ()))
    total = None
    for dscore_ref, unit_ref in zip(dscore_refs, unit_refs):
        rows, protos, part = dscore_ref.shape[0] * dscore_ref.shape[1], dscore_ref.shape[2], unit_ref.shape[-1]
        term = lax.dot_general(
            dscore_ref[...].reshape(rows, protos), unit_ref[...].reshape(rows, part), both, preferred_element_type=F32
        )
        total = term if total is None else total + term
    protos, part = total.shape
    sent_ref[0:protos] = total.astype(BF16)
    sent_ref[protos:] = split_rows(jnp.concatenate([loss_ref[...]] * (part // LANES), axis=1))
    own_ref[...] = total


def proto_gradient(dscore, unit, loss, index, batch_size):
    top, share, protos = dscore.shape[0], *dscore.shape[4:]
    width = unit.shape[1]
    part = width // batch_size
    rows = top * share
    last = batch_size - 1
    unit = unit.reshape(top, 2, 2, 2, share, width)

    def dscore_at(number):
        return pl.BlockSpec(
            (top, None, None, None, share, protos),
            lambda i, index: (0, number >> 2, number >> 1 & 1, number & 1, 0, 0),
            pipeline_mode=pl.Buffered(1),
        )

    def unit_at(number):
        return pl.BlockSpec(
            (top, None, None, None, share, part),
            lambda i, index: (
                0, number >> 2, number >> 1 & 1, number & 1, 0, index[0] ^ (last - i),
            ),
        )

    return pl.pallas_call(
        proto_gradient_kernel,
        grid_spec=pltpu.PrefetchScalarGridSpec(
            num_scalar_prefetch=1,
            grid=(batch_size,),
            in_specs=[dscore_at(number) for number in range(8)] + [unit_at(number) for number in range(8)]
            + [pl.BlockSpec((1, LANES), lambda i, index: (0, 0))],
            out_specs=[
                pl.BlockSpec((protos, part), lambda i, index: (0, 0)),
                pl.BlockSpec((None, protos + 16, part), lambda i, index: (last - i, 0, 0)),
            ],
        ),
        out_shape=[
            jax.ShapeDtypeStruct((protos, part), F32),
            jax.ShapeDtypeStruct((batch_size, protos + 16, part), BF16),
        ],
        compiler_params=params(20),
        cost_estimate=cost(MIB, MIB),
        name="proto_gradient",
    )(index, *[in_vmem(dscore)] * 8, *[unit] * 8, loss)


def embed_gradient_kernel(index_ref, embeddings_ref, *refs):
    del index_ref
    *part_refs, out_ref = refs
    gunit = part_refs[0][...]
    for ref in part_refs[1:]:
        gunit = gunit + ref[...].astype(F32)
    hidden = embeddings_ref[...].astype(F32)
    inverse = 1.0 / jnp.sqrt(jnp.sum(hidden * hidden, axis=1, keepdims=True) + NORM_EPSILON)
    along = jnp.sum(hidden * gunit, axis=1, keepdims=True)
    out_ref[...] = inverse * gunit - hidden * (inverse * inverse * inverse * along)


def embed_gradient(index, embeddings, values):
    share, width = values[0].shape
    whole = pl.BlockSpec((share, width), lambda i, index: (0, 0))
    return pl.pallas_call(
        embed_gradient_kernel,
        grid_spec=pltpu.PrefetchScalarGridSpec(
            num_scalar_prefetch=1,
            grid=(1,),
            in_specs=[pl.BlockSpec((share, width), lambda i, index: (index[0], 0))] + [whole for _ in values],
            out_specs=whole,
        ),
        out_shape=jax.ShapeDtypeStruct((share, width), F32),
        compiler_params=params(60),
        cost_estimate=cost(8 * share * width, 4 * MIB),
        name="embed_gradient",
    )(index, embeddings, *values)


PLACE = ("top", "middle", "low")


def swap(value, axis, distance):
    size = lax.axis_size(axis)
    return lax.ppermute(value, axis, [(i, i ^ distance) for i in range(size)])


def parts_of(value, axis):
    size = lax.axis_size(axis)
    if size > 4:
        return [lax.psum(value, axis)]
    return [value] + [swap(value, axis, distance) for distance in range(1, size)]


def proto_parts_of(value):
    return parts_of(value + swap(value, "core", 1), PLACE)


def scalar(value):
    return jnp.full((1,), value, jnp.int32)


def on_device(embeddings, prototypes, partners):
    row_count, width = embeddings.shape
    proto_count = prototypes.shape[0]
    batch_size = lax.axis_size("batch")
    places = lax.axis_size(PLACE)
    proto_size = 2 * places
    total_rows = row_count * batch_size
    centroids = proto_count * proto_size
    share = row_count // proto_size
    batch_index = lax.axis_index("batch")
    low = lax.axis_index("low")
    middle = lax.axis_index("middle")
    place = lax.axis_index(PLACE)
    core = lax.axis_index("core")
    proto_index = 2 * place + core

    quarter = row_count // 4
    steps = quarter // OWN_BLOCK
    own = own_rows(embeddings, scalar((2 * low + core) * steps), OWN_BLOCK, steps)
    table = lax.all_gather(own, ("batch", "low", "core"), axis=0, tiled=True)

    unit, wnorm, scores, expo, zsum, columns = scores_of(embeddings, prototypes, share)
    columns = parts_of(columns, "batch")
    for iteration in range(ITERS - 1):
        row_totals = proto_parts_of(row_pass(columns, expo, centroids))
        columns = parts_of(column_pass(row_totals, expo, total_rows), "batch")

    row_part = row_pass(columns, expo, centroids)
    row_totals = functools.reduce(jnp.add, proto_parts_of(jnp.concatenate([row_part, zsum], axis=0)))
    own_totals, zsum = row_totals[0], row_totals[1]
    all_totals = jnp.concatenate([own_totals] + [swap(own_totals, "batch", distance) for distance in range(1, batch_size)])
    away = (partners // row_count ^ batch_index) * row_count + partners % row_count
    partner_totals = lookup(away[:, 0], away[:, 1], all_totals).reshape(2, row_count)
    row_totals = jnp.concatenate([partner_totals, zsum[None]], axis=0)
    dscore, loss = partner_pass(
        partners[:, 0], partners[:, 1], columns, row_totals, table, wnorm, scores, centroids, total_rows, proto_size
    )
    dscore = dscore.reshape(places // 4, 2, 2, 2, share, proto_count)

    def after(value, *earlier):
        return lax.optimization_barrier((value, *earlier))[0]

    def part_of(number, other_after=(), own_after=()):
        place_bits = [middle ^ (number >> 1), low ^ (number & 1)]

        def run(other, dtype, earlier):
            where = after(jnp.stack(place_bits + [core ^ other]).astype(jnp.int32), *earlier)
            return gradients(where, dscore, wnorm, dtype)

        gunit = run(1, BF16, other_after)
        return [run(0, F32, own_after), swap(gunit, "core", 1)]

    loss = loss + swap(loss, "core", 1)
    forwarded = add_blocks(part_of(3), BF16)
    from_forwarder = swap(forwarded, PLACE, 1)
    near = add_blocks(part_of(1, [forwarded], [forwarded]), BF16)
    from_near = swap(near, PLACE, 1)
    across = part_of(2, [near], [near])
    values = part_of(0, [near], [from_near])

    grad_proto, proto_sent = proto_gradient(dscore, unit, loss, after(scalar(batch_index), values[1]), batch_size)
    from_forwarder = after(from_forwarder, proto_sent)
    across = add_blocks(across + [from_forwarder], BF16)
    values += [from_near, swap(across, PLACE, 2)]
    proto_sent = after(proto_sent, across)

    bit = 2
    while (1 << bit) < places:
        kept, sent = combine(scalar((place >> bit) % 2), values)
        values = [kept, swap(sent, PLACE, 1 << bit)]
        bit += 1
    grad_embed = embed_gradient(scalar(proto_index), embeddings, [value[0] for value in values])
    arrived = [swap(proto_sent[distance], "batch", distance) for distance in range(batch_size - 1, 0, -1)]
    for block in arrived:
        grad_proto = grad_proto + block[:proto_count].astype(F32)
        loss = loss + jnp.sum(block[proto_count : proto_count + 3, :LANES].astype(F32), axis=0, keepdims=True)
    loss = functools.reduce(jnp.add, parts_of(loss, PLACE))
    loss = loss[0, 0] / total_rows

    return (loss, grad_proto, grad_embed)


def solution(mesh):
    batch_size, proto_size = mesh.shape["batch"], mesh.shape["proto"]
    devices = mesh.devices.reshape(batch_size, proto_size // 8, 2, 2, 2)
    proto = PLACE + ("core",)
    return jax.shard_map(
        on_device,
        mesh=jax.sharding.Mesh(devices, ("batch",) + proto),
        in_specs=(P("batch", None), P(proto, None), P("batch", None)),
        out_specs=(P(), P(proto, "batch"), P(("batch",) + proto, None)),
        check_vma=False,
    )
```

```python
import functools

import jax
import jax.numpy as jnp
from jax import lax
from jax.experimental import pallas as pl
from jax.experimental.pallas import tpu as pltpu
from jax.sharding import PartitionSpec as P

ITERS = 3
BALANCE_SMOOTHING = 0.05
SOFTMAX_HEAT = 0.1
NORM_EPSILON = 1e-06
LANES = 128
CHUNK = 256
STREAMS = 4
OWN_BLOCK = 256
MIB = 1 << 20
F32 = jnp.float32
BF16 = jnp.bfloat16


def params(mib=60):
    return pltpu.CompilerParams(vmem_limit_bytes=mib * MIB)


def in_vmem(value):
    return pltpu.with_memory_space_constraint(value, pltpu.VMEM)


def cost(flops, moved, exps=0):
    return pl.CostEstimate(flops=flops, bytes_accessed=moved, transcendentals=exps)


def normalized(block):
    wide = block.astype(F32)
    inverse = 1.0 / jnp.sqrt(jnp.sum(wide * wide, axis=1, keepdims=True) + NORM_EPSILON)
    return wide * inverse


def lane_row_sums(values):
    columns = values.shape[1]
    part = values[:, 0:LANES]
    for start in range(LANES, columns, LANES):
        part = part + values[:, start : start + LANES]
    return jnp.sum(part.T, axis=0, keepdims=True)


def split_rows(row):
    high = row.astype(BF16).astype(F32)
    middle = (row - high).astype(BF16).astype(F32)
    low = row - high - middle
    place = lax.broadcasted_iota(jnp.int32, (16, row.shape[1]), 0)
    stacked = jnp.where(place == 0, high, jnp.where(place == 1, middle, jnp.where(place == 2, low, 0.0)))
    return stacked.astype(BF16)


def total_of(refs):
    total = refs[0][...]
    for ref in refs[1:]:
        total = total + ref[...]
    return total


def own_rows_kernel(index_ref, embeddings_ref, table_ref, stage_ref):
    del index_ref
    rows, columns = embeddings_ref.shape
    unit = normalized(embeddings_ref[...]).astype(BF16).astype(F32)
    groups = columns // LANES
    for k in range(groups):
        stage_ref[pl.ds(k, rows, stride=groups), :] = unit[:, k * LANES : (k + 1) * LANES]
    table_ref[...] = stage_ref[...].reshape(rows, groups, LANES).astype(BF16)


def own_rows(embeddings, index, block, count):
    columns = embeddings.shape[1]
    groups = columns // LANES
    return pl.pallas_call(
        own_rows_kernel,
        grid_spec=pltpu.PrefetchScalarGridSpec(
            num_scalar_prefetch=1,
            grid=(count,),
            in_specs=[pl.BlockSpec((block, columns), lambda i, index: (index[0] + i, 0))],
            out_specs=pl.BlockSpec((block, groups, LANES), lambda i, index: (i, 0, 0)),
            scratch_shapes=[pltpu.VMEM((block * groups, LANES), F32)],
        ),
        out_shape=jax.ShapeDtypeStruct((block * count, groups, LANES), BF16),
        compiler_params=params(60),
        name="own_rows",
    )(index, embeddings)


def scores_kernel(embeddings_ref, prototypes_ref, unit_ref, wnorm_ref, scores_ref, expo_ref, zsum_ref, column_ref):
    step = pl.program_id(0)

    @pl.when(step == 0)
    def _():
        wnorm_ref[...] = normalized(prototypes_ref[...]).astype(BF16)

    share = embeddings_ref.shape[0] // 2
    sums = None
    for k in range(2):
        at = slice(k * share, (k + 1) * share)
        unit = normalized(embeddings_ref[at]).astype(BF16)
        unit_ref[at] = unit
        scores = lax.dot_general(unit, wnorm_ref[...], (((1,), (1,)), ((), ())), preferred_element_type=F32)
        scores_ref[at] = scores
        soft = jnp.exp(scores * (1.0 / SOFTMAX_HEAT))
        zsum_ref[:, at] = lane_row_sums(soft)
        expo = soft * soft
        expo_ref[at] = expo.astype(BF16)
        part = jnp.sum(expo, axis=0, keepdims=True)
        sums = part if sums is None else sums + part

    @pl.when(step == 0)
    def _():
        column_ref[...] = sums

    @pl.when(step > 0)
    def _():
        column_ref[...] += sums


def scores_of(embeddings, prototypes, share):
    rows, columns = embeddings.shape
    protos = prototypes.shape[0]
    return pl.pallas_call(
        scores_kernel,
        grid=(rows // share // 2,),
        in_specs=[
            pl.BlockSpec((2 * share, columns), lambda i: (i, 0)),
            pl.BlockSpec((protos, columns), lambda i: (0, 0), pipeline_mode=pl.Buffered(1)),
        ],
        out_specs=[
            pl.BlockSpec((2 * share, columns), lambda i: (i, 0)),
            pl.BlockSpec((protos, columns), lambda i: (0, 0)),
            pl.BlockSpec((2 * share, protos), lambda i: (i, 0)),
            pl.BlockSpec((2 * share, protos), lambda i: (i, 0)),
            pl.BlockSpec((1, 2 * share), lambda i: (0, i)),
            pl.BlockSpec((1, protos), lambda i: (0, 0)),
        ],
        out_shape=[
            jax.ShapeDtypeStruct((rows, columns), BF16),
            jax.ShapeDtypeStruct((protos, columns), BF16),
            jax.ShapeDtypeStruct((rows, protos), F32),
            jax.ShapeDtypeStruct((rows, protos), BF16),
            jax.ShapeDtypeStruct((1, rows), F32),
            jax.ShapeDtypeStruct((1, protos), F32),
        ],
        compiler_params=params(28),
        cost_estimate=cost(2 * rows * columns * protos, 22 * MIB, rows * protos),
        name="scores",
    )(embeddings, prototypes)


def row_kernel(count, parts, *refs):
    column_refs, expo_refs, row_ref = refs[:parts], refs[parts:-1], refs[-1]
    scale = split_rows(1.0 / (count * total_of(column_refs)))
    block = expo_refs[0].shape[0]
    for k, expo_ref in enumerate(expo_refs):
        sums = lax.dot_general(scale, expo_ref[...], (((1,), (1,)), ((), ())), preferred_element_type=F32)
        row_ref[:, k * block : (k + 1) * block] = jnp.sum(sums, axis=0, keepdims=True)


def streams_of(shape):
    return [pl.BlockSpec(shape, functools.partial(lambda k, i: (STREAMS * i + k, 0), k)) for k in range(STREAMS)]


def row_pass(columns, expo, count):
    rows, protos = expo.shape
    block = rows // 8
    return pl.pallas_call(
        functools.partial(row_kernel, count, len(columns)),
        grid=(rows // block // STREAMS,),
        in_specs=[pl.BlockSpec((1, protos), lambda i: (0, 0)) for _ in columns] + streams_of((block, protos)),
        out_specs=pl.BlockSpec((1, STREAMS * block), lambda i: (0, i)),
        out_shape=jax.ShapeDtypeStruct((1, rows), F32),
        compiler_params=params(8),
        cost_estimate=cost(2 * rows * protos, 4 * MIB),
        name="row_pass",
    )(*columns, *[in_vmem(expo)] * STREAMS)


def column_kernel(count, parts, *refs):
    row_refs, expo_refs, column_ref = refs[:parts], refs[parts:-1], refs[-1]
    step = pl.program_id(0)
    scale = split_rows(1.0 / (count * total_of(row_refs)))
    block = expo_refs[0].shape[0]
    total = None
    for k, expo_ref in enumerate(expo_refs):
        sums = lax.dot_general(
            scale[:, k * block : (k + 1) * block], expo_ref[...], (((1,), (0,)), ((), ())), preferred_element_type=F32
        )
        total = sums if total is None else total + sums
    total = jnp.sum(total, axis=0, keepdims=True)

    @pl.when(step == 0)
    def _():
        column_ref[...] = total

    @pl.when(step > 0)
    def _():
        column_ref[...] += total


def column_pass(row_totals, expo, count):
    rows, protos = expo.shape
    block = rows // 8
    return pl.pallas_call(
        functools.partial(column_kernel, count, len(row_totals)),
        grid=(rows // block // STREAMS,),
        in_specs=[pl.BlockSpec((1, STREAMS * block), lambda i: (0, i)) for _ in row_totals]
        + streams_of((block, protos)),
        out_specs=pl.BlockSpec((1, protos), lambda i: (0, 0)),
        out_shape=jax.ShapeDtypeStruct((1, protos), F32),
        compiler_params=params(8),
        cost_estimate=cost(2 * rows * protos, 4 * MIB),
        name="column_pass",
    )(*row_totals, *[in_vmem(expo)] * STREAMS)


def partner_kernel(count, total, heat_scale, proto_size, parts, first_ref, second_ref, *refs):
    column_refs = refs[:parts]
    totals_ref, source_ref, wnorm_ref, scores_ref, dscore_ref, loss_ref, table_ref, semaphores, *stages = refs[parts:]
    step = pl.program_id(0)
    groups = table_ref.shape[1]

    @pl.when(step == 0)
    def _():
        parts = semaphores.shape[0]
        size = source_ref.shape[0] // parts
        copies = [
            pltpu.make_async_copy(
                source_ref.at[pl.ds(k * size, size)], table_ref.at[pl.ds(k * size, size)], semaphores.at[k]
            )
            for k in range(parts)
        ]
        for copy in copies:
            copy.start()
        for copy in copies:
            copy.wait()

    rows = dscore_ref.shape[0]
    wnorm = wnorm_ref[...]
    scale = 1.0 / (count * total_of(column_refs))
    place_in = lax.broadcasted_iota(jnp.int32, (8, CHUNK), 0)
    loss = jnp.zeros((), F32)
    for start in range(0, rows, CHUNK):
        at = slice(start, start + CHUNK)
        row_totals, zsum = totals_ref[0:2, at], totals_ref[2:3, at]
        weights = total * (1.0 / (total * row_totals))
        code_totals = 0.5 * jnp.sum(weights * row_totals, axis=0, keepdims=True)
        log_part = jnp.sum(code_totals * jnp.log(zsum)) * (1.0 / proto_size)
        stacked = jnp.where(
            place_in == 0,
            weights[0:1],
            jnp.where(place_in == 1, weights[1:2], jnp.where(place_in == 2, code_totals / zsum, 0.0)),
        ).T
        codes = []
        for number, which_ref in enumerate((first_ref, second_ref)):
            stage_ref = stages[number]
            for row in range(CHUNK):
                place = which_ref[step * rows + start + row]
                stage_ref[row * groups : (row + 1) * groups, :] = table_ref[place].astype(F32)
            unit = jnp.concatenate(
                [stage_ref[pl.ds(k, CHUNK, stride=groups), :].astype(BF16) for k in range(groups)], axis=1
            )
            scores = lax.dot_general(unit, wnorm, (((1,), (1,)), ((), ())), preferred_element_type=F32)
            soft = jnp.exp(scores * (1.0 / SOFTMAX_HEAT))
            expo = soft * soft
            codes.append((stacked[:, number : number + 1] * expo * scale).astype(BF16).astype(F32))
        targets = 0.5 * (codes[0] + codes[1])
        heated = scores_ref[at] * (1.0 / SOFTMAX_HEAT)
        loss = loss + (log_part - jnp.sum(targets * heated))
        dscore_ref[at] = ((jnp.exp(heated) * stacked[:, 2:3] - targets) * heat_scale).astype(BF16)

    @pl.when(step == 0)
    def _():
        loss_ref[...] = jnp.full(loss_ref.shape, loss, F32)

    @pl.when(step > 0)
    def _():
        loss_ref[...] += loss


def partner_pass(first, second, columns, totals, table, wnorm, scores, count, total, proto_size):
    rows = first.shape[0]
    protos, columns_of_table = wnorm.shape
    groups = columns_of_table // LANES
    block = 2 * CHUNK
    heat_scale = count / (32.0 * SOFTMAX_HEAT)
    return pl.pallas_call(
        functools.partial(partner_kernel, count, total, heat_scale, proto_size, len(columns)),
        grid_spec=pltpu.PrefetchScalarGridSpec(
            num_scalar_prefetch=2,
            grid=(rows // block,),
            in_specs=[pl.BlockSpec((1, protos), lambda i, *_: (0, 0)) for _ in columns]
            + [
                pl.BlockSpec((3, block), lambda i, *_: (0, i)),
                pl.BlockSpec(memory_space=pl.ANY),
                pl.BlockSpec(wnorm.shape, lambda i, *_: (0, 0), pipeline_mode=pl.Buffered(1)),
                pl.BlockSpec((block, protos), lambda i, *_: (i, 0)),
            ],
            out_specs=[
                pl.BlockSpec((block, protos), lambda i, *_: (i, 0)),
                pl.BlockSpec((1, LANES), lambda i, *_: (0, 0)),
            ],
            scratch_shapes=[
                pltpu.VMEM(table.shape, BF16),
                pltpu.SemaphoreType.DMA((STREAMS,)),
            ]
            + [pltpu.VMEM((CHUNK * groups, LANES), F32)] * 2,
        ),
        out_shape=[jax.ShapeDtypeStruct((rows, protos), BF16), jax.ShapeDtypeStruct((1, LANES), F32)],
        compiler_params=params(46),
        cost_estimate=cost(4 * rows * columns_of_table * protos, 32 * MIB, 3 * rows * protos),
        name="partner_scores",
    )(first, second, *columns, totals, table, wnorm, scores)


def lookup_kernel(first_ref, second_ref, totals_ref, out_ref):
    rows = first_ref.shape[0]
    for number, which_ref in enumerate((first_ref, second_ref)):

        @pl.loop(0, rows // 16)
        def _(i):
            for j in range(16):
                row = i * 16 + j
                out_ref[number * rows + row] = totals_ref[which_ref[row]]


def lookup(first, second, totals):
    return pl.pallas_call(
        lookup_kernel,
        grid_spec=pltpu.PrefetchScalarGridSpec(
            num_scalar_prefetch=2,
            grid=(1,),
            in_specs=[pl.BlockSpec(memory_space=pltpu.SMEM)],
            out_specs=pl.BlockSpec(memory_space=pltpu.SMEM),
        ),
        out_shape=jax.ShapeDtypeStruct((2 * first.shape[0],), F32),
        compiler_params=params(8),
        cost_estimate=cost(MIB, MIB),
        name="lookup",
    )(first, second, totals)


def gradient_kernel(where_ref, dscore_ref, wnorm_ref, gunit_ref):
    del where_ref
    gunit_ref[0] = jnp.dot(dscore_ref[0], wnorm_ref[...], preferred_element_type=F32).astype(gunit_ref.dtype)


def gradients(where, dscore, wnorm, dtype):
    top, share, protos = dscore.shape[0], *dscore.shape[4:]
    width = wnorm.shape[1]
    return pl.pallas_call(
        gradient_kernel,
        grid_spec=pltpu.PrefetchScalarGridSpec(
            num_scalar_prefetch=1,
            grid=(top,),
            in_specs=[
                pl.BlockSpec(
                    (1, None, None, None, share, protos), lambda i, where: (i, where[0], where[1], where[2], 0, 0)
                ),
                pl.BlockSpec((protos, width), lambda i, where: (0, 0), pipeline_mode=pl.Buffered(1)),
            ],
            out_specs=pl.BlockSpec((1, share, width), lambda i, where: (i, 0, 0)),
        ),
        out_shape=jax.ShapeDtypeStruct((top, share, width), dtype),
        compiler_params=params(16),
        cost_estimate=cost(MIB, MIB),
        name="gradients",
    )(where, in_vmem(dscore), in_vmem(wnorm))


def add_kernel(*refs):
    total = refs[0][...]
    for ref in refs[1:-1]:
        total = total + ref[...].astype(F32)
    refs[-1][...] = total.astype(refs[-1].dtype)


def add_blocks(values, dtype):
    count, share, width = values[0].shape
    at = pl.BlockSpec((1, share, width), lambda i: (i, 0, 0))
    return pl.pallas_call(
        add_kernel,
        grid=(count,),
        in_specs=[at for _ in values],
        out_specs=at,
        out_shape=jax.ShapeDtypeStruct(values[0].shape, dtype),
        compiler_params=params(12),
        cost_estimate=cost(count * share * width, 8 * count * share * width),
        name="add_blocks",
    )(*values)


def combine_kernel(parts, bit_ref, *refs):
    del bit_ref
    own_refs, other_refs, (own_ref, sent_ref) = refs[:parts], refs[parts : 2 * parts], refs[2 * parts :]
    add_kernel(*other_refs, sent_ref)
    add_kernel(*own_refs, own_ref)


def combine(bit, values):
    count, share, width = values[0].shape
    values = [value.reshape(count // 2, 2, share, width) for value in values]
    own_at = pl.BlockSpec((None, None, share, width), lambda i, bit: (i, bit[0], 0, 0))
    other_at = pl.BlockSpec((None, None, share, width), lambda i, bit: (i, 1 - bit[0], 0, 0))
    out_at = pl.BlockSpec((None, share, width), lambda i, bit: (i, 0, 0))
    return pl.pallas_call(
        functools.partial(combine_kernel, len(values)),
        grid_spec=pltpu.PrefetchScalarGridSpec(
            num_scalar_prefetch=1,
            grid=(count // 2,),
            in_specs=[own_at] * len(values) + [other_at] * len(values),
            out_specs=[out_at, out_at],
        ),
        out_shape=[
            jax.ShapeDtypeStruct((count // 2, share, width), F32),
            jax.ShapeDtypeStruct((count // 2, share, width), BF16),
        ],
        compiler_params=params(16),
        cost_estimate=cost(count * share * width, 9 * count * share * width),
        name="combine",
    )(bit, *values, *values)


def proto_gradient_kernel(index_ref, *refs):
    del index_ref
    dscore_refs, unit_refs, loss_ref, own_ref, sent_ref = refs[:8], refs[8:16], *refs[16:]
    both = (((0,), (0,)), ((), ()))
    total = None
    for dscore_ref, unit_ref in zip(dscore_refs, unit_refs):
        rows, protos, part = dscore_ref.shape[0] * dscore_ref.shape[1], dscore_ref.shape[2], unit_ref.shape[-1]
        term = lax.dot_general(
            dscore_ref[...].reshape(rows, protos), unit_ref[...].reshape(rows, part), both, preferred_element_type=F32
        )
        total = term if total is None else total + term
    protos, part = total.shape
    sent_ref[0:protos] = total.astype(BF16)
    sent_ref[protos:] = split_rows(jnp.concatenate([loss_ref[...]] * (part // LANES), axis=1))
    own_ref[...] = total


def proto_gradient(dscore, unit, loss, index, batch_size):
    top, share, protos = dscore.shape[0], *dscore.shape[4:]
    width = unit.shape[1]
    part = width // batch_size
    rows = top * share
    last = batch_size - 1
    unit = unit.reshape(top, 2, 2, 2, share, width)

    def dscore_at(number):
        return pl.BlockSpec(
            (top, None, None, None, share, protos),
            lambda i, index: (0, number >> 2, number >> 1 & 1, number & 1, 0, 0),
            pipeline_mode=pl.Buffered(1),
        )

    def unit_at(number):
        return pl.BlockSpec(
            (top, None, None, None, share, part),
            lambda i, index: (
                0, number >> 2, number >> 1 & 1, number & 1, 0, index[0] ^ (last - i),
            ),
        )

    return pl.pallas_call(
        proto_gradient_kernel,
        grid_spec=pltpu.PrefetchScalarGridSpec(
            num_scalar_prefetch=1,
            grid=(batch_size,),
            in_specs=[dscore_at(number) for number in range(8)] + [unit_at(number) for number in range(8)]
            + [pl.BlockSpec((1, LANES), lambda i, index: (0, 0))],
            out_specs=[
                pl.BlockSpec((protos, part), lambda i, index: (0, 0)),
                pl.BlockSpec((None, protos + 16, part), lambda i, index: (last - i, 0, 0)),
            ],
        ),
        out_shape=[
            jax.ShapeDtypeStruct((protos, part), F32),
            jax.ShapeDtypeStruct((batch_size, protos + 16, part), BF16),
        ],
        compiler_params=params(20),
        cost_estimate=cost(MIB, MIB),
        name="proto_gradient",
    )(index, *[in_vmem(dscore)] * 8, *[unit] * 8, loss)


def embed_gradient_kernel(index_ref, embeddings_ref, *refs):
    del index_ref
    *part_refs, out_ref = refs
    gunit = part_refs[0][...]
    for ref in part_refs[1:]:
        gunit = gunit + ref[...].astype(F32)
    hidden = embeddings_ref[...].astype(F32)
    inverse = 1.0 / jnp.sqrt(jnp.sum(hidden * hidden, axis=1, keepdims=True) + NORM_EPSILON)
    along = jnp.sum(hidden * gunit, axis=1, keepdims=True)
    out_ref[...] = inverse * gunit - hidden * (inverse * inverse * inverse * along)


def embed_gradient(index, embeddings, values):
    share, width = values[0].shape
    whole = pl.BlockSpec((share, width), lambda i, index: (0, 0))
    return pl.pallas_call(
        embed_gradient_kernel,
        grid_spec=pltpu.PrefetchScalarGridSpec(
            num_scalar_prefetch=1,
            grid=(1,),
            in_specs=[pl.BlockSpec((share, width), lambda i, index: (index[0], 0))] + [whole for _ in values],
            out_specs=whole,
        ),
        out_shape=jax.ShapeDtypeStruct((share, width), F32),
        compiler_params=params(60),
        cost_estimate=cost(8 * share * width, 4 * MIB),
        name="embed_gradient",
    )(index, embeddings, *values)


PLACE = ("top", "middle", "low")


def swap(value, axis, distance):
    size = lax.axis_size(axis)
    return lax.ppermute(value, axis, [(i, i ^ distance) for i in range(size)])


def parts_of(value, axis):
    size = lax.axis_size(axis)
    if size > 4:
        return [lax.psum(value, axis)]
    return [value] + [swap(value, axis, distance) for distance in range(1, size)]


def proto_parts_of(value):
    return parts_of(value + swap(value, "core", 1), PLACE)


def scalar(value):
    return jnp.full((1,), value, jnp.int32)


def on_device(embeddings, prototypes, partners):
    row_count, width = embeddings.shape
    proto_count = prototypes.shape[0]
    batch_size = lax.axis_size("batch")
    places = lax.axis_size(PLACE)
    proto_size = 2 * places
    total_rows = row_count * batch_size
    centroids = proto_count * proto_size
    share = row_count // proto_size
    batch_index = lax.axis_index("batch")
    low = lax.axis_index("low")
    middle = lax.axis_index("middle")
    place = lax.axis_index(PLACE)
    core = lax.axis_index("core")
    proto_index = 2 * place + core

    quarter = row_count // 4
    steps = quarter // OWN_BLOCK
    own = own_rows(embeddings, scalar((2 * low + core) * steps), OWN_BLOCK, steps)
    table = lax.all_gather(own, ("batch", "low", "core"), axis=0, tiled=True)

    unit, wnorm, scores, expo, zsum, columns = scores_of(embeddings, prototypes, share)
    columns = parts_of(columns, "batch")
    for iteration in range(ITERS - 1):
        row_totals = proto_parts_of(row_pass(columns, expo, centroids))
        columns = parts_of(column_pass(row_totals, expo, total_rows), "batch")

    row_part = row_pass(columns, expo, centroids)
    row_totals = functools.reduce(jnp.add, proto_parts_of(jnp.concatenate([row_part, zsum], axis=0)))
    own_totals, zsum = row_totals[0], row_totals[1]
    all_totals = jnp.concatenate([own_totals] + [swap(own_totals, "batch", distance) for distance in range(1, batch_size)])
    away = (partners // row_count ^ batch_index) * row_count + partners % row_count
    partner_totals = lookup(away[:, 0], away[:, 1], all_totals).reshape(2, row_count)
    row_totals = jnp.concatenate([partner_totals, zsum[None]], axis=0)
    dscore, loss = partner_pass(
        partners[:, 0], partners[:, 1], columns, row_totals, table, wnorm, scores, centroids, total_rows, proto_size
    )
    dscore = dscore.reshape(places // 4, 2, 2, 2, share, proto_count)

    def after(value, *earlier):
        return lax.optimization_barrier((value, *earlier))[0]

    def part_of(number, other_after=(), own_after=()):
        place_bits = [middle ^ (number >> 1), low ^ (number & 1)]

        def run(other, dtype, earlier):
            where = after(jnp.stack(place_bits + [core ^ other]).astype(jnp.int32), *earlier)
            return gradients(where, dscore, wnorm, dtype)

        gunit = run(1, BF16, other_after)
        return [run(0, F32, own_after), swap(gunit, "core", 1)]

    loss = loss + swap(loss, "core", 1)
    forwarded = add_blocks(part_of(3), BF16)
    from_forwarder = swap(forwarded, PLACE, 1)
    near = add_blocks(part_of(1, [forwarded], [forwarded]), BF16)
    from_near = swap(near, PLACE, 1)
    across = part_of(2, [near], [near])
    values = part_of(0, [near], [near])

    grad_proto, proto_sent = proto_gradient(dscore, unit, loss, after(scalar(batch_index), values[1]), batch_size)
    from_forwarder = after(from_forwarder, proto_sent)
    from_near = after(from_near, proto_sent)
    across = add_blocks(across + [from_forwarder], BF16)
    values += [from_near, swap(across, PLACE, 2)]
    proto_sent = after(proto_sent, across)

    bit = 2
    while (1 << bit) < places:
        kept, sent = combine(scalar((place >> bit) % 2), values)
        values = [kept, swap(sent, PLACE, 1 << bit)]
        bit += 1
    grad_embed = embed_gradient(scalar(proto_index), embeddings, [value[0] for value in values])
    arrived = [swap(proto_sent[distance], "batch", distance) for distance in range(batch_size - 1, 0, -1)]
    for block in arrived:
        grad_proto = grad_proto + block[:proto_count].astype(F32)
    rows = functools.reduce(jnp.add, [block[proto_count : proto_count + 3, :LANES].astype(F32) for block in arrived])
    loss = loss + jnp.sum(rows, axis=0, keepdims=True)
    loss = functools.reduce(jnp.add, parts_of(loss, PLACE))
    loss = loss[0, 0] / total_rows

    return (loss, grad_proto, grad_embed)


def solution(mesh):
    batch_size, proto_size = mesh.shape["batch"], mesh.shape["proto"]
    devices = mesh.devices.reshape(batch_size, proto_size // 8, 2, 2, 2)
    proto = PLACE + ("core",)
    return jax.shard_map(
        on_device,
        mesh=jax.sharding.Mesh(devices, ("batch",) + proto),
        in_specs=(P("batch", None), P(proto, None), P("batch", None)),
        out_specs=(P(), P(proto, "batch"), P(("batch",) + proto, None)),
        check_vma=False,
    )
```

```python
import functools

import jax
import jax.numpy as jnp
from jax import lax
from jax.experimental import pallas as pl
from jax.experimental.pallas import tpu as pltpu
from jax.sharding import PartitionSpec as P

ITERS = 3
BALANCE_SMOOTHING = 0.05
SOFTMAX_HEAT = 0.1
NORM_EPSILON = 1e-06
LANES = 128
CHUNK = 256
STREAMS = 4
OWN_BLOCK = 256
MIB = 1 << 20
F32 = jnp.float32
BF16 = jnp.bfloat16


def params(mib=60):
    return pltpu.CompilerParams(vmem_limit_bytes=mib * MIB)


def in_vmem(value):
    return pltpu.with_memory_space_constraint(value, pltpu.VMEM)


def cost(flops, moved, exps=0):
    return pl.CostEstimate(flops=flops, bytes_accessed=moved, transcendentals=exps)


def normalized(block):
    wide = block.astype(F32)
    inverse = 1.0 / jnp.sqrt(jnp.sum(wide * wide, axis=1, keepdims=True) + NORM_EPSILON)
    return wide * inverse


def lane_row_sums(values):
    columns = values.shape[1]
    part = values[:, 0:LANES]
    for start in range(LANES, columns, LANES):
        part = part + values[:, start : start + LANES]
    return jnp.sum(part.T, axis=0, keepdims=True)


def split_rows(row):
    high = row.astype(BF16).astype(F32)
    middle = (row - high).astype(BF16).astype(F32)
    low = row - high - middle
    place = lax.broadcasted_iota(jnp.int32, (16, row.shape[1]), 0)
    stacked = jnp.where(place == 0, high, jnp.where(place == 1, middle, jnp.where(place == 2, low, 0.0)))
    return stacked.astype(BF16)


def total_of(refs):
    total = refs[0][...]
    for ref in refs[1:]:
        total = total + ref[...]
    return total


def own_rows_kernel(index_ref, embeddings_ref, table_ref, stage_ref):
    del index_ref
    rows, columns = embeddings_ref.shape
    unit = normalized(embeddings_ref[...]).astype(BF16).astype(F32)
    groups = columns // LANES
    for k in range(groups):
        stage_ref[pl.ds(k, rows, stride=groups), :] = unit[:, k * LANES : (k + 1) * LANES]
    table_ref[...] = stage_ref[...].reshape(rows, groups, LANES).astype(BF16)


def own_rows(embeddings, index, block, count):
    columns = embeddings.shape[1]
    groups = columns // LANES
    return pl.pallas_call(
        own_rows_kernel,
        grid_spec=pltpu.PrefetchScalarGridSpec(
            num_scalar_prefetch=1,
            grid=(count,),
            in_specs=[pl.BlockSpec((block, columns), lambda i, index: (index[0] + i, 0))],
            out_specs=pl.BlockSpec((block, groups, LANES), lambda i, index: (i, 0, 0)),
            scratch_shapes=[pltpu.VMEM((block * groups, LANES), F32)],
        ),
        out_shape=jax.ShapeDtypeStruct((block * count, groups, LANES), BF16),
        compiler_params=params(60),
        name="own_rows",
    )(index, embeddings)


def scores_kernel(embeddings_ref, prototypes_ref, unit_ref, wnorm_ref, scores_ref, expo_ref, zsum_ref, column_ref):
    step = pl.program_id(0)

    @pl.when(step == 0)
    def _():
        wnorm_ref[...] = normalized(prototypes_ref[...]).astype(BF16)

    share = embeddings_ref.shape[0] // 2
    sums = None
    for k in range(2):
        at = slice(k * share, (k + 1) * share)
        unit = normalized(embeddings_ref[at]).astype(BF16)
        unit_ref[at] = unit
        scores = lax.dot_general(unit, wnorm_ref[...], (((1,), (1,)), ((), ())), preferred_element_type=F32)
        scores_ref[at] = scores
        soft = jnp.exp(scores * (1.0 / SOFTMAX_HEAT))
        zsum_ref[:, at] = lane_row_sums(soft)
        expo = soft * soft
        expo_ref[at] = expo.astype(BF16)
        part = jnp.sum(expo, axis=0, keepdims=True)
        sums = part if sums is None else sums + part

    @pl.when(step == 0)
    def _():
        column_ref[...] = sums

    @pl.when(step > 0)
    def _():
        column_ref[...] += sums


def scores_of(embeddings, prototypes, share):
    rows, columns = embeddings.shape
    protos = prototypes.shape[0]
    return pl.pallas_call(
        scores_kernel,
        grid=(rows // share // 2,),
        in_specs=[
            pl.BlockSpec((2 * share, columns), lambda i: (i, 0)),
            pl.BlockSpec((protos, columns), lambda i: (0, 0), pipeline_mode=pl.Buffered(1)),
        ],
        out_specs=[
            pl.BlockSpec((2 * share, columns), lambda i: (i, 0)),
            pl.BlockSpec((protos, columns), lambda i: (0, 0)),
            pl.BlockSpec((2 * share, protos), lambda i: (i, 0)),
            pl.BlockSpec((2 * share, protos), lambda i: (i, 0)),
            pl.BlockSpec((1, 2 * share), lambda i: (0, i)),
            pl.BlockSpec((1, protos), lambda i: (0, 0)),
        ],
        out_shape=[
            jax.ShapeDtypeStruct((rows, columns), BF16),
            jax.ShapeDtypeStruct((protos, columns), BF16),
            jax.ShapeDtypeStruct((rows, protos), F32),
            jax.ShapeDtypeStruct((rows, protos), BF16),
            jax.ShapeDtypeStruct((1, rows), F32),
            jax.ShapeDtypeStruct((1, protos), F32),
        ],
        compiler_params=params(28),
        cost_estimate=cost(2 * rows * columns * protos, 22 * MIB, rows * protos),
        name="scores",
    )(embeddings, prototypes)


def row_kernel(count, parts, *refs):
    column_refs, expo_refs, row_ref = refs[:parts], refs[parts:-1], refs[-1]
    scale = split_rows(1.0 / (count * total_of(column_refs)))
    block = expo_refs[0].shape[0]
    for k, expo_ref in enumerate(expo_refs):
        sums = lax.dot_general(scale, expo_ref[...], (((1,), (1,)), ((), ())), preferred_element_type=F32)
        row_ref[:, k * block : (k + 1) * block] = jnp.sum(sums, axis=0, keepdims=True)


def streams_of(shape):
    return [pl.BlockSpec(shape, functools.partial(lambda k, i: (STREAMS * i + k, 0), k)) for k in range(STREAMS)]


def row_pass(columns, expo, count):
    rows, protos = expo.shape
    block = rows // 8
    return pl.pallas_call(
        functools.partial(row_kernel, count, len(columns)),
        grid=(rows // block // STREAMS,),
        in_specs=[pl.BlockSpec((1, protos), lambda i: (0, 0)) for _ in columns] + streams_of((block, protos)),
        out_specs=pl.BlockSpec((1, STREAMS * block), lambda i: (0, i)),
        out_shape=jax.ShapeDtypeStruct((1, rows), F32),
        compiler_params=params(8),
        cost_estimate=cost(2 * rows * protos, 4 * MIB),
        name="row_pass",
    )(*columns, *[in_vmem(expo)] * STREAMS)


def column_kernel(count, parts, *refs):
    row_refs, expo_refs, column_ref = refs[:parts], refs[parts:-1], refs[-1]
    step = pl.program_id(0)
    scale = split_rows(1.0 / (count * total_of(row_refs)))
    block = expo_refs[0].shape[0]
    total = None
    for k, expo_ref in enumerate(expo_refs):
        sums = lax.dot_general(
            scale[:, k * block : (k + 1) * block], expo_ref[...], (((1,), (0,)), ((), ())), preferred_element_type=F32
        )
        total = sums if total is None else total + sums
    total = jnp.sum(total, axis=0, keepdims=True)

    @pl.when(step == 0)
    def _():
        column_ref[...] = total

    @pl.when(step > 0)
    def _():
        column_ref[...] += total


def column_pass(row_totals, expo, count):
    rows, protos = expo.shape
    block = rows // 8
    return pl.pallas_call(
        functools.partial(column_kernel, count, len(row_totals)),
        grid=(rows // block // STREAMS,),
        in_specs=[pl.BlockSpec((1, STREAMS * block), lambda i: (0, i)) for _ in row_totals]
        + streams_of((block, protos)),
        out_specs=pl.BlockSpec((1, protos), lambda i: (0, 0)),
        out_shape=jax.ShapeDtypeStruct((1, protos), F32),
        compiler_params=params(8),
        cost_estimate=cost(2 * rows * protos, 4 * MIB),
        name="column_pass",
    )(*row_totals, *[in_vmem(expo)] * STREAMS)


def partner_kernel(count, total, heat_scale, proto_size, parts, first_ref, second_ref, *refs):
    column_refs = refs[:parts]
    totals_ref, source_ref, wnorm_ref, scores_ref, dscore_ref, loss_ref, table_ref, semaphores, *stages = refs[parts:]
    step = pl.program_id(0)
    groups = table_ref.shape[1]

    @pl.when(step == 0)
    def _():
        parts = semaphores.shape[0]
        size = source_ref.shape[0] // parts
        copies = [
            pltpu.make_async_copy(
                source_ref.at[pl.ds(k * size, size)], table_ref.at[pl.ds(k * size, size)], semaphores.at[k]
            )
            for k in range(parts)
        ]
        for copy in copies:
            copy.start()
        for copy in copies:
            copy.wait()

    rows = dscore_ref.shape[0]
    wnorm = wnorm_ref[...]
    scale = 1.0 / (count * total_of(column_refs))
    place_in = lax.broadcasted_iota(jnp.int32, (8, CHUNK), 0)
    loss = jnp.zeros((), F32)
    for start in range(0, rows, CHUNK):
        at = slice(start, start + CHUNK)
        row_totals, zsum = totals_ref[0:2, at], totals_ref[2:3, at]
        weights = total * (1.0 / (total * row_totals))
        code_totals = 0.5 * jnp.sum(weights * row_totals, axis=0, keepdims=True)
        log_part = jnp.sum(code_totals * jnp.log(zsum)) * (1.0 / proto_size)
        stacked = jnp.where(
            place_in == 0,
            weights[0:1],
            jnp.where(place_in == 1, weights[1:2], jnp.where(place_in == 2, code_totals / zsum, 0.0)),
        ).T
        codes = []
        for number, which_ref in enumerate((first_ref, second_ref)):
            stage_ref = stages[number]
            for row in range(CHUNK):
                place = which_ref[step * rows + start + row]
                stage_ref[row * groups : (row + 1) * groups, :] = table_ref[place].astype(F32)
            unit = jnp.concatenate(
                [stage_ref[pl.ds(k, CHUNK, stride=groups), :].astype(BF16) for k in range(groups)], axis=1
            )
            scores = lax.dot_general(unit, wnorm, (((1,), (1,)), ((), ())), preferred_element_type=F32)
            soft = jnp.exp(scores * (1.0 / SOFTMAX_HEAT))
            expo = soft * soft
            codes.append((stacked[:, number : number + 1] * expo * scale).astype(BF16).astype(F32))
        targets = 0.5 * (codes[0] + codes[1])
        heated = scores_ref[at] * (1.0 / SOFTMAX_HEAT)
        loss = loss + (log_part - jnp.sum(targets * heated))
        dscore_ref[at] = ((jnp.exp(heated) * stacked[:, 2:3] - targets) * heat_scale).astype(BF16)

    @pl.when(step == 0)
    def _():
        loss_ref[...] = jnp.full(loss_ref.shape, loss, F32)

    @pl.when(step > 0)
    def _():
        loss_ref[...] += loss


def partner_pass(first, second, columns, totals, table, wnorm, scores, count, total, proto_size):
    rows = first.shape[0]
    protos, columns_of_table = wnorm.shape
    groups = columns_of_table // LANES
    block = 2 * CHUNK
    heat_scale = count / (32.0 * SOFTMAX_HEAT)
    return pl.pallas_call(
        functools.partial(partner_kernel, count, total, heat_scale, proto_size, len(columns)),
        grid_spec=pltpu.PrefetchScalarGridSpec(
            num_scalar_prefetch=2,
            grid=(rows // block,),
            in_specs=[pl.BlockSpec((1, protos), lambda i, *_: (0, 0)) for _ in columns]
            + [
                pl.BlockSpec((3, block), lambda i, *_: (0, i)),
                pl.BlockSpec(memory_space=pl.ANY),
                pl.BlockSpec(wnorm.shape, lambda i, *_: (0, 0), pipeline_mode=pl.Buffered(1)),
                pl.BlockSpec((block, protos), lambda i, *_: (i, 0)),
            ],
            out_specs=[
                pl.BlockSpec((block, protos), lambda i, *_: (i, 0)),
                pl.BlockSpec((1, LANES), lambda i, *_: (0, 0)),
            ],
            scratch_shapes=[
                pltpu.VMEM(table.shape, BF16),
                pltpu.SemaphoreType.DMA((STREAMS,)),
            ]
            + [pltpu.VMEM((CHUNK * groups, LANES), F32)] * 2,
        ),
        out_shape=[jax.ShapeDtypeStruct((rows, protos), BF16), jax.ShapeDtypeStruct((1, LANES), F32)],
        compiler_params=params(46),
        cost_estimate=cost(4 * rows * columns_of_table * protos, 32 * MIB, 3 * rows * protos),
        name="partner_scores",
    )(first, second, *columns, totals, table, wnorm, scores)


def lookup_kernel(first_ref, second_ref, totals_ref, out_ref):
    rows = first_ref.shape[0]
    for number, which_ref in enumerate((first_ref, second_ref)):

        @pl.loop(0, rows // 16)
        def _(i):
            for j in range(16):
                row = i * 16 + j
                out_ref[number * rows + row] = totals_ref[which_ref[row]]


def lookup(first, second, totals):
    return pl.pallas_call(
        lookup_kernel,
        grid_spec=pltpu.PrefetchScalarGridSpec(
            num_scalar_prefetch=2,
            grid=(1,),
            in_specs=[pl.BlockSpec(memory_space=pltpu.SMEM)],
            out_specs=pl.BlockSpec(memory_space=pltpu.SMEM),
        ),
        out_shape=jax.ShapeDtypeStruct((2 * first.shape[0],), F32),
        compiler_params=params(8),
        cost_estimate=cost(MIB, MIB),
        name="lookup",
    )(first, second, totals)


def gradient_kernel(where_ref, dscore_ref, wnorm_ref, gunit_ref):
    del where_ref
    gunit_ref[0] = jnp.dot(dscore_ref[0], wnorm_ref[...], preferred_element_type=F32).astype(gunit_ref.dtype)


def gradients(where, dscore, wnorm, dtype):
    top, share, protos = dscore.shape[0], *dscore.shape[4:]
    width = wnorm.shape[1]
    return pl.pallas_call(
        gradient_kernel,
        grid_spec=pltpu.PrefetchScalarGridSpec(
            num_scalar_prefetch=1,
            grid=(top,),
            in_specs=[
                pl.BlockSpec(
                    (1, None, None, None, share, protos), lambda i, where: (i, where[0], where[1], where[2], 0, 0)
                ),
                pl.BlockSpec((protos, width), lambda i, where: (0, 0), pipeline_mode=pl.Buffered(1)),
            ],
            out_specs=pl.BlockSpec((1, share, width), lambda i, where: (i, 0, 0)),
        ),
        out_shape=jax.ShapeDtypeStruct((top, share, width), dtype),
        compiler_params=params(16),
        cost_estimate=cost(MIB, MIB),
        name="gradients",
    )(where, in_vmem(dscore), in_vmem(wnorm))


def add_kernel(*refs):
    total = refs[0][...]
    for ref in refs[1:-1]:
        total = total + ref[...].astype(F32)
    refs[-1][...] = total.astype(refs[-1].dtype)


def add_blocks(values, dtype):
    count, share, width = values[0].shape
    at = pl.BlockSpec((1, share, width), lambda i: (i, 0, 0))
    return pl.pallas_call(
        add_kernel,
        grid=(count,),
        in_specs=[at for _ in values],
        out_specs=at,
        out_shape=jax.ShapeDtypeStruct(values[0].shape, dtype),
        compiler_params=params(12),
        cost_estimate=cost(count * share * width, 8 * count * share * width),
        name="add_blocks",
    )(*values)


def combine_kernel(parts, bit_ref, *refs):
    del bit_ref
    own_refs, other_refs, (own_ref, sent_ref) = refs[:parts], refs[parts : 2 * parts], refs[2 * parts :]
    add_kernel(*other_refs, sent_ref)
    add_kernel(*own_refs, own_ref)


def combine(bit, values):
    count, share, width = values[0].shape
    values = [value.reshape(count // 2, 2, share, width) for value in values]
    own_at = pl.BlockSpec((None, None, share, width), lambda i, bit: (i, bit[0], 0, 0))
    other_at = pl.BlockSpec((None, None, share, width), lambda i, bit: (i, 1 - bit[0], 0, 0))
    out_at = pl.BlockSpec((None, share, width), lambda i, bit: (i, 0, 0))
    return pl.pallas_call(
        functools.partial(combine_kernel, len(values)),
        grid_spec=pltpu.PrefetchScalarGridSpec(
            num_scalar_prefetch=1,
            grid=(count // 2,),
            in_specs=[own_at] * len(values) + [other_at] * len(values),
            out_specs=[out_at, out_at],
        ),
        out_shape=[
            jax.ShapeDtypeStruct((count // 2, share, width), F32),
            jax.ShapeDtypeStruct((count // 2, share, width), BF16),
        ],
        compiler_params=params(16),
        cost_estimate=cost(count * share * width, 9 * count * share * width),
        name="combine",
    )(bit, *values, *values)


def proto_gradient_kernel(index_ref, *refs):
    del index_ref
    dscore_refs, unit_refs, loss_ref, own_ref, sent_ref = refs[:8], refs[8:16], *refs[16:]
    both = (((0,), (0,)), ((), ()))
    total = None
    for dscore_ref, unit_ref in zip(dscore_refs, unit_refs):
        rows, protos, part = dscore_ref.shape[0] * dscore_ref.shape[1], dscore_ref.shape[2], unit_ref.shape[-1]
        term = lax.dot_general(
            dscore_ref[...].reshape(rows, protos), unit_ref[...].reshape(rows, part), both, preferred_element_type=F32
        )
        total = term if total is None else total + term
    protos, part = total.shape
    sent_ref[0:protos] = total.astype(BF16)
    sent_ref[protos:] = split_rows(jnp.concatenate([loss_ref[...]] * (part // LANES), axis=1))
    own_ref[...] = total


def proto_gradient(dscore, unit, loss, index, batch_size):
    top, share, protos = dscore.shape[0], *dscore.shape[4:]
    width = unit.shape[1]
    part = width // batch_size
    rows = top * share
    last = batch_size - 1
    unit = unit.reshape(top, 2, 2, 2, share, width)

    def dscore_at(number):
        return pl.BlockSpec(
            (top, None, None, None, share, protos),
            lambda i, index: (0, number >> 2, number >> 1 & 1, number & 1, 0, 0),
            pipeline_mode=pl.Buffered(1),
        )

    def unit_at(number):
        return pl.BlockSpec(
            (top, None, None, None, share, part),
            lambda i, index: (
                0, number >> 2, number >> 1 & 1, number & 1, 0, index[0] ^ (last - i),
            ),
        )

    return pl.pallas_call(
        proto_gradient_kernel,
        grid_spec=pltpu.PrefetchScalarGridSpec(
            num_scalar_prefetch=1,
            grid=(batch_size,),
            in_specs=[dscore_at(number) for number in range(8)] + [unit_at(number) for number in range(8)]
            + [pl.BlockSpec((1, LANES), lambda i, index: (0, 0))],
            out_specs=[
                pl.BlockSpec((protos, part), lambda i, index: (0, 0)),
                pl.BlockSpec((None, protos + 16, part), lambda i, index: (last - i, 0, 0)),
            ],
        ),
        out_shape=[
            jax.ShapeDtypeStruct((protos, part), F32),
            jax.ShapeDtypeStruct((batch_size, protos + 16, part), BF16),
        ],
        compiler_params=params(20),
        cost_estimate=cost(MIB, MIB),
        name="proto_gradient",
    )(index, *[in_vmem(dscore)] * 8, *[unit] * 8, loss)


def embed_gradient_kernel(index_ref, embeddings_ref, *refs):
    del index_ref
    *part_refs, out_ref = refs
    gunit = part_refs[0][...]
    for ref in part_refs[1:]:
        gunit = gunit + ref[...].astype(F32)
    hidden = embeddings_ref[...].astype(F32)
    inverse = 1.0 / jnp.sqrt(jnp.sum(hidden * hidden, axis=1, keepdims=True) + NORM_EPSILON)
    along = jnp.sum(hidden * gunit, axis=1, keepdims=True)
    out_ref[...] = inverse * gunit - hidden * (inverse * inverse * inverse * along)


def embed_gradient(index, embeddings, values):
    share, width = values[0].shape
    whole = pl.BlockSpec((share, width), lambda i, index: (0, 0))
    return pl.pallas_call(
        embed_gradient_kernel,
        grid_spec=pltpu.PrefetchScalarGridSpec(
            num_scalar_prefetch=1,
            grid=(1,),
            in_specs=[pl.BlockSpec((share, width), lambda i, index: (index[0], 0))] + [whole for _ in values],
            out_specs=whole,
        ),
        out_shape=jax.ShapeDtypeStruct((share, width), F32),
        compiler_params=params(60),
        cost_estimate=cost(8 * share * width, 4 * MIB),
        name="embed_gradient",
    )(index, embeddings, *values)


PLACE = ("top", "middle", "low")


def swap(value, axis, distance):
    size = lax.axis_size(axis)
    return lax.ppermute(value, axis, [(i, i ^ distance) for i in range(size)])


def parts_of(value, axis):
    size = lax.axis_size(axis)
    if size > 4:
        return [lax.psum(value, axis)]
    return [value] + [swap(value, axis, distance) for distance in range(1, size)]


def proto_parts_of(value):
    return parts_of(value + swap(value, "core", 1), PLACE)


def scalar(value):
    return jnp.full((1,), value, jnp.int32)


def on_device(embeddings, prototypes, partners):
    row_count, width = embeddings.shape
    proto_count = prototypes.shape[0]
    batch_size = lax.axis_size("batch")
    places = lax.axis_size(PLACE)
    proto_size = 2 * places
    total_rows = row_count * batch_size
    centroids = proto_count * proto_size
    share = row_count // proto_size
    batch_index = lax.axis_index("batch")
    low = lax.axis_index("low")
    middle = lax.axis_index("middle")
    place = lax.axis_index(PLACE)
    core = lax.axis_index("core")
    proto_index = 2 * place + core

    quarter = row_count // 4
    steps = quarter // OWN_BLOCK
    own = own_rows(embeddings, scalar((2 * low + core) * steps), OWN_BLOCK, steps)
    table = lax.all_gather(own, ("batch", "low", "core"), axis=0, tiled=True)

    unit, wnorm, scores, expo, zsum, columns = scores_of(embeddings, prototypes, share)
    columns = parts_of(columns, "batch")
    for iteration in range(ITERS - 1):
        row_totals = proto_parts_of(row_pass(columns, expo, centroids))
        columns = parts_of(column_pass(row_totals, expo, total_rows), "batch")

    row_part = row_pass(columns, expo, centroids)
    row_totals = functools.reduce(jnp.add, proto_parts_of(jnp.concatenate([row_part, zsum], axis=0)))
    own_totals, zsum = row_totals[0], row_totals[1]
    all_totals = jnp.concatenate([own_totals] + [swap(own_totals, "batch", distance) for distance in range(1, batch_size)])
    away = (partners // row_count ^ batch_index) * row_count + partners % row_count
    partner_totals = lookup(away[:, 0], away[:, 1], all_totals).reshape(2, row_count)
    row_totals = jnp.concatenate([partner_totals, zsum[None]], axis=0)
    dscore, loss = partner_pass(
        partners[:, 0], partners[:, 1], columns, row_totals, table, wnorm, scores, centroids, total_rows, proto_size
    )
    dscore = dscore.reshape(places // 4, 2, 2, 2, share, proto_count)

    def after(value, *earlier):
        return lax.optimization_barrier((value, *earlier))[0]

    def part_of(number, other_after=(), own_after=()):
        place_bits = [middle ^ (number >> 1), low ^ (number & 1)]

        def run(other, dtype, earlier):
            where = after(jnp.stack(place_bits + [core ^ other]).astype(jnp.int32), *earlier)
            return gradients(where, dscore, wnorm, dtype)

        gunit = run(1, BF16, other_after)
        return [run(0, F32, own_after), swap(gunit, "core", 1)]

    loss = loss + swap(loss, "core", 1)
    forwarded = add_blocks(part_of(3), BF16)
    from_forwarder = swap(forwarded, PLACE, 1)
    near = add_blocks(part_of(1, [forwarded], [forwarded]), BF16)
    from_near = swap(near, PLACE, 1)
    across = part_of(2, [near], [near])
    values = part_of(0, [near], [near])

    grad_proto, proto_sent = proto_gradient(dscore, unit, loss, after(scalar(batch_index), values[1]), batch_size)
    from_forwarder = after(from_forwarder, proto_sent, from_near)
    across = add_blocks(across + [from_forwarder], BF16)
    values += [from_near, swap(across, PLACE, 2)]

    bit = 2
    while (1 << bit) < places:
        kept, sent = combine(scalar((place >> bit) % 2), values)
        values = [kept, swap(sent, PLACE, 1 << bit)]
        bit += 1
    grad_embed = embed_gradient(scalar(proto_index), embeddings, [value[0] for value in values])
    arrived = [swap(proto_sent[distance], "batch", distance) for distance in range(batch_size - 1, 0, -1)]
    for block in arrived:
        grad_proto = grad_proto + block[:proto_count].astype(F32)
    rows = functools.reduce(jnp.add, [block[proto_count : proto_count + 3, :LANES].astype(F32) for block in arrived])
    loss = loss + jnp.sum(rows, axis=0, keepdims=True)
    loss = functools.reduce(jnp.add, parts_of(loss, PLACE))
    loss = loss[0, 0] / total_rows

    return (loss, grad_proto, grad_embed)


def solution(mesh):
    batch_size, proto_size = mesh.shape["batch"], mesh.shape["proto"]
    devices = mesh.devices.reshape(batch_size, proto_size // 8, 2, 2, 2)
    proto = PLACE + ("core",)
    return jax.shard_map(
        on_device,
        mesh=jax.sharding.Mesh(devices, ("batch",) + proto),
        in_specs=(P("batch", None), P(proto, None), P("batch", None)),
        out_specs=(P(), P(proto, "batch"), P(("batch",) + proto, None)),
        check_vma=False,
    )
```
